32 devices in a mesh: req: 16 (over z, y, x), tp: 2 (over core).
Axes of the slice: x: 2, y: 2, z: 4, core: 2. Of those that a mesh axis runs over, the one named last changes fastest.
Arguments:
- hidden_in: bfloat16 [2048, 5120], P('req', 'tp'), may hold values from -1.5 to 1.5
- queries: bfloat16 [2048, 5120], P('req', 'tp'), may hold values from -100 to 100
- new_keys: bfloat16 [2048, 5120], P('req', 'tp'), may hold values from -12 to 12
- new_values: bfloat16 [2048, 5120], P('req', 'tp'), may hold values from -6 to 6
- query_gain: float32 [5120], P('tp'), may hold values from 0.1 to 1.9
- key_gain: float32 [5120], P('tp'), may hold values from 0.1 to 1.9
- cache_keys: bfloat16 [256, 256, 5120], P('req', None, 'tp'), may hold values from -50 to 50
- cache_values: bfloat16 [256, 256, 5120], P('req', None, 'tp'), may hold values from -6 to 6
- seg_ids: int32 [2048], replicated, may hold values from 0 to 15, never falling along the last dimension, each value on 1 to 256 neighbouring positions
- cache_pages: int32 [16], replicated, may hold values from 1 to 32, 256 in all
- page_table: int32 [256], replicated, may hold values from 0 to 255, each once
- out_weight: bfloat16 [5120, 5120], P('tp', 'req'), may hold values from -0.078125 to 0.078125
- out_bias: float32 [5120], P('tp'), may hold values from -1.8 to 1.8
- gate_mod: float32 [16, 5120], P(None, 'tp'), may hold values from -8 to 8
Outputs:
- hidden_out: bfloat16 [2048, 5120], P('req', 'tp')
The draws below stay inside these ranges and needn't reach their ends.
Inputs may be any that keep to these rules, and one draw needn't show every extreme that they name: `seg_ids`: segment numbers never fall; segment r holds the new tokens of request r; every request has 1 to 256 new tokens, one exactly 256. `cache_pages`: every request has at least one cached page; the counts sum to 256; the largest is exactly 32. A permutation; logical page g (the requests' pages in order of request, each request's in order) lies in slot page_table[g] % 16 of the req index page_table[g] // 16.
All inputs are finite; a program needn't handle non-finite values.
Results may differ from the reference program's by a relative error of at most 0.012.
Values may be sent and summed in bfloat16 or wider, within the bound.
No kernel may reach another device: no remote copies, remote signals or barrier semaphores. Data moves between devices by JAX's collectives and lax.ppermute only.
A program may use at most 192 MiB of HBM per device.

```python
import math
import jax
import jax.numpy as jnp
import numpy as np
from jax import lax

D = 5120
HEADS = 40
HEAD_DIM = 128
PAGE = 256
P_DEV = 16
TOKENS = 2048
REQS = 16
SEG_MOST = 256
TOTAL_PAGES = 256
MAX_PAGES = 32
N_REQ = 16


def draw_queries(key, part):
    own_key = jax.random.fold_in(key, 11)
    key_base = jax.random.fold_in(own_key, 0)
    column = 0.6 * 3.0 ** (jnp.arange(D, dtype=jnp.float32) / D)
    base = jnp.clip(jax.random.normal(key_base, (TOKENS, D), jnp.float32), -6.0, 6.0)
    values = base * column[None, :]
    return values.astype(jnp.bfloat16)


def draw_new_keys(key, part):
    own_key = jax.random.fold_in(key, 23)
    key_base = jax.random.fold_in(own_key, 0)
    column = 0.6 * 3.0 ** (jnp.arange(D, dtype=jnp.float32) / D)
    base = jnp.clip(jax.random.normal(key_base, (TOKENS, D), jnp.float32), -6.0, 6.0)
    values = base * column[None, :]
    return values.astype(jnp.bfloat16)


def draw_cache_keys(key, part):
    own_key = jax.random.fold_in(key, 37)
    key_base = jax.random.fold_in(own_key, 0)
    shape_full = (TOTAL_PAGES, PAGE, D)
    values = jnp.clip(jax.random.normal(key_base, shape_full, jnp.float32), -6.0, 6.0)
    return values.astype(jnp.bfloat16)


def steps_of(stream_key, dims, cuts, least, largest):
    level = 1.0
    for axis_at, blocks in cuts:
        draws = jax.random.uniform(jax.random.fold_in(jax.random.fold_in(stream_key, 6), axis_at), (blocks,), jnp.float32, least / len(cuts), largest / len(cuts))
        level = level * jnp.repeat(jnp.exp(draws), dims[axis_at] // blocks).reshape((-1,) + (1,) * (len(dims) - 1 - axis_at))
    return level


def length_profile(amount, total, most, lean):
    portions = [(1 << 20) // math.isqrt(grade ** lean) + 1 for grade in range(2, amount + 1)]
    surplus, holding = total - most - (amount - 1), [1] * (amount - 1)
    while surplus > 0:
        candidates = [i for i in range(amount - 1) if holding[i] < most]
        whole, left = sum([portions[i] for i in candidates]), surplus
        for i in candidates:
            more = min(most - holding[i], max(1, left * portions[i] // whole), surplus)
            holding[i] = holding[i] + more
            surplus = surplus - more
    return np.array([most] + holding)


def uneven(stream_key, number_of, total, bound, slope):
    if number_of == 2:
        one = jax.random.randint(stream_key, (), max(1, total - bound), min(bound, total - 1) + 1)
        return jnp.stack([one, total - one])
    sizes = jnp.asarray(length_profile(number_of, total, bound, slope), jnp.int32)
    twos = (number_of - 1) // 2
    source_of, receiver = sizes[1:1 + 2 * twos:2], sizes[2:2 + 2 * twos:2]
    margin = jnp.minimum(source_of - 1, bound - receiver)
    shifted = jax.random.randint(jax.random.fold_in(stream_key, 1), (twos,), 0, 1 << 20) % (margin + 1)
    sizes = sizes.at[1:1 + 2 * twos:2].set(source_of - shifted).at[2:2 + 2 * twos:2].set(receiver + shifted)
    return sizes[jax.random.permutation(jax.random.fold_in(stream_key, 2), number_of)]


def centred(key, extent, scale, reach, cuts=(), kind=jnp.bfloat16):
    drawn = scale * jax.random.normal(key, extent, jnp.float32)
    if cuts:
        drawn = drawn * steps_of(key, extent, cuts, -0.22, 0.18)
    return jnp.clip(drawn, -reach, reach).astype(kind)


def setup_inputs(seed: int = 0) -> dict:
    arg_keys = jax.random.split(jax.random.key(seed), 15)
    hidden_in = centred(arg_keys[0], (TOKENS, D), 0.25, 1.5, ((0, 16), (1, 2)))
    queries = draw_queries(jax.random.fold_in(arg_keys[14], 71), 0)
    new_keys = draw_new_keys(jax.random.fold_in(arg_keys[14], 71), 0)
    new_values = centred(arg_keys[3], (TOKENS, D), 1.0, 6.0, ((0, 16), (1, 2)))
    query_gain = jnp.clip(1.0 + 0.18 * jax.random.normal(arg_keys[4], (D,), jnp.float32), 0.1, 1.9)
    key_gain = jnp.clip(1.0 + 0.18 * jax.random.normal(arg_keys[5], (D,), jnp.float32), 0.1, 1.9)
    cache_keys = draw_cache_keys(jax.random.fold_in(arg_keys[14], 71), 0)
    cache_values = centred(arg_keys[7], (TOTAL_PAGES, PAGE, D), 1.0, 6.0, ((0, 16), (2, 2)))
    seg_ids = jnp.searchsorted(jnp.cumsum(uneven(arg_keys[8], REQS, TOKENS, SEG_MOST, 2)), jnp.arange(TOKENS), side="right").astype(jnp.int32)
    cache_pages = uneven(arg_keys[9], REQS, TOTAL_PAGES, MAX_PAGES, 3).astype(jnp.int32)
    page_table = jax.random.permutation(arg_keys[10], TOTAL_PAGES).astype(jnp.int32)
    out_weight = centred(arg_keys[11], (D, D), D ** -0.5, 0.078125, ((0, 2), (1, 16)))
    out_bias = centred(arg_keys[12], (D,), 0.3, 1.8, ((0, 2),), jnp.float32)
    gate_mod = centred(arg_keys[13], (REQS, D), 2.0, 8.0, ((1, 2),), jnp.float32)
    return dict(hidden_in=hidden_in, queries=queries, new_keys=new_keys, new_values=new_values, query_gain=query_gain, key_gain=key_gain, cache_keys=cache_keys, cache_values=cache_values, seg_ids=seg_ids, cache_pages=cache_pages, page_table=page_table, out_weight=out_weight, out_bias=out_bias, gate_mod=gate_mod)


EPSILON = 1e-06
LOW_SCORE = -1e+30

def norm_turn(values, gain, positions):
    wide = values.astype(jnp.float32)
    mean_square = lax.optimization_barrier(jnp.mean(wide * wide, axis=1, keepdims=True))
    normed = wide * lax.rsqrt(mean_square + EPSILON) * gain[None, :]
    row_count, width_count = normed.shape
    split_heads = normed.reshape(row_count, width_count // HEAD_DIM, HEAD_DIM)
    halfway = HEAD_DIM // 2
    frequency = 10000.0 ** (-jnp.arange(halfway, dtype=jnp.float32) / halfway)
    angles = positions.astype(jnp.float32)[:, None] * frequency[None, :]
    cosine = jnp.cos(angles)[:, None, :]
    sine_part = jnp.sin(angles)[:, None, :]
    lower_half = split_heads[:, :, :halfway]
    upper_half = split_heads[:, :, halfway:]
    turned = jnp.concatenate([lower_half * cosine - upper_half * sine_part, upper_half * cosine + lower_half * sine_part], axis=2)
    return lax.optimization_barrier(turned.reshape(row_count, width_count).astype(jnp.bfloat16))

def combine_pair(first, second):
    first_max, first_sum, first_out = first
    second_max, second_sum, second_out = second
    highest = jnp.maximum(first_max, second_max)
    first_weight = jnp.exp(first_max - highest)
    second_weight = jnp.exp(second_max - highest)
    return (highest, first_sum * first_weight + second_sum * second_weight, first_out * first_weight[..., None] + second_out * second_weight[..., None])

def attend_block(query_rows, key_rows, value_rows, allowed):
    heads_here = query_rows.shape[1] // HEAD_DIM
    score_scale = 1.0 / math.sqrt(HEAD_DIM)
    query_wide = query_rows.astype(jnp.float32).reshape(query_rows.shape[0], heads_here, HEAD_DIM)
    key_wide = key_rows.astype(jnp.float32).reshape(key_rows.shape[0], heads_here, HEAD_DIM)
    scores = jnp.einsum('qhd,khd->hqk', query_wide, key_wide) * score_scale
    scores = jnp.where(allowed[None], scores, LOW_SCORE)
    peak_score = lax.optimization_barrier(jnp.max(scores, axis=2))
    weights = jnp.where(allowed[None], jnp.exp(scores - peak_score[:, :, None]), 0.0)
    weight_sum = lax.optimization_barrier(jnp.sum(weights, axis=2))
    rounded = lax.optimization_barrier(weights.astype(jnp.bfloat16)).astype(jnp.float32)
    value_wide = value_rows.astype(jnp.float32).reshape(value_rows.shape[0], heads_here, HEAD_DIM)
    blended = jnp.einsum('hqk,khd->qhd', rounded, value_wide)
    row_any = jnp.any(allowed, axis=1)
    peak_score = jnp.where(row_any[None, :], peak_score, LOW_SCORE)
    return (peak_score.T, weight_sum.T, blended)

def reference(hidden_in, queries, new_keys, new_values, query_gain, key_gain, cache_keys, cache_values, seg_ids, cache_pages, page_table, out_weight, out_bias, gate_mod):
    req_ids = jnp.arange(REQS, dtype=jnp.int32)
    starts = lax.optimization_barrier(jnp.sum((seg_ids[None, :] < req_ids[:, None]).astype(jnp.int32), axis=1)).astype(jnp.int32)
    token_pick = seg_ids[:, None] == req_ids[None, :]
    token_start = lax.optimization_barrier(jnp.sum(jnp.where(token_pick, starts[None, :], 0), axis=1)).astype(jnp.int32)
    token_cache = lax.optimization_barrier(jnp.sum(jnp.where(token_pick, cache_pages[None, :], 0), axis=1)).astype(jnp.int32)
    positions = token_cache * PAGE + jnp.arange(TOKENS, dtype=jnp.int32) - token_start
    q_rot = norm_turn(queries, query_gain, positions)
    k_rot = norm_turn(new_keys, key_gain, positions)
    padded_queries = jnp.concatenate([q_rot, jnp.zeros((SEG_MOST, D), jnp.bfloat16)], axis=0)
    padded_segs = jnp.concatenate([seg_ids, jnp.full((SEG_MOST,), -1, jnp.int32)])
    page_ends = jnp.cumsum(cache_pages).astype(jnp.int32)
    inverse = jnp.zeros((TOTAL_PAGES,), jnp.int32).at[page_table].set(jnp.arange(TOTAL_PAGES, dtype=jnp.int32))

    def absorb_slot(running, physical):
        logical = lax.dynamic_index_in_dim(inverse, physical, 0, keepdims=False).astype(jnp.int32)
        page_keys = lax.dynamic_index_in_dim(cache_keys, physical, 0, keepdims=False)
        page_values = lax.dynamic_index_in_dim(cache_values, physical, 0, keepdims=False)
        owner_req = jnp.sum((page_ends <= logical).astype(jnp.int32)).astype(jnp.int32)
        owner_row = jnp.sum(jnp.where(req_ids == owner_req, starts, 0)).astype(jnp.int32)
        window = lax.dynamic_slice_in_dim(padded_queries, owner_row, SEG_MOST, 0)
        inside = lax.dynamic_slice_in_dim(padded_segs, owner_row, SEG_MOST, 0) == owner_req
        allowed = jnp.broadcast_to(inside[:, None], (SEG_MOST, PAGE))
        fresh = attend_block(window, page_keys, page_values, allowed)
        earlier = tuple((lax.dynamic_slice_in_dim(part_arr, owner_row, SEG_MOST, 0) for part_arr in running))
        merged = combine_pair(earlier, fresh)
        updated = tuple((lax.dynamic_update_slice_in_dim(whole_arr, new_arr, owner_row, 0) for whole_arr, new_arr in zip(running, merged)))
        return (updated, None)

    def empty_state():
        return (jnp.full((TOKENS + SEG_MOST, HEADS), LOW_SCORE, jnp.float32), jnp.zeros((TOKENS + SEG_MOST, HEADS), jnp.float32), jnp.zeros((TOKENS + SEG_MOST, HEADS, HEAD_DIM), jnp.float32))

    def holder_pass(overall, holder):
        slots = (holder * P_DEV + jnp.arange(P_DEV, dtype=jnp.int32)).astype(jnp.int32)
        running, _ = lax.scan(absorb_slot, empty_state(), slots)
        holder_max, holder_sum, holder_acc = running
        holder_out = lax.optimization_barrier((holder_acc / jnp.maximum(holder_sum, 1.0)[..., None]).astype(jnp.bfloat16)).astype(jnp.float32)
        overall = combine_pair(overall, (holder_max, holder_sum, holder_sum[..., None] * holder_out))
        return (overall, None)
    overall, _ = lax.scan(holder_pass, empty_state(), jnp.arange(N_REQ, dtype=jnp.int32))
    cache_part = tuple((part_arr[:TOKENS] for part_arr in overall))
    block_rows = min(512, TOKENS)
    padded_keys = jnp.concatenate([jnp.zeros((SEG_MOST, D), jnp.bfloat16), k_rot], axis=0)
    padded_values = jnp.concatenate([jnp.zeros((SEG_MOST, D), jnp.bfloat16), new_values], axis=0)
    front_segs = jnp.concatenate([jnp.full((SEG_MOST,), -1, jnp.int32), seg_ids])

    def near_block(block_index):
        first_row = (block_index * block_rows).astype(jnp.int32)
        query_rows = lax.dynamic_slice_in_dim(q_rot, first_row, block_rows, 0)
        key_rows = lax.dynamic_slice_in_dim(padded_keys, first_row, block_rows + SEG_MOST, 0)
        value_rows = lax.dynamic_slice_in_dim(padded_values, first_row, block_rows + SEG_MOST, 0)
        key_segs = lax.dynamic_slice_in_dim(front_segs, first_row, block_rows + SEG_MOST, 0)
        key_index = first_row - SEG_MOST + jnp.arange(block_rows + SEG_MOST, dtype=jnp.int32)
        row_index = first_row + jnp.arange(block_rows, dtype=jnp.int32)
        row_segs = lax.dynamic_slice_in_dim(seg_ids, first_row, block_rows, 0)
        allowed = (key_segs[None, :] == row_segs[:, None]) & (key_index[None, :] <= row_index[:, None])
        return attend_block(query_rows, key_rows, value_rows, allowed)
    near_max, near_sum, near_out = lax.map(near_block, jnp.arange(TOKENS // block_rows, dtype=jnp.int32))
    near_part = (near_max.reshape(TOKENS, HEADS), near_sum.reshape(TOKENS, HEADS), near_out.reshape(TOKENS, HEADS, HEAD_DIM))
    highest, total_sum, total_out = combine_pair(cache_part, near_part)
    attended = (total_out / total_sum[..., None]).reshape(TOKENS, D).astype(jnp.bfloat16)
    projected = jnp.dot(attended, out_weight, preferred_element_type=jnp.float32) + out_bias[None, :]
    gate_rows = jnp.take(gate_mod, seg_ids, axis=0)
    return (hidden_in.astype(jnp.float32) + gate_rows * projected).astype(jnp.bfloat16)
```

```python
import functools
import math

import jax
import jax.numpy as jnp
from jax import lax
from jax.experimental import pallas as pl
from jax.experimental.pallas import tpu as pltpu
from jax.sharding import PartitionSpec as P

HEAD_DIM = 128
EPSILON = 1e-06
LOW_SCORE = -1e30
PLANE = 4
PIECE = 16
SCORE_SCALE = math.log2(math.e) / math.sqrt(HEAD_DIM)


def send_xor(value, by):
    size = lax.axis_size("req")
    return lax.ppermute(value, "req", [(i, i ^ by) for i in range(size)])


def send_line(value, by):
    size = lax.axis_size("req")
    line = size // PLANE
    pairs = [(i, ((i // PLANE + by) % line) * PLANE + i % PLANE) for i in range(size)]
    return lax.ppermute(value, "req", pairs)


def group_count(width):
    return 2 if width // HEAD_DIM % 2 == 0 else 1


def turn_kernel(q_ref, k_ref, scale_ref, gain_q_ref, gain_k_ref, cos_ref, sin_ref, *outs):
    cosine = cos_ref[...]
    sine = sin_ref[...]
    width = q_ref.shape[1]
    group_width = width // group_count(width)
    k_out = outs[-1]
    for side, (ref, gain) in enumerate(((q_ref, gain_q_ref), (k_ref, gain_k_ref))):
        scale = scale_ref[:, side : side + 1]
        for col in range(0, width, HEAD_DIM):
            x = ref[:, col : col + HEAD_DIM].astype(jnp.float32) * scale * gain[:, col : col + HEAD_DIM]
            y = (x * cosine + pltpu.roll(x, HEAD_DIM // 2, 1) * sine).astype(jnp.bfloat16)
            if side == 1:
                k_out[:, col : col + HEAD_DIM] = y
            else:
                at = col % group_width
                outs[col // group_width][:, at : at + HEAD_DIM] = y


def turn(queries, new_keys, scales, gain_q, gain_k, cosine, sine):
    rows, width = queries.shape
    groups = group_count(width)
    part = jax.ShapeDtypeStruct((rows, width // groups), jnp.bfloat16)
    return pl.pallas_call(
        turn_kernel,
        out_shape=[part] * groups + [jax.ShapeDtypeStruct((rows, width), jnp.bfloat16)],
        compiler_params=pltpu.CompilerParams(vmem_limit_bytes=32 * 2**20),
        name="norm_turn",
    )(queries, new_keys, scales, gain_q[None], gain_k[None], cosine, sine)


def attend_kernel(
    table_ref,
    slot_ref,
    q_low_ref,
    q_high_ref,
    keys_ref,
    values_ref,
    near_keys_ref,
    near_values_ref,
    near_starts_ref,
    keep_ref,
    send_ref,
    q_all,
    acc,
    peak,
    total,
    sems,
):
    step = pl.program_id(0)
    half, rows, width = q_low_ref.shape
    blocks = 2 * half
    heads = width // HEAD_DIM
    lane = lax.broadcasted_iota(jnp.int32, (1, rows), 1)

    def update(slots, keys, values, row_masks, allowed):
        old_peak = [peak[s] for s in slots]
        old_total = [total[s] for s in slots]
        new_peak = [[] for _ in slots]
        new_total = [[] for _ in slots]
        for h in range(heads):
            cols = slice(h * HEAD_DIM, (h + 1) * HEAD_DIM)
            q = [q_all[s, :, cols] for s in slots]
            q = q[0] if len(q) == 1 else jnp.concatenate(q, axis=0)
            scores = lax.dot_general(
                keys[:, cols], q, (((1,), (1,)), ((), ())), preferred_element_type=jnp.float32
            )
            if allowed is not None:
                scores = jnp.where(allowed, scores, LOW_SCORE)
            before = [p[h : h + 1] for p in old_peak]
            before = before[0] if len(before) == 1 else jnp.concatenate(before, axis=1)
            top = jnp.maximum(jnp.max(scores, axis=0, keepdims=True), before)
            weights = jnp.exp2(scores * SCORE_SCALE - top * SCORE_SCALE)
            weight_sum = jnp.sum(weights, axis=0, keepdims=True)
            fade = jnp.exp2((before - top) * SCORE_SCALE)
            blended = lax.dot_general(
                values[:, cols],
                weights.astype(jnp.bfloat16),
                (((0,), (0,)), ((), ())),
                preferred_element_type=jnp.float32,
            )
            for i, s in enumerate(slots):
                span = slice(i * rows, (i + 1) * rows)
                mask = row_masks[i]
                held = acc[s, cols, :]
                acc[s, cols, :] = jnp.where(mask, held * fade[:, span] + blended[:, span], held)
                new_peak[i].append(jnp.where(mask, top[:, span], old_peak[i][h : h + 1]))
                earlier = old_total[i][h : h + 1]
                new_total[i].append(
                    jnp.where(mask, earlier * fade[:, span] + weight_sum[:, span], earlier)
                )
        for i, s in enumerate(slots):
            for h in range(heads):
                peak[s, h : h + 1, :] = new_peak[i][h]
                total[s, h : h + 1, :] = new_total[i][h]

    @pl.when(step == 0)
    def _():
        low = pltpu.make_async_copy(q_low_ref, q_all.at[pl.ds(0, half)], sems.at[0])
        high = pltpu.make_async_copy(q_high_ref, q_all.at[pl.ds(half, half)], sems.at[1])
        low.start()
        high.start()
        acc[...] = jnp.zeros_like(acc)
        peak[...] = jnp.full(peak.shape, LOW_SCORE, jnp.float32)
        total[...] = jnp.zeros_like(total)
        low.wait()
        high.wait()
        first = slot_ref[blocks + 1]

        def near_block(j, carry):
            slot = slot_ref[jnp.minimum(first + j, blocks)]
            row = (first + j) * rows + lane
            begin = near_starts_ref[j]
            key = first * rows + lax.broadcasted_iota(jnp.int32, (rows, rows), 0)
            allowed = (key >= begin) & (key <= row)
            some = begin < (first + 1) * rows
            update([slot], near_keys_ref[...], near_values_ref[...], [some], allowed)
            return carry

        lax.fori_loop(0, 3, near_block, 0)

    @pl.when(step > 0)
    def _():
        begin = table_ref[4 * step - 4]
        end = table_ref[4 * step - 3]
        first = table_ref[4 * step - 2]
        count = table_ref[4 * step - 1]

        def pair(j, carry):
            low = first + 2 * j
            row = low * rows + lane
            masks = [(r >= begin) & (r < end) for r in (row, row + rows)]
            update([slot_ref[low], slot_ref[low + 1]], keys_ref[0], values_ref[0], masks, None)
            return carry

        lax.fori_loop(0, count, pair, 0)

    @pl.when(step == pl.num_programs(0) - 1)
    def _():
        for at, out in ((0, keep_ref), (half, send_ref)):

            def finish(i, carry, at=at, out=out):
                sums = jnp.maximum(total[at + i], 1.0)
                write_block(
                    out.at[i],
                    lambda h: acc[at + i, h * HEAD_DIM : (h + 1) * HEAD_DIM, :],
                    1.0 / sums,
                    peak[at + i] * SCORE_SCALE + jnp.log2(sums),
                    heads,
                )
                return carry

            lax.fori_loop(0, half, finish, 0)


def write_block(out, block, factors, levels, heads):
    for h in range(heads):
        out[h * HEAD_DIM : (h + 1) * HEAD_DIM, :] = (block(h) * factors[h : h + 1]).astype(jnp.bfloat16)
    left = levels
    for i in range(3):
        part = left.astype(jnp.bfloat16)
        at = heads * HEAD_DIM + i * PIECE
        out[at : at + PIECE, :] = part
        left = left - part.astype(jnp.float32)


def read_levels(ref, heads):
    at = heads * HEAD_DIM
    parts = [ref[at + i * PIECE : at + (i + 1) * PIECE, :].astype(jnp.float32) for i in range(3)]
    return parts[0] + (parts[1] + parts[2])


def attend(group, table, slots, q_low, q_high, cache_keys, cache_values, near_keys, near_values, near_starts):
    half, rows, width = q_low.shape
    pages, page_len, _ = cache_keys.shape
    heads = width // HEAD_DIM
    blocks = 2 * half
    out = jax.ShapeDtypeStruct((half, width + 3 * PIECE, rows), jnp.bfloat16)
    page_spec = pl.BlockSpec((1, page_len, width), lambda i, *_: (jnp.maximum(i - 1, 0), 0, group))
    near_spec = pl.BlockSpec((rows, width), lambda i, *_: (0, group))
    whole = lambda shape: pl.BlockSpec(shape, lambda i, *_: (0,) * len(shape))
    return pl.pallas_call(
        attend_kernel,
        grid_spec=pltpu.PrefetchScalarGridSpec(
            num_scalar_prefetch=2,
            grid=(pages + 1,),
            in_specs=[
                pl.BlockSpec(memory_space=pl.ANY),
                pl.BlockSpec(memory_space=pl.ANY),
                page_spec,
                page_spec,
                near_spec,
                near_spec,
                whole((3, 1, rows)),
            ],
            out_specs=[whole(out.shape), whole(out.shape)],
            scratch_shapes=[
                pltpu.VMEM((blocks + 1, rows, width), jnp.bfloat16),
                pltpu.VMEM((blocks + 1, width, rows), jnp.float32),
                pltpu.VMEM((blocks + 1, PIECE, rows), jnp.float32),
                pltpu.VMEM((blocks + 1, PIECE, rows), jnp.float32),
                pltpu.SemaphoreType.DMA((2,)),
            ],
        ),
        out_shape=[out, out],
        compiler_params=pltpu.CompilerParams(
            dimension_semantics=("arbitrary",), vmem_limit_bytes=56 * 2**20
        ),
        cost_estimate=pl.CostEstimate(
            flops=pages * heads * 256 * page_len * HEAD_DIM * 16,
            bytes_accessed=pages * page_len * width * 4,
            transcendentals=pages * heads * 256 * page_len,
        ),
        name="cache_attend",
    )(table, slots, q_low, q_high, cache_keys, cache_values, near_keys, near_values, near_starts)


def merged(refs, heads):
    levels = [read_levels(ref, heads) for ref in refs]
    top = functools.reduce(jnp.maximum, levels)
    weights = [jnp.exp2(level - top) for level in levels]
    total = functools.reduce(jnp.add, weights)
    factors = [w / total for w in weights]

    def block(h):
        cols = slice(h * HEAD_DIM, (h + 1) * HEAD_DIM)
        return functools.reduce(
            jnp.add, [ref[cols, :].astype(jnp.float32) * f[h : h + 1] for ref, f in zip(refs, factors)]
        )

    return block, top + jnp.log2(total)


def combine_kernel(mine_low, mine_high, got_low, got_high, keep_ref, send_ref):
    heads = (mine_low.shape[1] - 3 * PIECE) // HEAD_DIM
    for mine, got, out in ((mine_low, got_low, keep_ref), (mine_high, got_high, send_ref)):
        block, levels = merged([mine.at[0], got.at[0]], heads)
        write_block(out.at[0], block, jnp.ones_like(levels), levels, heads)


def combine(mine, got):
    count, depth, rows = mine.shape
    half = count // 2
    low = pl.BlockSpec((1, depth, rows), lambda i: (i, 0, 0))
    high = pl.BlockSpec((1, depth, rows), lambda i: (i + half, 0, 0))
    out = jax.ShapeDtypeStruct((half, depth, rows), jnp.bfloat16)
    return pl.pallas_call(
        combine_kernel,
        grid=(half,),
        in_specs=[low, high, low, high],
        out_specs=[low, low],
        out_shape=[out, out],
        compiler_params=pltpu.CompilerParams(vmem_limit_bytes=24 * 2**20),
        cost_estimate=pl.CostEstimate(
            flops=count * depth * rows * 4, bytes_accessed=count * depth * rows * 6, transcendentals=0
        ),
        name="combine_pairs",
    )(mine, mine, got, got)


def last_kernel(*refs):
    out_ref = refs[-1]
    heads = out_ref.shape[0] // HEAD_DIM
    block, _ = merged(refs[:-1], heads)
    for h in range(heads):
        out_ref[h * HEAD_DIM : (h + 1) * HEAD_DIM, :] = block(h).astype(jnp.bfloat16)


def combine_last(parts):
    depth, rows = parts[0].shape
    return pl.pallas_call(
        last_kernel,
        out_shape=jax.ShapeDtypeStruct((depth - 3 * PIECE, rows), jnp.bfloat16),
        compiler_params=pltpu.CompilerParams(vmem_limit_bytes=24 * 2**20),
        cost_estimate=pl.CostEstimate(
            flops=len(parts) * depth * rows * 2,
            bytes_accessed=(len(parts) + 1) * depth * rows * 2,
            transcendentals=0,
        ),
        name="combine_last",
    )(*parts)


def local(
    hidden_in,
    queries,
    new_keys,
    new_values,
    query_gain,
    key_gain,
    cache_keys,
    cache_values,
    seg_ids,
    cache_pages,
    page_table,
    out_weight,
    out_bias,
    gate_mod,
):
    tok_dev, local_width = queries.shape
    size = lax.axis_size("req")
    tp_size = lax.axis_size("tp")
    model_width = local_width * tp_size
    line = size // PLANE
    device = lax.axis_index("req")
    spot = device % PLANE
    place = device // PLANE
    slot_count, page_len, _ = cache_keys.shape
    request_count = cache_pages.shape[0]
    total_pages = page_table.shape[0]
    first_row = device * tok_dev
    own_rows = first_row + jnp.arange(tok_dev, dtype=jnp.int32)
    own_segs = lax.dynamic_slice_in_dim(seg_ids, first_row, tok_dev, 0)
    req_ids = jnp.arange(request_count, dtype=jnp.int32)
    starts = jnp.sum((seg_ids[None, :] < req_ids[:, None]).astype(jnp.int32), axis=1)
    ends = jnp.sum((seg_ids[None, :] <= req_ids[:, None]).astype(jnp.int32), axis=1)
    own_pick = own_segs[:, None] == req_ids[None, :]
    own_start = jnp.sum(jnp.where(own_pick, starts[None, :], 0), axis=1)
    own_cache = jnp.sum(jnp.where(own_pick, cache_pages[None, :], 0), axis=1)
    positions = own_cache * page_len + own_rows - own_start

    wide_q = queries.astype(jnp.float32)
    wide_k = new_keys.astype(jnp.float32)
    sums = lax.psum(
        jnp.stack([jnp.sum(wide_q * wide_q, axis=1), jnp.sum(wide_k * wide_k, axis=1)], axis=1), "tp"
    )
    scales = lax.rsqrt(sums / model_width + EPSILON)
    halfway = HEAD_DIM // 2
    frequency = 10000.0 ** (-jnp.arange(halfway, dtype=jnp.float32) / halfway)
    angles = positions.astype(jnp.float32)[:, None] * frequency[None, :]
    cosine = jnp.cos(angles)
    sine = jnp.sin(angles)
    turned = turn(
        queries,
        new_keys,
        scales,
        query_gain,
        key_gain,
        jnp.concatenate([cosine, cosine], axis=1),
        jnp.concatenate([-sine, sine], axis=1),
    )
    q_parts, k_rot = turned[:-1], turned[-1]

    physical = device * slot_count + jnp.arange(slot_count, dtype=jnp.int32)
    logical = jnp.sum(
        jnp.where(
            page_table[None, :] == physical[:, None],
            jnp.arange(total_pages, dtype=jnp.int32)[None, :],
            0,
        ),
        axis=1,
    )
    page_ends = jnp.cumsum(cache_pages)
    owners = jnp.sum((page_ends[None, :] <= logical[:, None]).astype(jnp.int32), axis=1)
    owner_pick = owners[:, None] == req_ids[None, :]
    owner_starts = jnp.sum(jnp.where(owner_pick, starts[None, :], 0), axis=1)
    owner_ends = jnp.sum(jnp.where(owner_pick, ends[None, :], 0), axis=1)
    owner_first = owner_starts // tok_dev
    owner_pairs = ((owner_ends - 1) // tok_dev - owner_first + 2) // 2
    table = jnp.stack([owner_starts, owner_ends, owner_first, owner_pairs], axis=1).reshape(-1)

    near_blocks = device + jnp.arange(3, dtype=jnp.int32)
    near_rows = (near_blocks[:, None] * tok_dev + jnp.arange(tok_dev, dtype=jnp.int32)[None, :]).reshape(-1)
    padded_segs = jnp.concatenate([seg_ids, jnp.full((2 * tok_dev,), -1, jnp.int32)])
    near_segs = lax.dynamic_slice_in_dim(padded_segs, first_row, 3 * tok_dev, 0)
    near_starts = jnp.sum(
        jnp.where(near_segs[:, None] == req_ids[None, :], starts[None, :], 0), axis=1
    )
    near_starts = jnp.where(near_segs < 0, near_rows + size * tok_dev, near_starts)
    near_starts = near_starts.reshape(3, 1, tok_dev)

    block = jnp.arange(size, dtype=jnp.int32)
    back = (place - block // PLANE) % line
    across = (block % PLANE) ^ spot

    def gather_queries(part, order):
        got = [part[None]] + [send_line(part, k)[None] for k in range(1, line)]
        near = jnp.concatenate(got, axis=0)
        low = jnp.concatenate([near, send_xor(near, order[0])], axis=0)
        return low, send_xor(low, order[1])

    attended = []
    for group in range(len(q_parts)):
        order = (2, 1) if group % 2 == 0 else (1, 2)
        low, high = gather_queries(q_parts[group], order)
        slot = jnp.where((across & order[1]) > 0, 2 * line, 0)
        slot = slot + jnp.where((across & order[0]) > 0, line, 0) + back
        slots = jnp.concatenate([slot, jnp.stack([jnp.int32(size), device])])
        keep, send = attend(
            group, table, slots, low, high, cache_keys, cache_values, k_rot, new_values, near_starts
        )
        keep, send = combine(keep, send_xor(send, order[1]))
        parts = combine_line(keep, send_xor(send, order[0]))
        attended.append(combine_last([parts[0]] + [send_line(parts[k], -k) for k in range(1, line)]))
    attended = jnp.concatenate(attended, axis=0)

    weight = out_weight.T
    columns = weight.shape[0]
    gathered = jnp.zeros((line * columns, local_width), jnp.bfloat16)
    for k in range(line):
        got = weight if k == 0 else send_line(weight, k)
        gathered = lax.dynamic_update_slice_in_dim(gathered, got, ((place - k) % line) * columns, 0)

    spread = jnp.concatenate([attended] + [send_xor(attended, k) for k in range(1, PLANE)], axis=1)
    partial_proj = jnp.dot(gathered, spread, preferred_element_type=jnp.float32)
    summed = lax.psum_scatter(partial_proj, "tp", scatter_dimension=0, tiled=True)
    mine = [summed[:, :tok_dev]] + [
        send_xor(summed[:, k * tok_dev : (k + 1) * tok_dev], k) for k in range(1, PLANE)
    ]
    mine = [part.reshape(line // tp_size, columns, tok_dev) for part in mine]
    swapped = [jnp.where((spot & 1) > 0, mine[i ^ 1], mine[i]) for i in range(PLANE)]
    swapped = [jnp.where((spot & 2) > 0, swapped[i ^ 2], swapped[i]) for i in range(PLANE)]
    projected = jnp.stack(swapped, axis=1).reshape(local_width, tok_dev).T

    gate_rows = jnp.dot(own_pick.astype(jnp.float32), gate_mod, precision=lax.Precision.HIGHEST)
    return (hidden_in.astype(jnp.float32) + gate_rows * (projected + out_bias[None, :])).astype(
        jnp.bfloat16
    )


def pair_kernel(mine, got, *outs):
    heads = (mine.shape[1] - 3 * PIECE) // HEAD_DIM
    for i, out in enumerate(outs):
        block, levels = merged([mine.at[i], got.at[i]], heads)
        write_block(out, block, jnp.ones_like(levels), levels, heads)


def combine_line(mine, got):
    count, depth, rows = mine.shape
    out = jax.ShapeDtypeStruct((depth, rows), jnp.bfloat16)
    return pl.pallas_call(
        pair_kernel,
        out_shape=[out] * count,
        compiler_params=pltpu.CompilerParams(vmem_limit_bytes=32 * 2**20),
        cost_estimate=pl.CostEstimate(
            flops=count * depth * rows * 4, bytes_accessed=count * depth * rows * 6, transcendentals=0
        ),
        name="combine_line",
    )(mine, got)


def solution(mesh):
    return jax.shard_map(
        local,
        mesh=mesh,
        in_specs=(
            P("req", "tp"),
            P("req", "tp"),
            P("req", "tp"),
            P("req", "tp"),
            P("tp"),
            P("tp"),
            P("req", None, "tp"),
            P("req", None, "tp"),
            P(),
            P(),
            P(),
            P("tp", "req"),
            P("tp"),
            P(None, "tp"),
        ),
        out_specs=P("req", "tp"),
        check_vma=False,
    )
```

```python
import functools
import math

import jax
import jax.numpy as jnp
from jax import lax
from jax.experimental import pallas as pl
from jax.experimental.pallas import tpu as pltpu
from jax.sharding import PartitionSpec as P

HEAD_DIM = 128
EPSILON = 1e-06
LOW_SCORE = -1e30
PLANE = 4
PIECE = 16
LEVEL_ROWS = 32
SCORE_SCALE = math.log2(math.e) / math.sqrt(HEAD_DIM)


def send_xor(value, by):
    size = lax.axis_size("req")
    return lax.ppermute(value, "req", [(i, i ^ by) for i in range(size)])


def send_line(value, by):
    size = lax.axis_size("req")
    line = size // PLANE
    pairs = [(i, ((i // PLANE + by) % line) * PLANE + i % PLANE) for i in range(size)]
    return lax.ppermute(value, "req", pairs)


def group_count(width):
    return 4 if width // HEAD_DIM % 4 == 0 else 1


def send_tp(value, by):
    size = lax.axis_size("tp")
    return lax.ppermute(value, "tp", [(i, (i + by) % size) for i in range(size)])


def place_kernel(spots_ref, *refs):
    *blocks, out, sems = refs
    copies = [
        pltpu.make_async_copy(ref, out.at[spots_ref[i]], sems.at[i]) for i, ref in enumerate(blocks)
    ]
    for copy in copies:
        copy.start()
    for copy in copies:
        copy.wait()


def place_blocks(spots, blocks):
    return pl.pallas_call(
        place_kernel,
        grid_spec=pltpu.PrefetchScalarGridSpec(
            num_scalar_prefetch=1,
            grid=(1,),
            in_specs=[pl.BlockSpec(memory_space=pl.ANY)] * len(blocks),
            out_specs=pl.BlockSpec(memory_space=pl.ANY),
            scratch_shapes=[pltpu.SemaphoreType.DMA((len(blocks),))],
        ),
        out_shape=jax.ShapeDtypeStruct((len(blocks),) + blocks[0].shape, blocks[0].dtype),
        name="place_weights",
    )(spots, *blocks)


def turn_kernel(q_ref, k_ref, scale_ref, gain_q_ref, gain_k_ref, cos_ref, sin_ref, _, q_out, k_out):
    cosine = cos_ref[...]
    sine = sin_ref[...]
    sides = ((q_ref, gain_q_ref, q_out), (k_ref, gain_k_ref, k_out))
    for side, (ref, gain, out) in enumerate(sides):
        scale = scale_ref[:, side : side + 1]
        for col in range(0, ref.shape[1], HEAD_DIM):
            cols = slice(col, col + HEAD_DIM)
            x = ref[:, cols].astype(jnp.float32) * scale * gain[:, cols]
            y = x * cosine + pltpu.roll(x, HEAD_DIM // 2, 1) * sine
            out[:, cols] = y.astype(jnp.bfloat16)


def turn(group, queries, new_keys, scales, gain_q, gain_k, cosine, sine, after):
    rows, width = queries.shape
    width = width // group_count(width)
    part = jax.ShapeDtypeStruct((rows, width), jnp.bfloat16)
    part_spec = pl.BlockSpec((rows, width), lambda i: (0, group))
    gain_spec = pl.BlockSpec((1, width), lambda i: (0, group))
    whole = lambda shape: pl.BlockSpec(shape, lambda i: (0, 0))
    return pl.pallas_call(
        turn_kernel,
        grid=(1,),
        in_specs=[
            part_spec,
            part_spec,
            whole(scales.shape),
            gain_spec,
            gain_spec,
            whole(cosine.shape),
            whole(sine.shape),
            pl.BlockSpec(memory_space=pl.ANY),
        ],
        out_specs=[whole(part.shape), whole(part.shape)],
        out_shape=[part, part],
        compiler_params=pltpu.CompilerParams(vmem_limit_bytes=16 * 2**20),
        name="norm_turn",
    )(queries, new_keys, scales, gain_q[None], gain_k[None], cosine, sine, after)


def attend_kernel(
    table_ref,
    slot_ref,
    q_low_ref,
    q_high_ref,
    keys_ref,
    values_ref,
    near_keys_ref,
    near_values_ref,
    near_starts_ref,
    keep_ref,
    send_ref,
    q_all,
    acc,
    peak,
    total,
    sems,
):
    step = pl.program_id(0)
    half, rows, width = q_low_ref.shape
    blocks = 2 * half
    heads = width // HEAD_DIM
    lane = lax.broadcasted_iota(jnp.int32, (1, rows), 1)

    def update(slots, keys_ref, values_ref, masks, allowed):
        ones = jnp.ones((PIECE, keys_ref.shape[0]), jnp.bfloat16)
        mask = jnp.concatenate(masks, axis=1)
        old_peak = jnp.concatenate([peak[s] for s in slots], axis=1)
        old_total = jnp.concatenate([total[s] for s in slots], axis=1)
        scores, weights, tops, fades = {}, {}, {}, {}

        def score(h):
            cols = slice(h * HEAD_DIM, (h + 1) * HEAD_DIM)
            q = jnp.concatenate([q_all[s, :, cols] for s in slots], axis=0)
            scores[h] = lax.dot_general(
                keys_ref[:, cols], q, (((1,), (1,)), ((), ())), preferred_element_type=jnp.float32
            )

        def weigh(h):
            found = scores.pop(h)
            if allowed is not None:
                found = jnp.where(allowed, found, LOW_SCORE)
            before = old_peak[h : h + 1]
            top = jnp.maximum(jnp.max(found, axis=0, keepdims=True), before)
            tops[h] = jnp.where(mask, top, before)
            fades[h] = jnp.where(mask, jnp.exp2(before - top), 1.0)
            weights[h] = jnp.exp2(found - jnp.where(mask, top, -LOW_SCORE)).astype(jnp.bfloat16)

        def blend(h):
            cols = slice(h * HEAD_DIM, (h + 1) * HEAD_DIM)
            values = jnp.concatenate([values_ref[:, cols].T, ones], axis=0)
            blended = jnp.dot(values, weights.pop(h), preferred_element_type=jnp.float32)
            fade = fades.pop(h)
            held = [acc[s, cols, :] for s in slots]
            sums = old_total[h : h + 1] * fade + blended[HEAD_DIM : HEAD_DIM + 1]
            for i, s in enumerate(slots):
                span = slice(i * rows, (i + 1) * rows)
                acc[s, cols, :] = held[i] * fade[:, span] + blended[:HEAD_DIM, span]
                peak[s, h : h + 1, :] = tops[h][:, span]
                total[s, h : h + 1, :] = sums[:, span]

        for h in range(heads + 2):
            if h < heads:
                score(h)
            if 1 <= h <= heads:
                weigh(h - 1)
            if h >= 2:
                blend(h - 2)

    @pl.when(step == 0)
    def _():
        low = pltpu.make_async_copy(q_low_ref, q_all.at[pl.ds(0, half)], sems.at[0])
        high = pltpu.make_async_copy(q_high_ref, q_all.at[pl.ds(half, half)], sems.at[1])
        low.start()
        high.start()
        q_all[blocks] = jnp.zeros((rows, width), jnp.bfloat16)
        acc[...] = jnp.zeros_like(acc)
        peak[...] = jnp.full(peak.shape, LOW_SCORE, jnp.float32)
        total[...] = jnp.zeros_like(total)
        low.wait()
        high.wait()
        first = slot_ref[blocks + 1]

        def near_pair(j, carry):
            low = first + 2 * j
            row = low * rows + jnp.concatenate([lane, lane + rows], axis=1)
            begin = near_starts_ref[j]
            key = first * rows + lax.broadcasted_iota(jnp.int32, (rows, 2 * rows), 0)
            allowed = (key >= begin) & (key <= row)
            some = begin < (first + 1) * rows
            slots = [slot_ref[jnp.minimum(low + i, blocks)] for i in range(2)]
            masks = [some[:, :rows], some[:, rows:]]
            update(slots, near_keys_ref, near_values_ref, masks, allowed)
            return carry

        lax.fori_loop(0, 2, near_pair, 0)

    @pl.when(step > 0)
    def _():
        begin = table_ref[4 * step - 4]
        end = table_ref[4 * step - 3]
        first = table_ref[4 * step - 2]
        count = table_ref[4 * step - 1]

        def pair(j, carry):
            low = first + 2 * j
            row = low * rows + lane
            masks = [(r >= begin) & (r < end) for r in (row, row + rows)]
            slots = [slot_ref[low], slot_ref[low + 1]]
            update(slots, keys_ref.at[0], values_ref.at[0], masks, None)
            return carry

        lax.fori_loop(0, count, pair, 0)

    @pl.when(step == pl.num_programs(0) - 1)
    def _():
        for at, out in ((0, keep_ref), (half, send_ref)):

            def finish(i, carry, at=at, out=out):
                sums = jnp.maximum(total[at + i], 1.0)
                write_block(
                    out.at[i],
                    lambda h: acc[at + i, h * HEAD_DIM : (h + 1) * HEAD_DIM, :],
                    1.0 / sums,
                    peak[at + i] + jnp.log2(sums),
                    heads,
                )
                return carry

            lax.fori_loop(0, half, finish, 0)


def write_block(out, block, factors, levels, heads):
    for h in range(heads):
        out[h * HEAD_DIM : (h + 1) * HEAD_DIM, :] = (block(h) * factors[h : h + 1]).astype(jnp.bfloat16)
    first = levels.astype(jnp.bfloat16).astype(jnp.float32)
    second = (levels - first).astype(jnp.bfloat16).astype(jnp.float32)
    third = levels - first - second
    stacked = jnp.concatenate([first, second, third, jnp.zeros_like(levels)], axis=0)
    out[heads * HEAD_DIM :, :] = stacked.astype(jnp.bfloat16)


def read_levels(ref, heads):
    stacked = ref[heads * HEAD_DIM :, :].astype(jnp.float32)
    return stacked[:8] + (stacked[8:16] + stacked[16:24])


def attend(group, table, slots, q_low, q_high, cache_keys, cache_values, near_keys, near_values, near_starts):
    half, rows, width = q_low.shape
    pages, page_len, _ = cache_keys.shape
    heads = width // HEAD_DIM
    blocks = 2 * half
    assert heads <= 8
    out = jax.ShapeDtypeStruct((half, width + LEVEL_ROWS, rows), jnp.bfloat16)
    page_spec = pl.BlockSpec((1, page_len, width), lambda i, *_: (jnp.maximum(i - 1, 0), 0, group))
    near_spec = pl.BlockSpec((rows, width), lambda i, *_: (0, group))
    own_spec = pl.BlockSpec((rows, width), lambda i, *_: (0, 0))
    whole = lambda shape: pl.BlockSpec(shape, lambda i, *_: (0,) * len(shape))
    return pl.pallas_call(
        attend_kernel,
        grid_spec=pltpu.PrefetchScalarGridSpec(
            num_scalar_prefetch=2,
            grid=(pages + 1,),
            in_specs=[
                pl.BlockSpec(memory_space=pl.ANY),
                pl.BlockSpec(memory_space=pl.ANY),
                page_spec,
                page_spec,
                own_spec,
                near_spec,
                whole((2, 1, 2 * rows)),
            ],
            out_specs=[whole(out.shape), whole(out.shape)],
            scratch_shapes=[
                pltpu.VMEM((blocks + 1, rows, width), jnp.bfloat16),
                pltpu.VMEM((blocks + 1, width, rows), jnp.float32),
                pltpu.VMEM((blocks + 1, 8, rows), jnp.float32),
                pltpu.VMEM((blocks + 1, 8, rows), jnp.float32),
                pltpu.SemaphoreType.DMA((2,)),
            ],
        ),
        out_shape=[out, out],
        compiler_params=pltpu.CompilerParams(
            dimension_semantics=("arbitrary",), vmem_limit_bytes=56 * 2**20
        ),
        cost_estimate=pl.CostEstimate(
            flops=pages * heads * 256 * page_len * HEAD_DIM * 8,
            bytes_accessed=pages * page_len * width * 4,
            transcendentals=pages * heads * 256 * page_len,
        ),
        name="cache_attend",
    )(table, slots, q_low, q_high, cache_keys, cache_values, near_keys, near_values, near_starts)


def merged(refs, heads):
    levels = [read_levels(ref, heads) for ref in refs]
    top = functools.reduce(jnp.maximum, levels)
    weights = [jnp.exp2(level - top) for level in levels]
    total = functools.reduce(jnp.add, weights)
    factors = [w / total for w in weights]

    def block(h):
        cols = slice(h * HEAD_DIM, (h + 1) * HEAD_DIM)
        return functools.reduce(
            jnp.add, [ref[cols, :].astype(jnp.float32) * f[h : h + 1] for ref, f in zip(refs, factors)]
        )

    return block, top + jnp.log2(total)


def combine_kernel(mine_low, mine_high, got_low, got_high, keep_ref, send_ref):
    heads = (mine_low.shape[1] - LEVEL_ROWS) // HEAD_DIM
    for mine, got, out in ((mine_low, got_low, keep_ref), (mine_high, got_high, send_ref)):
        block, levels = merged([mine.at[0], got.at[0]], heads)
        write_block(out.at[0], block, jnp.ones_like(levels), levels, heads)


def combine(mine, got):
    count, depth, rows = mine.shape
    half = count // 2
    low = pl.BlockSpec((1, depth, rows), lambda i: (i, 0, 0))
    high = pl.BlockSpec((1, depth, rows), lambda i: (i + half, 0, 0))
    out = jax.ShapeDtypeStruct((half, depth, rows), jnp.bfloat16)
    return pl.pallas_call(
        combine_kernel,
        grid=(half,),
        in_specs=[low, high, low, high],
        out_specs=[low, low],
        out_shape=[out, out],
        compiler_params=pltpu.CompilerParams(vmem_limit_bytes=24 * 2**20),
        cost_estimate=pl.CostEstimate(
            flops=count * depth * rows * 4, bytes_accessed=count * depth * rows * 6, transcendentals=0
        ),
        name="combine_pairs",
    )(mine, mine, got, got)


def last_kernel(*refs):
    out_ref = refs[-1]
    heads = out_ref.shape[0] // HEAD_DIM
    block, _ = merged(refs[:-1], heads)
    for h in range(heads):
        out_ref[h * HEAD_DIM : (h + 1) * HEAD_DIM, :] = block(h).astype(jnp.bfloat16)


def combine_last(parts):
    depth, rows = parts[0].shape
    return pl.pallas_call(
        last_kernel,
        out_shape=jax.ShapeDtypeStruct((depth - LEVEL_ROWS, rows), jnp.bfloat16),
        compiler_params=pltpu.CompilerParams(vmem_limit_bytes=24 * 2**20),
        cost_estimate=pl.CostEstimate(
            flops=len(parts) * depth * rows * 2,
            bytes_accessed=(len(parts) + 1) * depth * rows * 2,
            transcendentals=0,
        ),
        name="combine_last",
    )(*parts)


def local(
    hidden_in,
    queries,
    new_keys,
    new_values,
    query_gain,
    key_gain,
    cache_keys,
    cache_values,
    seg_ids,
    cache_pages,
    page_table,
    out_weight,
    out_bias,
    gate_mod,
):
    tok_dev, local_width = queries.shape
    size = lax.axis_size("req")
    tp_size = lax.axis_size("tp")
    model_width = local_width * tp_size
    line = size // PLANE
    device = lax.axis_index("req")
    spot = device % PLANE
    place = device // PLANE
    slot_count, page_len, _ = cache_keys.shape
    request_count = cache_pages.shape[0]
    total_pages = page_table.shape[0]
    first_row = device * tok_dev
    own_rows = first_row + jnp.arange(tok_dev, dtype=jnp.int32)
    own_segs = lax.dynamic_slice_in_dim(seg_ids, first_row, tok_dev, 0)
    req_ids = jnp.arange(request_count, dtype=jnp.int32)
    starts = jnp.sum((seg_ids[None, :] < req_ids[:, None]).astype(jnp.int32), axis=1)
    ends = jnp.sum((seg_ids[None, :] <= req_ids[:, None]).astype(jnp.int32), axis=1)
    own_pick = own_segs[:, None] == req_ids[None, :]
    own_start = jnp.sum(jnp.where(own_pick, starts[None, :], 0), axis=1)
    own_cache = jnp.sum(jnp.where(own_pick, cache_pages[None, :], 0), axis=1)
    positions = own_cache * page_len + own_rows - own_start

    wide_q = queries.astype(jnp.float32)
    wide_k = new_keys.astype(jnp.float32)
    sums = lax.psum(
        jnp.stack([jnp.sum(wide_q * wide_q, axis=1), jnp.sum(wide_k * wide_k, axis=1)], axis=1), "tp"
    )
    scales = lax.rsqrt(sums / model_width + EPSILON) * jnp.array([[SCORE_SCALE, 1.0]], jnp.float32)
    halfway = HEAD_DIM // 2
    frequency = 10000.0 ** (-jnp.arange(halfway, dtype=jnp.float32) / halfway)
    angles = positions.astype(jnp.float32)[:, None] * frequency[None, :]
    cosine = jnp.cos(angles)
    sine = jnp.sin(angles)
    cosine = jnp.concatenate([cosine, cosine], axis=1)
    sine = jnp.concatenate([-sine, sine], axis=1)

    physical = device * slot_count + jnp.arange(slot_count, dtype=jnp.int32)
    logical = jnp.sum(
        jnp.where(
            page_table[None, :] == physical[:, None],
            jnp.arange(total_pages, dtype=jnp.int32)[None, :],
            0,
        ),
        axis=1,
    )
    page_ends = jnp.cumsum(cache_pages)
    owners = jnp.sum((page_ends[None, :] <= logical[:, None]).astype(jnp.int32), axis=1)
    owner_pick = owners[:, None] == req_ids[None, :]
    owner_starts = jnp.sum(jnp.where(owner_pick, starts[None, :], 0), axis=1)
    owner_ends = jnp.sum(jnp.where(owner_pick, ends[None, :], 0), axis=1)
    owner_first = owner_starts // tok_dev
    owner_pairs = ((owner_ends - 1) // tok_dev - owner_first + 2) // 2
    table = jnp.stack([owner_starts, owner_ends, owner_first, owner_pairs], axis=1).reshape(-1)

    near_blocks = device + jnp.arange(4, dtype=jnp.int32)
    near_rows = (near_blocks[:, None] * tok_dev + jnp.arange(tok_dev, dtype=jnp.int32)[None, :]).reshape(-1)
    padded_segs = jnp.concatenate([seg_ids, jnp.full((3 * tok_dev,), -1, jnp.int32)])
    near_segs = lax.dynamic_slice_in_dim(padded_segs, first_row, 4 * tok_dev, 0)
    near_starts = jnp.sum(
        jnp.where(near_segs[:, None] == req_ids[None, :], starts[None, :], 0), axis=1
    )
    near_starts = jnp.where(near_segs < 0, near_rows + size * tok_dev, near_starts)
    near_starts = near_starts.reshape(2, 1, 2 * tok_dev)

    block = jnp.arange(size, dtype=jnp.int32)
    back = (place - block // PLANE) % line
    across = (block % PLANE) ^ spot

    def order_of(group):
        return (2, 1) if group % 2 == 0 else (1, 2)

    groups = group_count(local_width)
    near, near_keys = [], []
    after = scales
    for group in range(groups):
        part, key_part = turn(
            group, queries, new_keys, scales, query_gain, key_gain, cosine, sine, after
        )
        got = [part[None]] + [send_line(part, k)[None] for k in range(1, line)]
        near.append(jnp.concatenate(got, axis=0))
        near_keys.append(key_part)
        after = near[-1]

    weight, _ = lax.optimization_barrier((out_weight.T, after))
    columns = weight.shape[0]
    blocks_each = line // tp_size
    tp_device = lax.axis_index("tp")
    from_place = (place - jnp.arange(line, dtype=jnp.int32)) % line
    weight_spots = ((from_place // blocks_each - tp_device) % tp_size) * blocks_each
    weight_spots = weight_spots + from_place % blocks_each
    weights = place_blocks(weight_spots, [weight] + [send_line(weight, k) for k in range(1, line)])
    weights = weights.reshape(tp_size, blocks_each * columns, local_width)
    weights = [weights[0]] + [send_tp(weights[k], k) for k in range(1, tp_size)]

    attended = []
    for group in range(groups):
        order = order_of(group)
        low = jnp.concatenate([near[group], send_xor(near[group], order[0])], axis=0)
        high = send_xor(low, order[1])
        slot = jnp.where((across & order[1]) > 0, 2 * line, 0)
        slot = slot + jnp.where((across & order[0]) > 0, line, 0) + back
        slots = jnp.concatenate([slot, jnp.stack([jnp.int32(size), device])])
        keep, send = attend(
            group, table, slots, low, high, cache_keys, cache_values, near_keys[group], new_values, near_starts
        )
        keep, send = combine(keep, send_xor(send, order[1]))
        parts = combine_line(keep, send_xor(send, order[0]))
        attended.append(combine_last([parts[0]] + [send_line(parts[k], -k) for k in range(1, line)]))

    projected = 0.0
    depth = 0
    for some in ([attended[:-1], attended[-1:]] if groups > 1 else [attended]):
        some = jnp.concatenate(some, axis=0)
        spread = jnp.concatenate([some] + [send_xor(some, k) for k in range(1, PLANE)], axis=1)
        for k in range(tp_size):
            part = spread if k == 0 else send_tp(spread, k)
            projected = projected + jnp.dot(
                weights[k][:, depth : depth + some.shape[0]], part, preferred_element_type=jnp.float32
            )
        depth += some.shape[0]
    sent = projected.astype(jnp.bfloat16)
    mine = [projected[:, :tok_dev]] + [
        send_xor(sent[:, k * tok_dev : (k + 1) * tok_dev], k).astype(jnp.float32) for k in range(1, PLANE)
    ]
    mine = [part.reshape(blocks_each, columns, tok_dev) for part in mine]
    swapped = [jnp.where((spot & 1) > 0, mine[i ^ 1], mine[i]) for i in range(PLANE)]
    swapped = [jnp.where((spot & 2) > 0, swapped[i ^ 2], swapped[i]) for i in range(PLANE)]
    projected = jnp.stack(swapped, axis=1).reshape(local_width, tok_dev).T

    gate_rows = jnp.dot(own_pick.astype(jnp.float32), gate_mod, precision=lax.Precision.HIGHEST)
    return (hidden_in.astype(jnp.float32) + gate_rows * (projected + out_bias[None, :])).astype(
        jnp.bfloat16
    )


def pair_kernel(mine, got, *outs):
    heads = (mine.shape[1] - LEVEL_ROWS) // HEAD_DIM
    for i, out in enumerate(outs):
        block, levels = merged([mine.at[i], got.at[i]], heads)
        write_block(out, block, jnp.ones_like(levels), levels, heads)


def combine_line(mine, got):
    count, depth, rows = mine.shape
    out = jax.ShapeDtypeStruct((depth, rows), jnp.bfloat16)
    return pl.pallas_call(
        pair_kernel,
        out_shape=[out] * count,
        compiler_params=pltpu.CompilerParams(vmem_limit_bytes=32 * 2**20),
        cost_estimate=pl.CostEstimate(
            flops=count * depth * rows * 4, bytes_accessed=count * depth * rows * 6, transcendentals=0
        ),
        name="combine_line",
    )(mine, got)


def solution(mesh):
    return jax.shard_map(
        local,
        mesh=mesh,
        in_specs=(
            P("req", "tp"),
            P("req", "tp"),
            P("req", "tp"),
            P("req", "tp"),
            P("tp"),
            P("tp"),
            P("req", None, "tp"),
            P("req", None, "tp"),
            P(),
            P(),
            P(),
            P("tp", "req"),
            P("tp"),
            P(None, "tp"),
        ),
        out_specs=P("req", "tp"),
        check_vma=False,
    )
```

```python
import functools
import math

import jax
import jax.numpy as jnp
from jax import lax
from jax.experimental import pallas as pl
from jax.experimental.pallas import tpu as pltpu
from jax.sharding import PartitionSpec as P

HEAD_DIM = 128
EPSILON = 1e-06
LOW_SCORE = -1e30
PLANE = 4
PIECE = 16
LEVEL_ROWS = 32
SCORE_SCALE = math.log2(math.e) / math.sqrt(HEAD_DIM)


def send_xor(value, by):
    size = lax.axis_size("req")
    return lax.ppermute(value, "req", [(i, i ^ by) for i in range(size)])


def send_line(value, by):
    size = lax.axis_size("req")
    line = size // PLANE
    pairs = [(i, ((i // PLANE + by) % line) * PLANE + i % PLANE) for i in range(size)]
    return lax.ppermute(value, "req", pairs)


def group_count(width):
    return 4 if width // HEAD_DIM % 4 == 0 else 1


def send_tp(value, by):
    size = lax.axis_size("tp")
    return lax.ppermute(value, "tp", [(i, (i + by) % size) for i in range(size)])


def place_kernel(spots_ref, *refs):
    *blocks, _, out = refs
    for i, ref in enumerate(blocks):
        out[spots_ref[i]] = ref[...]


def place_blocks(spots, blocks, after):
    depth, width = blocks[0].shape
    chunk = next(c for c in (512, 256, 128) if width % c == 0)
    return pl.pallas_call(
        place_kernel,
        grid_spec=pltpu.PrefetchScalarGridSpec(
            num_scalar_prefetch=1,
            grid=(width // chunk,),
            in_specs=[pl.BlockSpec((depth, chunk), lambda i, *_: (0, i))] * len(blocks)
            + [pl.BlockSpec(memory_space=pl.ANY)],
            out_specs=pl.BlockSpec((len(blocks), depth, chunk), lambda i, *_: (0, 0, i)),
        ),
        out_shape=jax.ShapeDtypeStruct((len(blocks), depth, width), blocks[0].dtype),
        compiler_params=pltpu.CompilerParams(vmem_limit_bytes=16 * 2**20),
        name="place_weights",
    )(spots, *blocks, after)


def turn_kernel(q_ref, k_ref, scale_ref, gain_q_ref, gain_k_ref, cos_ref, sin_ref, _, q_out, k_out):
    cosine = cos_ref[...]
    sine = sin_ref[...]
    sides = ((q_ref, gain_q_ref, q_out), (k_ref, gain_k_ref, k_out))
    for side, (ref, gain, out) in enumerate(sides):
        scale = scale_ref[:, side : side + 1]
        for col in range(0, ref.shape[1], HEAD_DIM):
            cols = slice(col, col + HEAD_DIM)
            x = ref[:, cols].astype(jnp.float32) * scale * gain[:, cols]
            y = x * cosine + pltpu.roll(x, HEAD_DIM // 2, 1) * sine
            out[:, cols] = y.astype(jnp.bfloat16)


def turn(group, queries, new_keys, scales, gain_q, gain_k, cosine, sine, after):
    rows, width = queries.shape
    width = width // group_count(width)
    part = jax.ShapeDtypeStruct((rows, width), jnp.bfloat16)
    part_spec = pl.BlockSpec((rows, width), lambda i: (0, group))
    gain_spec = pl.BlockSpec((1, width), lambda i: (0, group))
    whole = lambda shape: pl.BlockSpec(shape, lambda i: (0, 0))
    return pl.pallas_call(
        turn_kernel,
        grid=(1,),
        in_specs=[
            part_spec,
            part_spec,
            whole(scales.shape),
            gain_spec,
            gain_spec,
            whole(cosine.shape),
            whole(sine.shape),
            pl.BlockSpec(memory_space=pl.ANY),
        ],
        out_specs=[whole(part.shape), whole(part.shape)],
        out_shape=[part, part],
        compiler_params=pltpu.CompilerParams(vmem_limit_bytes=16 * 2**20),
        name="norm_turn",
    )(queries, new_keys, scales, gain_q[None], gain_k[None], cosine, sine, after)


def attend_kernel(
    table_ref,
    slot_ref,
    q_low_ref,
    q_high_ref,
    keys_ref,
    values_ref,
    near_keys_ref,
    near_values_ref,
    near_starts_ref,
    keep_ref,
    send_ref,
    q_all,
    acc,
    peak,
    total,
    sems,
):
    step = pl.program_id(0)
    half, rows, width = q_low_ref.shape
    blocks = 2 * half
    heads = width // HEAD_DIM
    lane = lax.broadcasted_iota(jnp.int32, (1, rows), 1)

    def update(slots, keys_ref, values_ref, masks, allowed):
        ones = jnp.ones((PIECE, keys_ref.shape[0]), jnp.bfloat16)
        mask = jnp.concatenate(masks, axis=1)
        old_peak = jnp.concatenate([peak[s] for s in slots], axis=1)
        old_total = jnp.concatenate([total[s] for s in slots], axis=1)
        scores, weights, tops, fades = {}, {}, {}, {}

        def score(h):
            cols = slice(h * HEAD_DIM, (h + 1) * HEAD_DIM)
            q = jnp.concatenate([q_all[s, :, cols] for s in slots], axis=0)
            scores[h] = lax.dot_general(
                keys_ref[:, cols], q, (((1,), (1,)), ((), ())), preferred_element_type=jnp.float32
            )

        def weigh(h):
            found = scores.pop(h)
            if allowed is not None:
                found = jnp.where(allowed, found, LOW_SCORE)
            before = old_peak[h : h + 1]
            top = jnp.maximum(jnp.max(found, axis=0, keepdims=True), before)
            tops[h] = jnp.where(mask, top, before)
            fades[h] = jnp.where(mask, jnp.exp2(before - top), 1.0)
            weights[h] = jnp.exp2(found - jnp.where(mask, top, -LOW_SCORE)).astype(jnp.bfloat16)

        def blend(h):
            cols = slice(h * HEAD_DIM, (h + 1) * HEAD_DIM)
            values = jnp.concatenate([values_ref[:, cols].T, ones], axis=0)
            blended = jnp.dot(values, weights.pop(h), preferred_element_type=jnp.float32)
            fade = fades.pop(h)
            held = [acc[s, cols, :] for s in slots]
            sums = old_total[h : h + 1] * fade + blended[HEAD_DIM : HEAD_DIM + 1]
            for i, s in enumerate(slots):
                span = slice(i * rows, (i + 1) * rows)
                acc[s, cols, :] = held[i] * fade[:, span] + blended[:HEAD_DIM, span]
                peak[s, h : h + 1, :] = tops[h][:, span]
                total[s, h : h + 1, :] = sums[:, span]

        for h in range(heads + 2):
            if h < heads:
                score(h)
            if 1 <= h <= heads:
                weigh(h - 1)
            if h >= 2:
                blend(h - 2)

    @pl.when(step == 0)
    def _():
        low = pltpu.make_async_copy(q_low_ref, q_all.at[pl.ds(0, half)], sems.at[0])
        high = pltpu.make_async_copy(q_high_ref, q_all.at[pl.ds(half, half)], sems.at[1])
        low.start()
        high.start()
        q_all[blocks] = jnp.zeros((rows, width), jnp.bfloat16)
        acc[...] = jnp.zeros_like(acc)
        peak[...] = jnp.full(peak.shape, LOW_SCORE, jnp.float32)
        total[...] = jnp.zeros_like(total)
        low.wait()
        high.wait()
        first = slot_ref[blocks + 1]

        def near_pair(j, carry):
            low = first + 2 * j
            row = low * rows + jnp.concatenate([lane, lane + rows], axis=1)
            begin = near_starts_ref[j]
            key = first * rows + lax.broadcasted_iota(jnp.int32, (rows, 2 * rows), 0)
            allowed = (key >= begin) & (key <= row)
            some = begin < (first + 1) * rows
            slots = [slot_ref[jnp.minimum(low + i, blocks)] for i in range(2)]
            masks = [some[:, :rows], some[:, rows:]]
            update(slots, near_keys_ref, near_values_ref, masks, allowed)
            return carry

        lax.fori_loop(0, 2, near_pair, 0)

    @pl.when(step > 0)
    def _():
        begin = table_ref[4 * step - 4]
        end = table_ref[4 * step - 3]
        first = table_ref[4 * step - 2]
        count = table_ref[4 * step - 1]

        def pair(j, carry):
            low = first + 2 * j
            row = low * rows + lane
            masks = [(r >= begin) & (r < end) for r in (row, row + rows)]
            slots = [slot_ref[low], slot_ref[low + 1]]
            update(slots, keys_ref.at[0], values_ref.at[0], masks, None)
            return carry

        lax.fori_loop(0, count, pair, 0)

    @pl.when(step == pl.num_programs(0) - 1)
    def _():
        for at, out in ((0, keep_ref), (half, send_ref)):

            def finish(i, carry, at=at, out=out):
                sums = jnp.maximum(total[at + i], 1.0)
                write_block(
                    out.at[i],
                    lambda h: acc[at + i, h * HEAD_DIM : (h + 1) * HEAD_DIM, :],
                    1.0 / sums,
                    peak[at + i] + jnp.log2(sums),
                    heads,
                )
                return carry

            lax.fori_loop(0, half, finish, 0)


def write_block(out, block, factors, levels, heads):
    for h in range(heads):
        out[h * HEAD_DIM : (h + 1) * HEAD_DIM, :] = (block(h) * factors[h : h + 1]).astype(jnp.bfloat16)
    first = levels.astype(jnp.bfloat16).astype(jnp.float32)
    second = (levels - first).astype(jnp.bfloat16).astype(jnp.float32)
    third = levels - first - second
    stacked = jnp.concatenate([first, second, third, jnp.zeros_like(levels)], axis=0)
    out[heads * HEAD_DIM :, :] = stacked.astype(jnp.bfloat16)


def read_levels(ref, heads):
    stacked = ref[heads * HEAD_DIM :, :].astype(jnp.float32)
    return stacked[:8] + (stacked[8:16] + stacked[16:24])


def attend(group, table, slots, q_low, q_high, cache_keys, cache_values, near_keys, near_values, near_starts):
    half, rows, width = q_low.shape
    pages, page_len, _ = cache_keys.shape
    heads = width // HEAD_DIM
    blocks = 2 * half
    assert heads <= 8
    out = jax.ShapeDtypeStruct((half, width + LEVEL_ROWS, rows), jnp.bfloat16)
    page_spec = pl.BlockSpec((1, page_len, width), lambda i, *_: (jnp.maximum(i - 1, 0), 0, group))
    near_spec = pl.BlockSpec((rows, width), lambda i, *_: (0, group))
    own_spec = pl.BlockSpec((rows, width), lambda i, *_: (0, 0))
    whole = lambda shape: pl.BlockSpec(shape, lambda i, *_: (0,) * len(shape))
    return pl.pallas_call(
        attend_kernel,
        grid_spec=pltpu.PrefetchScalarGridSpec(
            num_scalar_prefetch=2,
            grid=(pages + 1,),
            in_specs=[
                pl.BlockSpec(memory_space=pl.ANY),
                pl.BlockSpec(memory_space=pl.ANY),
                page_spec,
                page_spec,
                own_spec,
                near_spec,
                whole((2, 1, 2 * rows)),
            ],
            out_specs=[whole(out.shape), whole(out.shape)],
            scratch_shapes=[
                pltpu.VMEM((blocks + 1, rows, width), jnp.bfloat16),
                pltpu.VMEM((blocks + 1, width, rows), jnp.float32),
                pltpu.VMEM((blocks + 1, 8, rows), jnp.float32),
                pltpu.VMEM((blocks + 1, 8, rows), jnp.float32),
                pltpu.SemaphoreType.DMA((2,)),
            ],
        ),
        out_shape=[out, out],
        compiler_params=pltpu.CompilerParams(
            dimension_semantics=("arbitrary",), vmem_limit_bytes=56 * 2**20
        ),
        cost_estimate=pl.CostEstimate(
            flops=pages * heads * 256 * page_len * HEAD_DIM * 40,
            bytes_accessed=pages * page_len * width * 4,
            transcendentals=pages * heads * 256 * page_len,
        ),
        name="cache_attend",
    )(table, slots, q_low, q_high, cache_keys, cache_values, near_keys, near_values, near_starts)


def merged(refs, heads):
    levels = [read_levels(ref, heads) for ref in refs]
    top = functools.reduce(jnp.maximum, levels)
    weights = [jnp.exp2(level - top) for level in levels]
    total = functools.reduce(jnp.add, weights)
    factors = [w / total for w in weights]

    def block(h):
        cols = slice(h * HEAD_DIM, (h + 1) * HEAD_DIM)
        return functools.reduce(
            jnp.add, [ref[cols, :].astype(jnp.float32) * f[h : h + 1] for ref, f in zip(refs, factors)]
        )

    return block, top + jnp.log2(total)


def combine_kernel(mine_low, mine_high, got_low, got_high, keep_ref, send_ref):
    heads = (mine_low.shape[1] - LEVEL_ROWS) // HEAD_DIM
    for mine, got, out in ((mine_low, got_low, keep_ref), (mine_high, got_high, send_ref)):
        block, levels = merged([mine.at[0], got.at[0]], heads)
        write_block(out.at[0], block, jnp.ones_like(levels), levels, heads)


def combine(mine, got):
    count, depth, rows = mine.shape
    half = count // 2
    low = pl.BlockSpec((1, depth, rows), lambda i: (i, 0, 0))
    high = pl.BlockSpec((1, depth, rows), lambda i: (i + half, 0, 0))
    out = jax.ShapeDtypeStruct((half, depth, rows), jnp.bfloat16)
    return pl.pallas_call(
        combine_kernel,
        grid=(half,),
        in_specs=[low, high, low, high],
        out_specs=[low, low],
        out_shape=[out, out],
        compiler_params=pltpu.CompilerParams(vmem_limit_bytes=24 * 2**20),
        cost_estimate=pl.CostEstimate(
            flops=count * depth * rows * 4, bytes_accessed=count * depth * rows * 6, transcendentals=0
        ),
        name="combine_pairs",
    )(mine, mine, got, got)


def last_kernel(*refs):
    out_ref = refs[-1]
    heads = out_ref.shape[0] // HEAD_DIM
    block, _ = merged(refs[:-1], heads)
    for h in range(heads):
        out_ref[h * HEAD_DIM : (h + 1) * HEAD_DIM, :] = block(h).astype(jnp.bfloat16)


def combine_last(parts):
    depth, rows = parts[0].shape
    return pl.pallas_call(
        last_kernel,
        out_shape=jax.ShapeDtypeStruct((depth - LEVEL_ROWS, rows), jnp.bfloat16),
        compiler_params=pltpu.CompilerParams(vmem_limit_bytes=24 * 2**20),
        cost_estimate=pl.CostEstimate(
            flops=len(parts) * depth * rows * 2,
            bytes_accessed=(len(parts) + 1) * depth * rows * 2,
            transcendentals=0,
        ),
        name="combine_last",
    )(*parts)


def local(
    hidden_in,
    queries,
    new_keys,
    new_values,
    query_gain,
    key_gain,
    cache_keys,
    cache_values,
    seg_ids,
    cache_pages,
    page_table,
    out_weight,
    out_bias,
    gate_mod,
):
    tok_dev, local_width = queries.shape
    size = lax.axis_size("req")
    tp_size = lax.axis_size("tp")
    model_width = local_width * tp_size
    line = size // PLANE
    device = lax.axis_index("req")
    spot = device % PLANE
    place = device // PLANE
    slot_count, page_len, _ = cache_keys.shape
    request_count = cache_pages.shape[0]
    total_pages = page_table.shape[0]
    first_row = device * tok_dev
    own_rows = first_row + jnp.arange(tok_dev, dtype=jnp.int32)
    own_segs = lax.dynamic_slice_in_dim(seg_ids, first_row, tok_dev, 0)
    req_ids = jnp.arange(request_count, dtype=jnp.int32)
    starts = jnp.sum((seg_ids[None, :] < req_ids[:, None]).astype(jnp.int32), axis=1)
    ends = jnp.sum((seg_ids[None, :] <= req_ids[:, None]).astype(jnp.int32), axis=1)
    own_pick = own_segs[:, None] == req_ids[None, :]
    own_start = jnp.sum(jnp.where(own_pick, starts[None, :], 0), axis=1)
    own_cache = jnp.sum(jnp.where(own_pick, cache_pages[None, :], 0), axis=1)
    positions = own_cache * page_len + own_rows - own_start

    wide_q = queries.astype(jnp.float32)
    wide_k = new_keys.astype(jnp.float32)
    sums = lax.psum(
        jnp.stack([jnp.sum(wide_q * wide_q, axis=1), jnp.sum(wide_k * wide_k, axis=1)], axis=1), "tp"
    )
    scales = lax.rsqrt(sums / model_width + EPSILON) * jnp.array([[SCORE_SCALE, 1.0]], jnp.float32)
    halfway = HEAD_DIM // 2
    frequency = 10000.0 ** (-jnp.arange(halfway, dtype=jnp.float32) / halfway)
    angles = positions.astype(jnp.float32)[:, None] * frequency[None, :]
    cosine = jnp.cos(angles)
    sine = jnp.sin(angles)
    cosine = jnp.concatenate([cosine, cosine], axis=1)
    sine = jnp.concatenate([-sine, sine], axis=1)

    physical = device * slot_count + jnp.arange(slot_count, dtype=jnp.int32)
    logical = jnp.sum(
        jnp.where(
            page_table[None, :] == physical[:, None],
            jnp.arange(total_pages, dtype=jnp.int32)[None, :],
            0,
        ),
        axis=1,
    )
    page_ends = jnp.cumsum(cache_pages)
    owners = jnp.sum((page_ends[None, :] <= logical[:, None]).astype(jnp.int32), axis=1)
    owner_pick = owners[:, None] == req_ids[None, :]
    owner_starts = jnp.sum(jnp.where(owner_pick, starts[None, :], 0), axis=1)
    owner_ends = jnp.sum(jnp.where(owner_pick, ends[None, :], 0), axis=1)
    owner_first = owner_starts // tok_dev
    owner_pairs = ((owner_ends - 1) // tok_dev - owner_first + 2) // 2
    table = jnp.stack([owner_starts, owner_ends, owner_first, owner_pairs], axis=1).reshape(-1)

    near_blocks = device + jnp.arange(4, dtype=jnp.int32)
    near_rows = (near_blocks[:, None] * tok_dev + jnp.arange(tok_dev, dtype=jnp.int32)[None, :]).reshape(-1)
    padded_segs = jnp.concatenate([seg_ids, jnp.full((3 * tok_dev,), -1, jnp.int32)])
    near_segs = lax.dynamic_slice_in_dim(padded_segs, first_row, 4 * tok_dev, 0)
    near_starts = jnp.sum(
        jnp.where(near_segs[:, None] == req_ids[None, :], starts[None, :], 0), axis=1
    )
    near_starts = jnp.where(near_segs < 0, near_rows + size * tok_dev, near_starts)
    near_starts = near_starts.reshape(2, 1, 2 * tok_dev)

    block = jnp.arange(size, dtype=jnp.int32)
    back = (place - block // PLANE) % line
    across = (block % PLANE) ^ spot

    def order_of(group):
        return (2, 1) if group % 2 == 0 else (1, 2)

    groups = group_count(local_width)
    near, near_keys, low, high = [], [], [], []
    for group in range(groups):
        after = [scales, near, low, high][min(group, 3)]
        after = after if group == 0 else after[0]
        part, key_part = turn(
            group, queries, new_keys, scales, query_gain, key_gain, cosine, sine, after
        )
        got = [part[None]] + [send_line(part, k)[None] for k in range(1, line)]
        near.append(lax.optimization_barrier(jnp.concatenate(got, axis=0)))
        near_keys.append(key_part)
        order = order_of(group)
        low.append(jnp.concatenate([near[group], send_xor(near[group], order[0])], axis=0))
        high.append(send_xor(low[group], order[1]))

    weight, _ = lax.optimization_barrier((out_weight.T, near[-1]))
    weights = [weight]
    for _ in range(1, line):
        weights.append(send_line(weights[-1], 1))

    attended = []
    for group in range(groups):
        order = order_of(group)
        slot = jnp.where((across & order[1]) > 0, 2 * line, 0)
        slot = slot + jnp.where((across & order[0]) > 0, line, 0) + back
        slots = jnp.concatenate([slot, jnp.stack([jnp.int32(size), device])])
        keep, send = attend(
            group, table, slots, low[group], high[group], cache_keys, cache_values,
            near_keys[group], new_values, near_starts,
        )
        if group == groups - 1:
            after = keep
        keep, send = combine(keep, send_xor(send, order[1]))
        parts = combine_line(keep, send_xor(send, order[0]))
        attended.append(combine_last([parts[0]] + [send_line(parts[k], -k) for k in range(1, line)]))

    columns = weight.shape[0]
    blocks_each = line // tp_size
    tp_device = lax.axis_index("tp")
    from_place = (place - jnp.arange(line, dtype=jnp.int32)) % line
    weight_spots = ((from_place // blocks_each - tp_device) % tp_size) * blocks_each
    weight_spots = weight_spots + from_place % blocks_each
    weights = place_blocks(weight_spots, weights, after)
    weights = weights.reshape(tp_size, blocks_each * columns, local_width)
    weights = [weights[0]] + [send_tp(weights[k], k) for k in range(1, tp_size)]

    projected = 0.0
    depth = 0
    for some in ([attended[:-1], attended[-1:]] if groups > 1 else [attended]):
        some = jnp.concatenate(some, axis=0)
        spread = jnp.concatenate([some] + [send_xor(some, k) for k in range(1, PLANE)], axis=1)
        for k in range(tp_size):
            part = spread if k == 0 else send_tp(spread, k)
            projected = projected + jnp.dot(
                weights[k][:, depth : depth + some.shape[0]], part, preferred_element_type=jnp.float32
            )
        depth += some.shape[0]
    sent = projected.astype(jnp.bfloat16)
    mine = [projected[:, :tok_dev]] + [
        send_xor(sent[:, k * tok_dev : (k + 1) * tok_dev], k).astype(jnp.float32) for k in range(1, PLANE)
    ]
    mine = [part.reshape(blocks_each, columns, tok_dev) for part in mine]
    swapped = [jnp.where((spot & 1) > 0, mine[i ^ 1], mine[i]) for i in range(PLANE)]
    swapped = [jnp.where((spot & 2) > 0, swapped[i ^ 2], swapped[i]) for i in range(PLANE)]
    projected = jnp.stack(swapped, axis=1).reshape(local_width, tok_dev).T

    gate_rows = jnp.dot(own_pick.astype(jnp.float32), gate_mod, precision=lax.Precision.HIGHEST)
    return (hidden_in.astype(jnp.float32) + gate_rows * (projected + out_bias[None, :])).astype(
        jnp.bfloat16
    )


def pair_kernel(mine, got, *outs):
    heads = (mine.shape[1] - LEVEL_ROWS) // HEAD_DIM
    for i, out in enumerate(outs):
        block, levels = merged([mine.at[i], got.at[i]], heads)
        write_block(out, block, jnp.ones_like(levels), levels, heads)


def combine_line(mine, got):
    count, depth, rows = mine.shape
    out = jax.ShapeDtypeStruct((depth, rows), jnp.bfloat16)
    return pl.pallas_call(
        pair_kernel,
        out_shape=[out] * count,
        compiler_params=pltpu.CompilerParams(vmem_limit_bytes=32 * 2**20),
        cost_estimate=pl.CostEstimate(
            flops=count * depth * rows * 4, bytes_accessed=count * depth * rows * 6, transcendentals=0
        ),
        name="combine_line",
    )(mine, got)


def solution(mesh):
    return jax.shard_map(
        local,
        mesh=mesh,
        in_specs=(
            P("req", "tp"),
            P("req", "tp"),
            P("req", "tp"),
            P("req", "tp"),
            P("tp"),
            P("tp"),
            P("req", None, "tp"),
            P("req", None, "tp"),
            P(),
            P(),
            P(),
            P("tp", "req"),
            P("tp"),
            P(None, "tp"),
        ),
        out_specs=P("req", "tp"),
        check_vma=False,
    )
```

```python
import functools
import math

import jax
import jax.numpy as jnp
from jax import lax
from jax.experimental import pallas as pl
from jax.experimental.pallas import tpu as pltpu
from jax.sharding import PartitionSpec as P

HEAD_DIM = 128
EPSILON = 1e-06
LOW_SCORE = -1e30
PLANE = 4
PIECE = 16
LEVEL_ROWS = 32
SCORE_SCALE = math.log2(math.e) / math.sqrt(HEAD_DIM)


def send_xor(value, by):
    size = lax.axis_size("req")
    return lax.ppermute(value, "req", [(i, i ^ by) for i in range(size)])


def group_count(width):
    return 4 if width // HEAD_DIM % 4 == 0 else 1


def send_tp(value, by):
    size = lax.axis_size("tp")
    return lax.ppermute(value, "tp", [(i, (i + by) % size) for i in range(size)])


def turn_kernel(q_ref, k_ref, scale_ref, gain_q_ref, gain_k_ref, cos_ref, sin_ref, _, q_out, k_out):
    cosine = cos_ref[...]
    sine = sin_ref[...]
    sides = ((q_ref, gain_q_ref, q_out), (k_ref, gain_k_ref, k_out))
    for side, (ref, gain, out) in enumerate(sides):
        scale = scale_ref[:, side : side + 1]
        for col in range(0, ref.shape[1], HEAD_DIM):
            cols = slice(col, col + HEAD_DIM)
            x = ref[:, cols].astype(jnp.float32) * scale * gain[:, cols]
            y = x * cosine + pltpu.roll(x, HEAD_DIM // 2, 1) * sine
            out[:, cols] = y.astype(jnp.bfloat16)


def turn(group, queries, new_keys, scales, gain_q, gain_k, cosine, sine, after):
    rows, width = queries.shape
    width = width // group_count(width)
    part = jax.ShapeDtypeStruct((rows, width), jnp.bfloat16)
    part_spec = pl.BlockSpec((rows, width), lambda i: (0, group))
    gain_spec = pl.BlockSpec((1, width), lambda i: (0, group))
    whole = lambda shape: pl.BlockSpec(shape, lambda i: (0, 0))
    return pl.pallas_call(
        turn_kernel,
        grid=(1,),
        in_specs=[
            part_spec,
            part_spec,
            whole(scales.shape),
            gain_spec,
            gain_spec,
            whole(cosine.shape),
            whole(sine.shape),
            pl.BlockSpec(memory_space=pl.ANY),
        ],
        out_specs=[whole(part.shape), whole(part.shape)],
        out_shape=[part, part],
        compiler_params=pltpu.CompilerParams(vmem_limit_bytes=16 * 2**20),
        name="norm_turn",
    )(queries, new_keys, scales, gain_q[None], gain_k[None], cosine, sine, after)


def attend_kernel(
    table_ref,
    slot_ref,
    q_slot_ref,
    *refs,
):
    *q_refs, keys_ref, values_ref, near_keys_ref, near_values_ref, near_starts_ref, _, _ = refs[:-7]
    keep_ref, send_ref, q_all, acc, peak, total, sems = refs[-7:]
    step = pl.program_id(0)
    half, _, rows = keep_ref.shape
    width = acc.shape[1]
    blocks = 2 * half
    heads = width // HEAD_DIM
    lane = lax.broadcasted_iota(jnp.int32, (1, rows), 1)

    def update(slots, q_slots, keys_ref, values_ref, masks, allowed):
        ones = jnp.ones((PIECE, keys_ref.shape[0]), jnp.bfloat16)
        mask = jnp.concatenate(masks, axis=1)
        old_peak = jnp.concatenate([peak[s] for s in slots], axis=1)
        old_total = jnp.concatenate([total[s] for s in slots], axis=1)
        scores, weights, tops, fades = {}, {}, {}, {}

        def score(h):
            cols = slice(h * HEAD_DIM, (h + 1) * HEAD_DIM)
            q = jnp.concatenate([q_all[s, :, cols] for s in q_slots], axis=0)
            scores[h] = lax.dot_general(
                keys_ref[:, cols], q, (((1,), (1,)), ((), ())), preferred_element_type=jnp.float32
            )

        def weigh(h):
            found = scores.pop(h)
            if allowed is not None:
                found = jnp.where(allowed, found, LOW_SCORE)
            before = old_peak[h : h + 1]
            top = jnp.maximum(jnp.max(found, axis=0, keepdims=True), before)
            tops[h] = jnp.where(mask, top, before)
            fades[h] = jnp.where(mask, jnp.exp2(before - top), 1.0)
            weights[h] = jnp.exp2(found - jnp.where(mask, top, -LOW_SCORE)).astype(jnp.bfloat16)

        def blend(h):
            cols = slice(h * HEAD_DIM, (h + 1) * HEAD_DIM)
            values = jnp.concatenate([values_ref[:, cols].T, ones], axis=0)
            blended = jnp.dot(values, weights.pop(h), preferred_element_type=jnp.float32)
            fade = fades.pop(h)
            held = [acc[s, cols, :] for s in slots]
            sums = old_total[h : h + 1] * fade + blended[HEAD_DIM : HEAD_DIM + 1]
            for i, s in enumerate(slots):
                span = slice(i * rows, (i + 1) * rows)
                acc[s, cols, :] = held[i] * fade[:, span] + blended[:HEAD_DIM, span]
                peak[s, h : h + 1, :] = tops[h][:, span]
                total[s, h : h + 1, :] = sums[:, span]

        for h in range(heads + 2):
            if h < heads:
                score(h)
            if 1 <= h <= heads:
                weigh(h - 1)
            if h >= 2:
                blend(h - 2)

    @pl.when(step == 0)
    def _():
        share = blocks // len(q_refs)
        copies = [
            pltpu.make_async_copy(ref, q_all.at[pl.ds(i * share, share)], sems.at[i])
            for i, ref in enumerate(q_refs)
        ]
        for copy in copies:
            copy.start()
        q_all[blocks] = jnp.zeros((rows, width), jnp.bfloat16)
        acc[...] = jnp.zeros_like(acc)
        peak[...] = jnp.full(peak.shape, LOW_SCORE, jnp.float32)
        total[...] = jnp.zeros_like(total)
        for copy in copies:
            copy.wait()
        first = slot_ref[blocks + 1]

        def near_pair(j, carry):
            low = first + 2 * j
            row = low * rows + jnp.concatenate([lane, lane + rows], axis=1)
            begin = near_starts_ref[j]
            key = first * rows + lax.broadcasted_iota(jnp.int32, (rows, 2 * rows), 0)
            allowed = (key >= begin) & (key <= row)
            some = begin < (first + 1) * rows
            at = [jnp.minimum(low + i, blocks) for i in range(2)]
            slots, q_slots = [slot_ref[i] for i in at], [q_slot_ref[i] for i in at]
            masks = [some[:, :rows], some[:, rows:]]
            update(slots, q_slots, near_keys_ref, near_values_ref, masks, allowed)
            return carry

        lax.fori_loop(0, 2, near_pair, 0)

    @pl.when(step > 0)
    def _():
        begin = table_ref[4 * step - 4]
        end = table_ref[4 * step - 3]
        first = table_ref[4 * step - 2]
        count = table_ref[4 * step - 1]

        def pair(j, carry):
            low = first + 2 * j
            row = low * rows + lane
            masks = [(r >= begin) & (r < end) for r in (row, row + rows)]
            slots = [slot_ref[low], slot_ref[low + 1]]
            q_slots = [q_slot_ref[low], q_slot_ref[low + 1]]
            update(slots, q_slots, keys_ref.at[0], values_ref.at[0], masks, None)
            return carry

        lax.fori_loop(0, count, pair, 0)

    @pl.when(step == pl.num_programs(0) - 1)
    def _():
        for at, out in ((0, keep_ref), (half, send_ref)):

            def finish(i, carry, at=at, out=out):
                sums = jnp.maximum(total[at + i], 1.0)
                write_block(
                    out.at[i],
                    lambda h: acc[at + i, h * HEAD_DIM : (h + 1) * HEAD_DIM, :],
                    1.0 / sums,
                    peak[at + i] + jnp.log2(sums),
                    heads,
                )
                return carry

            lax.fori_loop(0, half, finish, 0)


def write_block(out, block, factors, levels, heads):
    for h in range(heads):
        out[h * HEAD_DIM : (h + 1) * HEAD_DIM, :] = (block(h) * factors[h : h + 1]).astype(jnp.bfloat16)
    first = levels.astype(jnp.bfloat16).astype(jnp.float32)
    second = (levels - first).astype(jnp.bfloat16).astype(jnp.float32)
    third = levels - first - second
    stacked = jnp.concatenate([first, second, third, jnp.zeros_like(levels)], axis=0)
    out[heads * HEAD_DIM :, :] = stacked.astype(jnp.bfloat16)


def read_levels(ref, heads):
    stacked = ref[heads * HEAD_DIM :, :].astype(jnp.float32)
    return stacked[:8] + (stacked[8:16] + stacked[16:24])


def attend(
    group, table, slots, q_slots, q_parts, cache_keys, cache_values, near_keys, near_values, near_starts, after
):
    rows, width = near_keys.shape
    half = sum(part.shape[0] for part in q_parts) // 2
    pages, page_len, _ = cache_keys.shape
    heads = width // HEAD_DIM
    blocks = 2 * half
    assert heads <= 8
    out = jax.ShapeDtypeStruct((half, width + LEVEL_ROWS, rows), jnp.bfloat16)
    page_spec = pl.BlockSpec((1, page_len, width), lambda i, *_: (jnp.maximum(i - 1, 0), 0, group))
    near_spec = pl.BlockSpec((rows, width), lambda i, *_: (0, group))
    own_spec = pl.BlockSpec((rows, width), lambda i, *_: (0, 0))
    whole = lambda shape: pl.BlockSpec(shape, lambda i, *_: (0,) * len(shape))
    return pl.pallas_call(
        attend_kernel,
        grid_spec=pltpu.PrefetchScalarGridSpec(
            num_scalar_prefetch=3,
            grid=(pages + 1,),
            in_specs=[pl.BlockSpec(memory_space=pl.ANY)] * len(q_parts)
            + [
                page_spec,
                page_spec,
                own_spec,
                near_spec,
                whole((2, 1, 2 * rows)),
                pl.BlockSpec(memory_space=pl.ANY),
                pl.BlockSpec(memory_space=pl.ANY),
            ],
            out_specs=[whole(out.shape), whole(out.shape)],
            scratch_shapes=[
                pltpu.VMEM((blocks + 1, rows, width), jnp.bfloat16),
                pltpu.VMEM((blocks + 1, width, rows), jnp.float32),
                pltpu.VMEM((blocks + 1, 8, rows), jnp.float32),
                pltpu.VMEM((blocks + 1, 8, rows), jnp.float32),
                pltpu.SemaphoreType.DMA((2,)),
            ],
        ),
        out_shape=[out, out],
        compiler_params=pltpu.CompilerParams(
            dimension_semantics=("arbitrary",), vmem_limit_bytes=56 * 2**20
        ),
        cost_estimate=pl.CostEstimate(
            flops=pages * heads * 256 * page_len * HEAD_DIM * 40,
            bytes_accessed=pages * page_len * width * 4,
            transcendentals=pages * heads * 256 * page_len,
        ),
        name="cache_attend",
    )(table, slots, q_slots, *q_parts, cache_keys, cache_values, near_keys, near_values, near_starts, *after)


def merged(refs, heads):
    levels = [read_levels(ref, heads) for ref in refs]
    top = functools.reduce(jnp.maximum, levels)
    weights = [jnp.exp2(level - top) for level in levels]
    total = functools.reduce(jnp.add, weights)
    factors = [w / total for w in weights]

    def block(h):
        cols = slice(h * HEAD_DIM, (h + 1) * HEAD_DIM)
        return functools.reduce(
            jnp.add, [ref[cols, :].astype(jnp.float32) * f[h : h + 1] for ref, f in zip(refs, factors)]
        )

    return block, top + jnp.log2(total)


def combine_kernel(mine_low, mine_high, got_low, got_high, _, keep_ref, send_ref):
    heads = (mine_low.shape[1] - LEVEL_ROWS) // HEAD_DIM
    for mine, got, out in ((mine_low, got_low, keep_ref), (mine_high, got_high, send_ref)):
        block, levels = merged([mine.at[0], got.at[0]], heads)
        write_block(out.at[0], block, jnp.ones_like(levels), levels, heads)


def combine(mine, got, after):
    count, depth, rows = mine.shape
    half = count // 2
    low = pl.BlockSpec((1, depth, rows), lambda i: (i, 0, 0))
    high = pl.BlockSpec((1, depth, rows), lambda i: (i + half, 0, 0))
    out = jax.ShapeDtypeStruct((half, depth, rows), jnp.bfloat16)
    return pl.pallas_call(
        combine_kernel,
        grid=(half,),
        in_specs=[low, high, low, high, pl.BlockSpec(memory_space=pl.ANY)],
        out_specs=[low, low],
        out_shape=[out, out],
        compiler_params=pltpu.CompilerParams(vmem_limit_bytes=24 * 2**20),
        cost_estimate=pl.CostEstimate(
            flops=count * depth * rows * 4, bytes_accessed=count * depth * rows * 6, transcendentals=0
        ),
        name="combine_pairs",
    )(mine, mine, got, got, after)


def last_kernel(*refs):
    out_ref = refs[-1]
    heads = out_ref.shape[0] // HEAD_DIM
    block, _ = merged(refs[:-2], heads)
    for h in range(heads):
        out_ref[h * HEAD_DIM : (h + 1) * HEAD_DIM, :] = block(h).astype(jnp.bfloat16)


def combine_last(parts, after):
    depth, rows = parts[0].shape
    whole = pl.BlockSpec(memory_space=pltpu.VMEM)
    return pl.pallas_call(
        last_kernel,
        in_specs=[whole] * len(parts) + [pl.BlockSpec(memory_space=pl.ANY)],
        out_shape=jax.ShapeDtypeStruct((depth - LEVEL_ROWS, rows), jnp.bfloat16),
        compiler_params=pltpu.CompilerParams(vmem_limit_bytes=24 * 2**20),
        cost_estimate=pl.CostEstimate(
            flops=len(parts) * depth * rows * 2,
            bytes_accessed=(len(parts) + 1) * depth * rows * 2,
            transcendentals=0,
        ),
        name="combine_last",
    )(*parts, after)


def local(
    hidden_in,
    queries,
    new_keys,
    new_values,
    query_gain,
    key_gain,
    cache_keys,
    cache_values,
    seg_ids,
    cache_pages,
    page_table,
    out_weight,
    out_bias,
    gate_mod,
):
    tok_dev, local_width = queries.shape
    size = lax.axis_size("req")
    tp_size = lax.axis_size("tp")
    model_width = local_width * tp_size
    line = size // PLANE
    device = lax.axis_index("req")
    spot = device % PLANE
    slot_count, page_len, _ = cache_keys.shape
    request_count = cache_pages.shape[0]
    total_pages = page_table.shape[0]
    first_row = device * tok_dev
    own_rows = first_row + jnp.arange(tok_dev, dtype=jnp.int32)
    own_segs = lax.dynamic_slice_in_dim(seg_ids, first_row, tok_dev, 0)
    req_ids = jnp.arange(request_count, dtype=jnp.int32)
    starts = jnp.sum((seg_ids[None, :] < req_ids[:, None]).astype(jnp.int32), axis=1)
    ends = jnp.sum((seg_ids[None, :] <= req_ids[:, None]).astype(jnp.int32), axis=1)
    own_pick = own_segs[:, None] == req_ids[None, :]
    own_start = jnp.sum(jnp.where(own_pick, starts[None, :], 0), axis=1)
    own_cache = jnp.sum(jnp.where(own_pick, cache_pages[None, :], 0), axis=1)
    positions = own_cache * page_len + own_rows - own_start

    wide_q = queries.astype(jnp.float32)
    wide_k = new_keys.astype(jnp.float32)
    sums = lax.psum(
        jnp.stack([jnp.sum(wide_q * wide_q, axis=1), jnp.sum(wide_k * wide_k, axis=1)], axis=1), "tp"
    )
    scales = lax.rsqrt(sums / model_width + EPSILON) * jnp.array([[SCORE_SCALE, 1.0]], jnp.float32)
    halfway = HEAD_DIM // 2
    frequency = 10000.0 ** (-jnp.arange(halfway, dtype=jnp.float32) / halfway)
    angles = positions.astype(jnp.float32)[:, None] * frequency[None, :]
    cosine = jnp.cos(angles)
    sine = jnp.sin(angles)
    cosine = jnp.concatenate([cosine, cosine], axis=1)
    sine = jnp.concatenate([-sine, sine], axis=1)

    physical = device * slot_count + jnp.arange(slot_count, dtype=jnp.int32)
    logical = jnp.sum(
        jnp.where(
            page_table[None, :] == physical[:, None],
            jnp.arange(total_pages, dtype=jnp.int32)[None, :],
            0,
        ),
        axis=1,
    )
    page_ends = jnp.cumsum(cache_pages)
    owners = jnp.sum((page_ends[None, :] <= logical[:, None]).astype(jnp.int32), axis=1)
    owner_pick = owners[:, None] == req_ids[None, :]
    owner_starts = jnp.sum(jnp.where(owner_pick, starts[None, :], 0), axis=1)
    owner_ends = jnp.sum(jnp.where(owner_pick, ends[None, :], 0), axis=1)
    owner_first = owner_starts // tok_dev
    owner_pairs = ((owner_ends - 1) // tok_dev - owner_first + 2) // 2
    table = jnp.stack([owner_starts, owner_ends, owner_first, owner_pairs], axis=1).reshape(-1)

    near_blocks = device + jnp.arange(4, dtype=jnp.int32)
    near_rows = (near_blocks[:, None] * tok_dev + jnp.arange(tok_dev, dtype=jnp.int32)[None, :]).reshape(-1)
    padded_segs = jnp.concatenate([seg_ids, jnp.full((3 * tok_dev,), -1, jnp.int32)])
    near_segs = lax.dynamic_slice_in_dim(padded_segs, first_row, 4 * tok_dev, 0)
    near_starts = jnp.sum(
        jnp.where(near_segs[:, None] == req_ids[None, :], starts[None, :], 0), axis=1
    )
    near_starts = jnp.where(near_segs < 0, near_rows + size * tok_dev, near_starts)
    near_starts = near_starts.reshape(2, 1, 2 * tok_dev)

    apart = jnp.arange(size, dtype=jnp.int32) ^ device
    beyond = jnp.stack([jnp.int32(size), device])
    natural = jnp.concatenate([jnp.arange(size, dtype=jnp.int32), beyond])
    masks = [1 << i for i in range((size - 1).bit_length())]
    columns = out_weight.shape[1]
    blocks_each = line // tp_size
    tp_device = lax.axis_index("tp")

    groups = group_count(local_width)
    orders = [masks if group in (0, 3) else [2, 1] + masks[2:] for group in range(groups)]
    slots = []
    for order in orders:
        slot = sum(jnp.where((apart & m) > 0, size >> (i + 1), 0) for i, m in enumerate(order))
        slots.append(jnp.concatenate([slot, beyond]))
    gathered, near_keys = [], []
    after = scales
    for group in range(groups):
        part, key_part = turn(
            group, queries, new_keys, scales, query_gain, key_gain, cosine, sine, after
        )
        near_keys.append(key_part)
        after = along_line if group == 2 else key_part
        if group % 2 == 0:
            gathered.append([lax.all_gather(part[None], "req", axis=0, tiled=True)])
            continue
        held, stages = part[None], []
        for m in orders[group][:0:-1]:
            held = lax.optimization_barrier(jnp.concatenate([held, send_xor(held, m)], axis=0))
            stages.append(held)
            if held.shape[0] == line and group == 1:
                along_line = held
        gathered.append([held, send_xor(held, orders[group][0])])
    weight, _ = lax.optimization_barrier((out_weight.T, near_keys[-1]))
    lines = [[z * PLANE + p for z in range(line)] for p in range(PLANE)]
    weight = lax.all_gather(weight, "req", axis=0, tiled=True, axis_index_groups=lines)

    weight = weight.reshape(tp_size, blocks_each * columns, local_width)
    weights = []
    for k in range(tp_size):
        part = lax.dynamic_index_in_dim(weight, (tp_device + k) % tp_size, 0, keepdims=False)
        weights.append(part if k == 0 else send_tp(part, k))

    waits = [near_starts] * 4
    if groups > 1:
        waits[:2] = stages[-2:]
    if groups > 1:
        turns = ((0, "a"), (1, "a"), (0, "c"), (3, "a"), (0, "c"), (1, "c"), (2, "a"))
        turns += ((3, "c"), (0, "c"), (1, "c"), (2, "c"), (0, "l"), (3, "c"), (1, "c"), (2, "c"))
        turns += ((1, "l"), (3, "c"), (2, "c"), (3, "l"), (2, "l"))
    else:
        turns = ((0, "a"),) + ((0, "c"),) * (len(masks) - 1) + ((0, "l"),)
    attended, state, left = [None] * groups, [None] * groups, [list(order) for order in orders]
    before = near_starts
    for group, step in turns:
        if step == "a":
            state[group] = attend(
                group, table, slots[group], natural if group % 2 == 0 else slots[group], gathered[group],
                cache_keys, cache_values, near_keys[group], new_values, near_starts, (before, waits[group]),
            )
            before = state[group][0]
        elif step == "c":
            keep, send = state[group]
            state[group] = combine(keep, send_xor(send, left[group].pop(0)), before)
            before = latest = state[group][0]
        else:
            if group == 3:
                before = weights[-1]
            keep, send = state[group]
            attended[group] = combine_last([keep[0], send_xor(send, left[group].pop(0))[0]], before)
            before = attended[group]
    if groups > 1:
        attended = [attended[group] for group in (0, 1, 3, 2)]
        attended[0], _ = lax.optimization_barrier((attended[0], latest))

    projected = 0.0
    share = local_width // groups
    if groups > 1:
        weight_sets = [[(0, 2 * share), (3 * share, 4 * share)], [(2 * share, 3 * share)]]
    else:
        weight_sets = [[(0, local_width)]]
    for some, spans in zip([attended[:-1], attended[-1:]] if groups > 1 else [attended], weight_sets):
        some = jnp.concatenate(some, axis=0)
        got = [send_xor(some, k) for k in range(1, PLANE)]
        *got, _ = lax.optimization_barrier((*got, attended[-1]))
        spread = jnp.concatenate([some] + got, axis=1)
        for k in range(tp_size):
            part = spread if k == 0 else send_tp(spread, k)
            at = 0
            for low, high in spans:
                projected = projected + jnp.dot(
                    weights[k][:, low:high],
                    part[at : at + high - low],
                    preferred_element_type=jnp.float32,
                )
                at += high - low
    sent = projected.astype(jnp.bfloat16)
    mine = [projected[:, :tok_dev]] + [
        send_xor(sent[:, k * tok_dev : (k + 1) * tok_dev], k).astype(jnp.float32) for k in range(1, PLANE)
    ]
    mine = [part.reshape(blocks_each, columns, tok_dev) for part in mine]
    swapped = [jnp.where((spot & 1) > 0, mine[i ^ 1], mine[i]) for i in range(PLANE)]
    swapped = [jnp.where((spot & 2) > 0, swapped[i ^ 2], swapped[i]) for i in range(PLANE)]
    projected = jnp.stack(swapped, axis=1).reshape(local_width, tok_dev).T

    gate_rows = jnp.dot(own_pick.astype(jnp.float32), gate_mod, precision=lax.Precision.HIGHEST)
    return (hidden_in.astype(jnp.float32) + gate_rows * (projected + out_bias[None, :])).astype(
        jnp.bfloat16
    )


def solution(mesh):
    return jax.shard_map(
        local,
        mesh=mesh,
        in_specs=(
            P("req", "tp"),
            P("req", "tp"),
            P("req", "tp"),
            P("req", "tp"),
            P("tp"),
            P("tp"),
            P("req", None, "tp"),
            P("req", None, "tp"),
            P(),
            P(),
            P(),
            P("tp", "req"),
            P("tp"),
            P(None, "tp"),
        ),
        out_specs=P("req", "tp"),
        check_vma=False,
    )
```

```python
import functools
import math

import jax
import jax.numpy as jnp
from jax import lax
from jax.experimental import pallas as pl
from jax.experimental.pallas import tpu as pltpu
from jax.sharding import PartitionSpec as P

HEAD_DIM = 128
EPSILON = 1e-06
LOW_SCORE = -1e30
PLANE = 4
PIECE = 16
LEVEL_ROWS = 32
SCORE_SCALE = math.log2(math.e) / math.sqrt(HEAD_DIM)


def send_xor(value, by):
    size = lax.axis_size("req")
    return lax.ppermute(value, "req", [(i, i ^ by) for i in range(size)])


def group_count(width):
    return 4 if width // HEAD_DIM % 4 == 0 else 1


def send_tp(value, by):
    size = lax.axis_size("tp")
    return lax.ppermute(value, "tp", [(i, (i + by) % size) for i in range(size)])


def turn_kernel(q_ref, k_ref, scale_ref, gain_q_ref, gain_k_ref, cos_ref, sin_ref, _, q_out, k_out):
    cosine = cos_ref[...]
    sine = sin_ref[...]
    sides = ((q_ref, gain_q_ref, q_out), (k_ref, gain_k_ref, k_out))
    for side, (ref, gain, out) in enumerate(sides):
        scale = scale_ref[:, side : side + 1]
        for col in range(0, ref.shape[1], HEAD_DIM):
            cols = slice(col, col + HEAD_DIM)
            x = ref[:, cols].astype(jnp.float32) * scale * gain[:, cols]
            y = x * cosine + pltpu.roll(x, HEAD_DIM // 2, 1) * sine
            out[:, cols] = y.astype(jnp.bfloat16)


def turn(group, queries, new_keys, scales, gain_q, gain_k, cosine, sine, after):
    rows, width = queries.shape
    width = width // group_count(width)
    part = jax.ShapeDtypeStruct((rows, width), jnp.bfloat16)
    part_spec = pl.BlockSpec((rows, width), lambda i: (0, group))
    gain_spec = pl.BlockSpec((1, width), lambda i: (0, group))
    whole = lambda shape: pl.BlockSpec(shape, lambda i: (0, 0))
    return pl.pallas_call(
        turn_kernel,
        grid=(1,),
        in_specs=[
            part_spec,
            part_spec,
            whole(scales.shape),
            gain_spec,
            gain_spec,
            whole(cosine.shape),
            whole(sine.shape),
            pl.BlockSpec(memory_space=pl.ANY),
        ],
        out_specs=[whole(part.shape), whole(part.shape)],
        out_shape=[part, part],
        compiler_params=pltpu.CompilerParams(vmem_limit_bytes=16 * 2**20),
        name="norm_turn",
    )(queries, new_keys, scales, gain_q[None], gain_k[None], cosine, sine, after)


def joined(parts, axis):
    return parts[0] if len(parts) == 1 else jnp.concatenate(parts, axis=axis)


def attend_kernel(
    q_column,
    table_ref,
    slot_ref,
    q_slot_ref,
    *refs,
):
    *q_refs, keys_ref, values_ref, near_keys_ref, near_values_ref, near_starts_ref, _, _ = refs[:-7]
    keep_ref, send_ref, q_all, acc, peak, total, sems = refs[-7:]
    step = pl.program_id(0)
    half, _, rows = keep_ref.shape
    width = acc.shape[1]
    blocks = 2 * half
    heads = width // HEAD_DIM
    lane = lax.broadcasted_iota(jnp.int32, (1, rows), 1)

    def update(slots, q_slots, keys_ref, values_ref, masks, allowed):
        ones = jnp.ones((PIECE, keys_ref.shape[0]), jnp.bfloat16)
        mask = joined(masks, 1)
        old_peak = joined([peak[s] for s in slots], 1)
        old_total = joined([total[s] for s in slots], 1)
        scores, weights, tops, fades = {}, {}, {}, {}

        def score(h):
            cols = slice(h * HEAD_DIM, (h + 1) * HEAD_DIM)
            q = joined([q_all[s, :, cols] for s in q_slots], 0)
            scores[h] = lax.dot_general(
                keys_ref[:, cols], q, (((1,), (1,)), ((), ())), preferred_element_type=jnp.float32
            )

        def weigh(h):
            found = scores.pop(h)
            if allowed is not None:
                found = jnp.where(allowed, found, LOW_SCORE)
            before = old_peak[h : h + 1]
            top = jnp.maximum(jnp.max(found, axis=0, keepdims=True), before)
            tops[h] = jnp.where(mask, top, before)
            fades[h] = jnp.where(mask, jnp.exp2(before - top), 1.0)
            weights[h] = jnp.exp2(found - jnp.where(mask, top, -LOW_SCORE)).astype(jnp.bfloat16)

        def blend(h):
            cols = slice(h * HEAD_DIM, (h + 1) * HEAD_DIM)
            values = jnp.concatenate([values_ref[:, cols].T, ones], axis=0)
            blended = jnp.dot(values, weights.pop(h), preferred_element_type=jnp.float32)
            fade = fades.pop(h)
            held = [acc[s, cols, :] for s in slots]
            sums = old_total[h : h + 1] * fade + blended[HEAD_DIM : HEAD_DIM + 1]
            for i, s in enumerate(slots):
                span = slice(i * rows, (i + 1) * rows)
                acc[s, cols, :] = held[i] * fade[:, span] + blended[:HEAD_DIM, span]
                peak[s, h : h + 1, :] = tops[h][:, span]
                total[s, h : h + 1, :] = sums[:, span]

        for h in range(heads + 2):
            if h < heads:
                score(h)
            if 1 <= h <= heads:
                weigh(h - 1)
            if h >= 2:
                blend(h - 2)

    @pl.when(step == 0)
    def _():
        share = blocks // len(q_refs)
        copies = [
            pltpu.make_async_copy(
                ref.at[:, :, pl.ds(q_column, width)], q_all.at[pl.ds(i * share, share)], sems.at[i]
            )
            for i, ref in enumerate(q_refs)
        ]
        for copy in copies:
            copy.start()
        q_all[blocks] = jnp.zeros((rows, width), jnp.bfloat16)
        acc[...] = jnp.zeros_like(acc)
        peak[...] = jnp.full(peak.shape, LOW_SCORE, jnp.float32)
        total[...] = jnp.zeros_like(total)
        for copy in copies:
            copy.wait()
        first = slot_ref[blocks + 1]

        def near_pair(j, carry):
            low = first + 2 * j
            row = low * rows + jnp.concatenate([lane, lane + rows], axis=1)
            begin = near_starts_ref[j]
            key = first * rows + lax.broadcasted_iota(jnp.int32, (rows, 2 * rows), 0)
            allowed = (key >= begin) & (key <= row)
            some = begin < (first + 1) * rows
            at = [jnp.minimum(low + i, blocks) for i in range(2)]
            slots, q_slots = [slot_ref[i] for i in at], [q_slot_ref[i] for i in at]
            masks = [some[:, :rows], some[:, rows:]]
            update(slots, q_slots, near_keys_ref, near_values_ref, masks, allowed)
            return carry

        lax.fori_loop(0, 2, near_pair, 0)

    @pl.when(step > 0)
    def _():
        begin = table_ref[4 * step - 4]
        end = table_ref[4 * step - 3]
        first = table_ref[4 * step - 2]
        count = table_ref[4 * step - 1]

        def visit(at):
            masks = [(b * rows + lane >= begin) & (b * rows + lane < end) for b in at]
            slots, q_slots = [slot_ref[b] for b in at], [q_slot_ref[b] for b in at]
            update(slots, q_slots, keys_ref.at[0], values_ref.at[0], masks, None)

        def pair(j, carry):
            visit([first + 2 * j, first + 2 * j + 1])
            return carry

        lax.fori_loop(0, count // 2, pair, 0)

        @pl.when(count % 2 == 1)
        def _():
            visit([first + count - 1])

    @pl.when(step == pl.num_programs(0) - 1)
    def _():
        for at, out in ((0, keep_ref), (half, send_ref)):

            def finish(i, carry, at=at, out=out):
                sums = jnp.maximum(total[at + i], 1.0)
                write_block(
                    out.at[i],
                    lambda h: acc[at + i, h * HEAD_DIM : (h + 1) * HEAD_DIM, :],
                    1.0 / sums,
                    peak[at + i] + jnp.log2(sums),
                    heads,
                )
                return carry

            lax.fori_loop(0, half, finish, 0)


def write_block(out, block, factors, levels, heads):
    for h in range(heads):
        out[h * HEAD_DIM : (h + 1) * HEAD_DIM, :] = (block(h) * factors[h : h + 1]).astype(jnp.bfloat16)
    first = levels.astype(jnp.bfloat16).astype(jnp.float32)
    second = (levels - first).astype(jnp.bfloat16).astype(jnp.float32)
    third = levels - first - second
    stacked = jnp.concatenate([first, second, third, jnp.zeros_like(levels)], axis=0)
    out[heads * HEAD_DIM :, :] = stacked.astype(jnp.bfloat16)


def read_levels(ref, heads):
    stacked = ref[heads * HEAD_DIM :, :].astype(jnp.float32)
    return stacked[:8] + (stacked[8:16] + stacked[16:24])


def attend(
    group, table, slots, q_slots, q_parts, cache_keys, cache_values, near_keys, near_values, near_starts, after
):
    rows, width = near_keys.shape
    half = sum(part.shape[0] for part in q_parts) // 2
    pages, page_len, _ = cache_keys.shape
    heads = width // HEAD_DIM
    blocks = 2 * half
    assert heads <= 8
    out = jax.ShapeDtypeStruct((half, width + LEVEL_ROWS, rows), jnp.bfloat16)
    page_spec = pl.BlockSpec((1, page_len, width), lambda i, *_: (jnp.maximum(i - 1, 0), 0, group))
    near_spec = pl.BlockSpec((rows, width), lambda i, *_: (0, group))
    own_spec = pl.BlockSpec((rows, width), lambda i, *_: (0, 0))
    whole = lambda shape: pl.BlockSpec(shape, lambda i, *_: (0,) * len(shape))
    q_column = group // 2 * width if len(q_parts) == 1 else 0
    return pl.pallas_call(
        functools.partial(attend_kernel, q_column),
        grid_spec=pltpu.PrefetchScalarGridSpec(
            num_scalar_prefetch=3,
            grid=(pages + 1,),
            in_specs=[pl.BlockSpec(memory_space=pl.ANY)] * len(q_parts)
            + [
                page_spec,
                page_spec,
                own_spec,
                near_spec,
                whole((2, 1, 2 * rows)),
                pl.BlockSpec(memory_space=pl.ANY),
                pl.BlockSpec(memory_space=pl.ANY),
            ],
            out_specs=[whole(out.shape), whole(out.shape)],
            scratch_shapes=[
                pltpu.VMEM((blocks + 1, rows, width), jnp.bfloat16),
                pltpu.VMEM((blocks + 1, width, rows), jnp.float32),
                pltpu.VMEM((blocks + 1, 8, rows), jnp.float32),
                pltpu.VMEM((blocks + 1, 8, rows), jnp.float32),
                pltpu.SemaphoreType.DMA((2,)),
            ],
        ),
        out_shape=[out, out],
        compiler_params=pltpu.CompilerParams(
            dimension_semantics=("arbitrary",), vmem_limit_bytes=56 * 2**20
        ),
        cost_estimate=pl.CostEstimate(
            flops=pages * heads * 256 * page_len * HEAD_DIM * 40,
            bytes_accessed=pages * page_len * width * 4,
            transcendentals=pages * heads * 256 * page_len,
        ),
        name="cache_attend",
    )(table, slots, q_slots, *q_parts, cache_keys, cache_values, near_keys, near_values, near_starts, *after)


def merged(refs, heads):
    levels = [read_levels(ref, heads) for ref in refs]
    top = functools.reduce(jnp.maximum, levels)
    weights = [jnp.exp2(level - top) for level in levels]
    total = functools.reduce(jnp.add, weights)
    factors = [w / total for w in weights]

    def block(h):
        cols = slice(h * HEAD_DIM, (h + 1) * HEAD_DIM)
        return functools.reduce(
            jnp.add, [ref[cols, :].astype(jnp.float32) * f[h : h + 1] for ref, f in zip(refs, factors)]
        )

    return block, top + jnp.log2(total)


def combine_kernel(*refs):
    *ins, _, keep_ref, send_ref = refs
    heads = (keep_ref.shape[1] - LEVEL_ROWS) // HEAD_DIM
    for g in range(len(ins) // 4):
        mine_low, mine_high, got_low, got_high = ins[4 * g : 4 * g + 4]
        for mine, got, out in ((mine_low, got_low, keep_ref), (mine_high, got_high, send_ref)):
            block, levels = merged([mine.at[0], got.at[0]], heads)
            write_block(out.at[g], block, jnp.ones_like(levels), levels, heads)


def combine(pairs, after):
    count, depth, rows = pairs[0][0].shape
    groups = len(pairs)
    half = count // 2
    low = pl.BlockSpec((1, depth, rows), lambda i: (i, 0, 0))
    high = pl.BlockSpec((1, depth, rows), lambda i: (i + half, 0, 0))
    into = pl.BlockSpec((groups, depth, rows), lambda i: (i, 0, 0))
    out = jax.ShapeDtypeStruct((half * groups, depth, rows), jnp.bfloat16)
    return pl.pallas_call(
        combine_kernel,
        grid=(half,),
        in_specs=[low, high, low, high] * groups + [pl.BlockSpec(memory_space=pl.ANY)],
        out_specs=[into, into],
        out_shape=[out, out],
        compiler_params=pltpu.CompilerParams(vmem_limit_bytes=24 * 2**20),
        cost_estimate=pl.CostEstimate(
            flops=groups * count * depth * rows * 4,
            bytes_accessed=groups * count * depth * rows * 6,
            transcendentals=0,
        ),
        name="combine_pairs",
    )(*[part for mine, got in pairs for part in (mine, mine, got, got)], after)


def last_kernel(mine_ref, got_ref, _, out_ref):
    groups, depth, _ = mine_ref.shape
    heads = (depth - LEVEL_ROWS) // HEAD_DIM
    for g in range(groups):
        block, _ = merged([mine_ref.at[g], got_ref.at[g]], heads)
        for h in range(heads):
            at = (g * heads + h) * HEAD_DIM
            out_ref[at : at + HEAD_DIM, :] = block(h).astype(jnp.bfloat16)


def combine_last(mine, got, after):
    groups, depth, rows = mine.shape
    whole = pl.BlockSpec(memory_space=pltpu.VMEM)
    return pl.pallas_call(
        last_kernel,
        in_specs=[whole, whole, pl.BlockSpec(memory_space=pl.ANY)],
        out_shape=jax.ShapeDtypeStruct((groups * (depth - LEVEL_ROWS), rows), jnp.bfloat16),
        compiler_params=pltpu.CompilerParams(vmem_limit_bytes=24 * 2**20),
        cost_estimate=pl.CostEstimate(
            flops=groups * depth * rows * 4, bytes_accessed=groups * depth * rows * 6, transcendentals=0
        ),
        name="combine_last",
    )(mine, got, after)


def local(
    hidden_in,
    queries,
    new_keys,
    new_values,
    query_gain,
    key_gain,
    cache_keys,
    cache_values,
    seg_ids,
    cache_pages,
    page_table,
    out_weight,
    out_bias,
    gate_mod,
):
    tok_dev, local_width = queries.shape
    size = lax.axis_size("req")
    tp_size = lax.axis_size("tp")
    model_width = local_width * tp_size
    line = size // PLANE
    device = lax.axis_index("req")
    spot = device % PLANE
    slot_count, page_len, _ = cache_keys.shape
    request_count = cache_pages.shape[0]
    total_pages = page_table.shape[0]
    first_row = device * tok_dev
    own_rows = first_row + jnp.arange(tok_dev, dtype=jnp.int32)
    own_segs = lax.dynamic_slice_in_dim(seg_ids, first_row, tok_dev, 0)
    req_ids = jnp.arange(request_count, dtype=jnp.int32)
    starts = jnp.sum((seg_ids[None, :] < req_ids[:, None]).astype(jnp.int32), axis=1)
    ends = jnp.sum((seg_ids[None, :] <= req_ids[:, None]).astype(jnp.int32), axis=1)
    own_pick = own_segs[:, None] == req_ids[None, :]
    own_start = jnp.sum(jnp.where(own_pick, starts[None, :], 0), axis=1)
    own_cache = jnp.sum(jnp.where(own_pick, cache_pages[None, :], 0), axis=1)
    positions = own_cache * page_len + own_rows - own_start

    wide_q = queries.astype(jnp.float32)
    wide_k = new_keys.astype(jnp.float32)
    sums = lax.psum(
        jnp.stack([jnp.sum(wide_q * wide_q, axis=1), jnp.sum(wide_k * wide_k, axis=1)], axis=1), "tp"
    )
    scales = lax.rsqrt(sums / model_width + EPSILON) * jnp.array([[SCORE_SCALE, 1.0]], jnp.float32)
    halfway = HEAD_DIM // 2
    frequency = 10000.0 ** (-jnp.arange(halfway, dtype=jnp.float32) / halfway)
    angles = positions.astype(jnp.float32)[:, None] * frequency[None, :]
    cosine = jnp.cos(angles)
    sine = jnp.sin(angles)
    cosine = jnp.concatenate([cosine, cosine], axis=1)
    sine = jnp.concatenate([-sine, sine], axis=1)

    physical = device * slot_count + jnp.arange(slot_count, dtype=jnp.int32)
    logical = jnp.sum(
        jnp.where(
            page_table[None, :] == physical[:, None],
            jnp.arange(total_pages, dtype=jnp.int32)[None, :],
            0,
        ),
        axis=1,
    )
    page_ends = jnp.cumsum(cache_pages)
    owners = jnp.sum((page_ends[None, :] <= logical[:, None]).astype(jnp.int32), axis=1)
    owner_pick = owners[:, None] == req_ids[None, :]
    owner_starts = jnp.sum(jnp.where(owner_pick, starts[None, :], 0), axis=1)
    owner_ends = jnp.sum(jnp.where(owner_pick, ends[None, :], 0), axis=1)
    owner_first = owner_starts // tok_dev
    owner_blocks = (owner_ends - 1) // tok_dev - owner_first + 1
    table = jnp.stack([owner_starts, owner_ends, owner_first, owner_blocks], axis=1).reshape(-1)

    near_blocks = device + jnp.arange(4, dtype=jnp.int32)
    near_rows = (near_blocks[:, None] * tok_dev + jnp.arange(tok_dev, dtype=jnp.int32)[None, :]).reshape(-1)
    padded_segs = jnp.concatenate([seg_ids, jnp.full((3 * tok_dev,), -1, jnp.int32)])
    near_segs = lax.dynamic_slice_in_dim(padded_segs, first_row, 4 * tok_dev, 0)
    near_starts = jnp.sum(
        jnp.where(near_segs[:, None] == req_ids[None, :], starts[None, :], 0), axis=1
    )
    near_starts = jnp.where(near_segs < 0, near_rows + size * tok_dev, near_starts)
    near_starts = near_starts.reshape(2, 1, 2 * tok_dev)

    apart = jnp.arange(size, dtype=jnp.int32) ^ device
    beyond = jnp.stack([jnp.int32(size), device])
    natural = jnp.concatenate([jnp.arange(size, dtype=jnp.int32), beyond])
    masks = [1 << i for i in range((size - 1).bit_length())]
    columns = out_weight.shape[1]
    blocks_each = line // tp_size
    tp_device = lax.axis_index("tp")

    groups = group_count(local_width)
    orders = [masks if group in (0, 3) else [2, 1] + masks[2:] for group in range(groups)]
    slots = []
    for order in orders:
        slot = sum(jnp.where((apart & m) > 0, size >> (i + 1), 0) for i, m in enumerate(order))
        slots.append(jnp.concatenate([slot, beyond]))
    gathered, near_keys, parts, stages = [None] * groups, [None] * groups, [None] * groups, []
    after = scales
    for group in [0, 2, 1, 3] if groups > 1 else [0]:
        parts[group], near_keys[group] = turn(
            group, queries, new_keys, scales, query_gain, key_gain, cosine, sine, after
        )
        after = near_keys[group]
        if group % 2 == 0:
            continue
        held = parts[group][None]
        for m in orders[group][:0:-1]:
            held = lax.optimization_barrier(jnp.concatenate([held, send_xor(held, m)], axis=0))
            stages.append(held)
            if held.shape[0] == line:
                after = held
        gathered[group] = held
    whole_blocks = lax.all_gather(
        jnp.concatenate(parts[::2], axis=1)[None], "req", axis=0, tiled=True
    )

    def gather_weights(after):
        weight, _ = lax.optimization_barrier((out_weight.T, after))
        lines = [[z * PLANE + p for z in range(line)] for p in range(PLANE)]
        weight = lax.all_gather(weight, "req", axis=0, tiled=True, axis_index_groups=lines)
        weight = weight.reshape(tp_size, blocks_each * columns, local_width)
        weights = []
        for k in range(tp_size):
            part = lax.dynamic_index_in_dim(weight, (tp_device + k) % tp_size, 0, keepdims=False)
            weights.append(part if k == 0 else send_tp(part, k))
        return weights

    last = len(masks) - 1
    if groups > 1:
        turns = ("a1", "a0", "c1", "a2", "c0", "a3", "c2", "c01", "c3", "c2", "c01", "c3", "c2", "l01")
        turns += ("c3", "l2", "l3")
    else:
        turns = ("a0",) + ("c0",) * last + ("l0",)
    state, stage, attended = {}, {}, []
    before = near_starts
    waits = [near_starts] * 4
    if groups > 1:
        waits[:2] = stages[-1], stages[-2]
    weights = None
    for turn_name in turns:
        step, names = turn_name[0], turn_name[1:]
        if step == "a":
            group = int(names)
            order = orders[group]
            if group % 2 == 0:
                q_parts = [whole_blocks]
            else:
                q_parts = [gathered[group], send_xor(gathered[group], order[0])]
            state[names] = attend(
                group, table, slots[group], natural if group % 2 == 0 else slots[group], q_parts,
                cache_keys, cache_values, near_keys[group], new_values, near_starts,
                (before, waits[group]),
            )
            stage[names] = 0
            before = state[names][0]
            if weights is None:
                weights = gather_weights(before)
            continue
        if names not in state:
            parts = list(names)
        else:
            parts = [names]
        pairs = []
        for part in parts:
            keep, send = state[part]
            pairs.append((keep, send_xor(send, orders[int(part[0])][stage[part]])))
        stage[names] = stage[parts[0]] + 1
        if step == "c":
            state[names] = combine(pairs, before)
            before = latest = state[names][0]
        else:
            if names == "2":
                before = weights[-1]
            before = combine_last(*pairs[0], before)
            attended.append((names, before))
    if groups > 1:
        attended[0] = (attended[0][0], lax.optimization_barrier((attended[0][1], latest))[0])

    projected = 0.0
    share = local_width // groups
    for some in [attended[:-1], attended[-1:]] if groups > 1 else [attended]:
        names = "".join(name for name, _ in some)
        some = joined([part for _, part in some], 0)
        got = [send_xor(some, k) for k in range(1, PLANE)]
        *got, _ = lax.optimization_barrier((*got, attended[-1][1]))
        spread = jnp.concatenate([some] + got, axis=1)
        spans = [(int(names[0]) * share, int(names[-1]) * share + share)]
        for k in range(tp_size):
            part = spread if k == 0 else send_tp(spread, k)
            at = 0
            for low, high in spans:
                projected = projected + jnp.dot(
                    weights[k][:, low:high],
                    part[at : at + high - low],
                    preferred_element_type=jnp.float32,
                )
                at += high - low
    sent = projected.astype(jnp.bfloat16)
    mine = [projected[:, :tok_dev]] + [
        send_xor(sent[:, k * tok_dev : (k + 1) * tok_dev], k).astype(jnp.float32) for k in range(1, PLANE)
    ]
    mine = [part.reshape(blocks_each, columns, tok_dev) for part in mine]
    swapped = [jnp.where((spot & 1) > 0, mine[i ^ 1], mine[i]) for i in range(PLANE)]
    swapped = [jnp.where((spot & 2) > 0, swapped[i ^ 2], swapped[i]) for i in range(PLANE)]
    projected = jnp.stack(swapped, axis=1).reshape(local_width, tok_dev).T

    gate_rows = jnp.dot(own_pick.astype(jnp.float32), gate_mod, precision=lax.Precision.HIGHEST)
    return (hidden_in.astype(jnp.float32) + gate_rows * (projected + out_bias[None, :])).astype(
        jnp.bfloat16
    )


def solution(mesh):
    return jax.shard_map(
        local,
        mesh=mesh,
        in_specs=(
            P("req", "tp"),
            P("req", "tp"),
            P("req", "tp"),
            P("req", "tp"),
            P("tp"),
            P("tp"),
            P("req", None, "tp"),
            P("req", None, "tp"),
            P(),
            P(),
            P(),
            P("tp", "req"),
            P("tp"),
            P(None, "tp"),
        ),
        out_specs=P("req", "tp"),
        check_vma=False,
    )
```

```python
import functools
import math

import jax
import jax.numpy as jnp
from jax import lax
from jax.experimental import pallas as pl
from jax.experimental.pallas import tpu as pltpu
from jax.sharding import PartitionSpec as P

HEAD_DIM = 128
EPSILON = 1e-06
LOW_SCORE = -1e30
PLANE = 4
PIECE = 16
LEVEL_ROWS = 32
SCORE_SCALE = math.log2(math.e) / math.sqrt(HEAD_DIM)


def send_xor(value, by):
    size = lax.axis_size("req")
    return lax.ppermute(value, "req", [(i, i ^ by) for i in range(size)])


def group_count(width):
    return 4 if width // HEAD_DIM % 4 == 0 else 1


def send_tp(value, by):
    size = lax.axis_size("tp")
    return lax.ppermute(value, "tp", [(i, (i + by) % size) for i in range(size)])


def turn_kernel(q_ref, k_ref, scale_ref, gain_q_ref, gain_k_ref, cos_ref, sin_ref, _, q_out, k_out):
    cosine = cos_ref[...]
    sine = sin_ref[...]
    sides = ((q_ref, gain_q_ref, q_out), (k_ref, gain_k_ref, k_out))
    for side, (ref, gain, out) in enumerate(sides):
        scale = scale_ref[:, side : side + 1]
        for col in range(0, ref.shape[1], HEAD_DIM):
            cols = slice(col, col + HEAD_DIM)
            x = ref[:, cols].astype(jnp.float32) * scale * gain[:, cols]
            y = x * cosine + pltpu.roll(x, HEAD_DIM // 2, 1) * sine
            out[:, cols] = y.astype(jnp.bfloat16)


def turn(group, queries, new_keys, scales, gain_q, gain_k, cosine, sine, after):
    rows, width = queries.shape
    width = width // group_count(width)
    part = jax.ShapeDtypeStruct((rows, width), jnp.bfloat16)
    part_spec = pl.BlockSpec((rows, width), lambda i: (0, group))
    gain_spec = pl.BlockSpec((1, width), lambda i: (0, group))
    whole = lambda shape: pl.BlockSpec(shape, lambda i: (0, 0))
    return pl.pallas_call(
        turn_kernel,
        grid=(1,),
        in_specs=[
            part_spec,
            part_spec,
            whole(scales.shape),
            gain_spec,
            gain_spec,
            whole(cosine.shape),
            whole(sine.shape),
            pl.BlockSpec(memory_space=pl.ANY),
        ],
        out_specs=[whole(part.shape), whole(part.shape)],
        out_shape=[part, part],
        compiler_params=pltpu.CompilerParams(vmem_limit_bytes=16 * 2**20),
        name="norm_turn",
    )(queries, new_keys, scales, gain_q[None], gain_k[None], cosine, sine, after)


def joined(parts, axis):
    return parts[0] if len(parts) == 1 else jnp.concatenate(parts, axis=axis)


def attend_kernel(
    q_column,
    table_ref,
    slot_ref,
    q_slot_ref,
    *refs,
):
    *q_refs, keys_ref, values_ref, near_keys_ref, near_values_ref, near_starts_ref, _, _ = refs[:-7]
    keep_ref, send_ref, q_all, acc, peak, total, sems = refs[-7:]
    step = pl.program_id(0)
    half, _, rows = keep_ref.shape
    width = acc.shape[1]
    blocks = 2 * half
    heads = width // HEAD_DIM
    lane = lax.broadcasted_iota(jnp.int32, (1, rows), 1)

    def update(slots, q_slots, keys_ref, values_ref, masks, allowed):
        ones = jnp.ones((PIECE, keys_ref.shape[0]), jnp.bfloat16)
        mask = joined(masks, 1)
        old_peak = joined([peak[s] for s in slots], 1)
        old_total = joined([total[s] for s in slots], 1)
        scores, weights, tops, fades = {}, {}, {}, {}

        def score(h):
            cols = slice(h * HEAD_DIM, (h + 1) * HEAD_DIM)
            q = joined([q_all[s, :, cols] for s in q_slots], 0)
            scores[h] = lax.dot_general(
                keys_ref[:, cols], q, (((1,), (1,)), ((), ())), preferred_element_type=jnp.float32
            )

        def weigh(h):
            found = scores.pop(h)
            if allowed is not None:
                found = jnp.where(allowed, found, LOW_SCORE)
            before = old_peak[h : h + 1]
            top = jnp.maximum(jnp.max(found, axis=0, keepdims=True), before)
            tops[h] = jnp.where(mask, top, before)
            fades[h] = jnp.where(mask, jnp.exp2(before - top), 1.0)
            weights[h] = jnp.exp2(found - jnp.where(mask, top, -LOW_SCORE)).astype(jnp.bfloat16)

        def blend(h):
            cols = slice(h * HEAD_DIM, (h + 1) * HEAD_DIM)
            values = jnp.concatenate([values_ref[:, cols].T, ones], axis=0)
            blended = jnp.dot(values, weights.pop(h), preferred_element_type=jnp.float32)
            fade = fades.pop(h)
            held = [acc[s, cols, :] for s in slots]
            sums = old_total[h : h + 1] * fade + blended[HEAD_DIM : HEAD_DIM + 1]
            for i, s in enumerate(slots):
                span = slice(i * rows, (i + 1) * rows)
                acc[s, cols, :] = held[i] * fade[:, span] + blended[:HEAD_DIM, span]
                peak[s, h : h + 1, :] = tops[h][:, span]
                total[s, h : h + 1, :] = sums[:, span]

        for h in range(heads + 2):
            if h < heads:
                score(h)
            if 1 <= h <= heads:
                weigh(h - 1)
            if h >= 2:
                blend(h - 2)

    @pl.when(step == 0)
    def _():
        share = blocks // len(q_refs)
        copies = [
            pltpu.make_async_copy(
                ref.at[:, :, pl.ds(q_column, width)], q_all.at[pl.ds(i * share, share)], sems.at[i]
            )
            for i, ref in enumerate(q_refs)
        ]
        for copy in copies:
            copy.start()
        q_all[blocks] = jnp.zeros((rows, width), jnp.bfloat16)
        acc[...] = jnp.zeros_like(acc)
        peak[...] = jnp.full(peak.shape, LOW_SCORE, jnp.float32)
        total[...] = jnp.zeros_like(total)
        for copy in copies:
            copy.wait()
        first = slot_ref[blocks + 1]

        def near_pair(j, carry):
            low = first + 2 * j
            row = low * rows + jnp.concatenate([lane, lane + rows], axis=1)
            begin = near_starts_ref[j]
            key = first * rows + lax.broadcasted_iota(jnp.int32, (rows, 2 * rows), 0)
            allowed = (key >= begin) & (key <= row)
            some = begin < (first + 1) * rows
            at = [jnp.minimum(low + i, blocks) for i in range(2)]
            slots, q_slots = [slot_ref[i] for i in at], [q_slot_ref[i] for i in at]
            masks = [some[:, :rows], some[:, rows:]]
            update(slots, q_slots, near_keys_ref, near_values_ref, masks, allowed)
            return carry

        lax.fori_loop(0, 2, near_pair, 0)

    @pl.when(step > 0)
    def _():
        begin = table_ref[4 * step - 4]
        end = table_ref[4 * step - 3]
        first = table_ref[4 * step - 2]
        count = table_ref[4 * step - 1]

        def visit(at):
            masks = [(b * rows + lane >= begin) & (b * rows + lane < end) for b in at]
            slots, q_slots = [slot_ref[b] for b in at], [q_slot_ref[b] for b in at]
            update(slots, q_slots, keys_ref.at[0], values_ref.at[0], masks, None)

        def pair(j, carry):
            visit([first + 2 * j, first + 2 * j + 1])
            return carry

        lax.fori_loop(0, count // 2, pair, 0)

        @pl.when(count % 2 == 1)
        def _():
            visit([first + count - 1])

    @pl.when(step == pl.num_programs(0) - 1)
    def _():
        for at, out in ((0, keep_ref), (half, send_ref)):

            def finish(i, carry, at=at, out=out):
                sums = jnp.maximum(total[at + i], 1.0)
                write_block(
                    out.at[i],
                    lambda h: acc[at + i, h * HEAD_DIM : (h + 1) * HEAD_DIM, :],
                    1.0 / sums,
                    peak[at + i] + jnp.log2(sums),
                    heads,
                )
                return carry

            lax.fori_loop(0, half, finish, 0)


def write_block(out, block, factors, levels, heads):
    for h in range(heads):
        out[h * HEAD_DIM : (h + 1) * HEAD_DIM, :] = (block(h) * factors[h : h + 1]).astype(jnp.bfloat16)
    first = levels.astype(jnp.bfloat16).astype(jnp.float32)
    second = (levels - first).astype(jnp.bfloat16).astype(jnp.float32)
    third = levels - first - second
    stacked = jnp.concatenate([first, second, third, jnp.zeros_like(levels)], axis=0)
    out[heads * HEAD_DIM :, :] = stacked.astype(jnp.bfloat16)


def read_levels(ref, heads):
    stacked = ref[heads * HEAD_DIM :, :].astype(jnp.float32)
    return stacked[:8] + (stacked[8:16] + stacked[16:24])


def attend(
    group, table, slots, q_slots, q_parts, cache_keys, cache_values, near_keys, near_values, near_starts, after
):
    rows, width = near_keys.shape
    half = sum(part.shape[0] for part in q_parts) // 2
    pages, page_len, _ = cache_keys.shape
    heads = width // HEAD_DIM
    blocks = 2 * half
    assert heads <= 8
    out = jax.ShapeDtypeStruct((half, width + LEVEL_ROWS, rows), jnp.bfloat16)
    page_spec = pl.BlockSpec((1, page_len, width), lambda i, *_: (jnp.maximum(i - 1, 0), 0, group))
    near_spec = pl.BlockSpec((rows, width), lambda i, *_: (0, group))
    own_spec = pl.BlockSpec((rows, width), lambda i, *_: (0, 0))
    whole = lambda shape: pl.BlockSpec(shape, lambda i, *_: (0,) * len(shape))
    q_column = group // 2 * width if len(q_parts) == 1 else 0
    return pl.pallas_call(
        functools.partial(attend_kernel, q_column),
        grid_spec=pltpu.PrefetchScalarGridSpec(
            num_scalar_prefetch=3,
            grid=(pages + 1,),
            in_specs=[pl.BlockSpec(memory_space=pl.ANY)] * len(q_parts)
            + [
                page_spec,
                page_spec,
                own_spec,
                near_spec,
                whole((2, 1, 2 * rows)),
                pl.BlockSpec(memory_space=pl.ANY),
                pl.BlockSpec(memory_space=pl.ANY),
            ],
            out_specs=[whole(out.shape), whole(out.shape)],
            scratch_shapes=[
                pltpu.VMEM((blocks + 1, rows, width), jnp.bfloat16),
                pltpu.VMEM((blocks + 1, width, rows), jnp.float32),
                pltpu.VMEM((blocks + 1, 8, rows), jnp.float32),
                pltpu.VMEM((blocks + 1, 8, rows), jnp.float32),
                pltpu.SemaphoreType.DMA((2,)),
            ],
        ),
        out_shape=[out, out],
        compiler_params=pltpu.CompilerParams(
            dimension_semantics=("arbitrary",), vmem_limit_bytes=56 * 2**20
        ),
        cost_estimate=pl.CostEstimate(
            flops=pages * heads * 256 * page_len * HEAD_DIM * 8,
            bytes_accessed=pages * page_len * width * 4,
            transcendentals=pages * heads * 256 * page_len,
        ),
        name="cache_attend",
    )(table, slots, q_slots, *q_parts, cache_keys, cache_values, near_keys, near_values, near_starts, *after)


def merged(refs, heads):
    levels = [read_levels(ref, heads) for ref in refs]
    top = functools.reduce(jnp.maximum, levels)
    weights = [jnp.exp2(level - top) for level in levels]
    total = functools.reduce(jnp.add, weights)
    factors = [w / total for w in weights]

    def block(h):
        cols = slice(h * HEAD_DIM, (h + 1) * HEAD_DIM)
        return functools.reduce(
            jnp.add, [ref[cols, :].astype(jnp.float32) * f[h : h + 1] for ref, f in zip(refs, factors)]
        )

    return block, top + jnp.log2(total)


def combine_kernel(*refs):
    *ins, _, keep_ref, send_ref = refs
    heads = (keep_ref.shape[1] - LEVEL_ROWS) // HEAD_DIM
    for g in range(len(ins) // 4):
        mine_low, mine_high, got_low, got_high = ins[4 * g : 4 * g + 4]
        for mine, got, out in ((mine_low, got_low, keep_ref), (mine_high, got_high, send_ref)):
            block, levels = merged([mine.at[0], got.at[0]], heads)
            write_block(out.at[g], block, jnp.ones_like(levels), levels, heads)


def combine(pairs, after):
    count, depth, rows = pairs[0][0].shape
    groups = len(pairs)
    half = count // 2
    low = pl.BlockSpec((1, depth, rows), lambda i: (i, 0, 0))
    high = pl.BlockSpec((1, depth, rows), lambda i: (i + half, 0, 0))
    into = pl.BlockSpec((groups, depth, rows), lambda i: (i, 0, 0))
    out = jax.ShapeDtypeStruct((half * groups, depth, rows), jnp.bfloat16)
    return pl.pallas_call(
        combine_kernel,
        grid=(half,),
        in_specs=[low, high, low, high] * groups + [pl.BlockSpec(memory_space=pl.ANY)],
        out_specs=[into, into],
        out_shape=[out, out],
        compiler_params=pltpu.CompilerParams(vmem_limit_bytes=24 * 2**20),
        cost_estimate=pl.CostEstimate(
            flops=groups * count * depth * rows * 4,
            bytes_accessed=groups * count * depth * rows * 6,
            transcendentals=0,
        ),
        name="combine_pairs",
    )(*[part for mine, got in pairs for part in (mine, mine, got, got)], after)


def last_kernel(mine_ref, got_ref, _, out_ref):
    groups, depth, _ = mine_ref.shape
    heads = (depth - LEVEL_ROWS) // HEAD_DIM
    for g in range(groups):
        block, _ = merged([mine_ref.at[g], got_ref.at[g]], heads)
        for h in range(heads):
            at = (g * heads + h) * HEAD_DIM
            out_ref[at : at + HEAD_DIM, :] = block(h).astype(jnp.bfloat16)


def combine_last(mine, got, after):
    groups, depth, rows = mine.shape
    whole = pl.BlockSpec(memory_space=pltpu.VMEM)
    return pl.pallas_call(
        last_kernel,
        in_specs=[whole, whole, pl.BlockSpec(memory_space=pl.ANY)],
        out_shape=jax.ShapeDtypeStruct((groups * (depth - LEVEL_ROWS), rows), jnp.bfloat16),
        compiler_params=pltpu.CompilerParams(vmem_limit_bytes=24 * 2**20),
        cost_estimate=pl.CostEstimate(
            flops=groups * depth * rows * 4, bytes_accessed=groups * depth * rows * 6, transcendentals=0
        ),
        name="combine_last",
    )(mine, got, after)


def local(
    hidden_in,
    queries,
    new_keys,
    new_values,
    query_gain,
    key_gain,
    cache_keys,
    cache_values,
    seg_ids,
    cache_pages,
    page_table,
    out_weight,
    out_bias,
    gate_mod,
):
    tok_dev, local_width = queries.shape
    size = lax.axis_size("req")
    tp_size = lax.axis_size("tp")
    model_width = local_width * tp_size
    line = size // PLANE
    device = lax.axis_index("req")
    spot = device % PLANE
    slot_count, page_len, _ = cache_keys.shape
    request_count = cache_pages.shape[0]
    total_pages = page_table.shape[0]
    first_row = device * tok_dev
    own_rows = first_row + jnp.arange(tok_dev, dtype=jnp.int32)
    own_segs = lax.dynamic_slice_in_dim(seg_ids, first_row, tok_dev, 0)
    req_ids = jnp.arange(request_count, dtype=jnp.int32)
    starts = jnp.sum((seg_ids[None, :] < req_ids[:, None]).astype(jnp.int32), axis=1)
    ends = jnp.sum((seg_ids[None, :] <= req_ids[:, None]).astype(jnp.int32), axis=1)
    own_pick = own_segs[:, None] == req_ids[None, :]
    own_start = jnp.sum(jnp.where(own_pick, starts[None, :], 0), axis=1)
    own_cache = jnp.sum(jnp.where(own_pick, cache_pages[None, :], 0), axis=1)
    positions = own_cache * page_len + own_rows - own_start

    wide_q = queries.astype(jnp.float32)
    wide_k = new_keys.astype(jnp.float32)
    sums = lax.psum(
        jnp.stack([jnp.sum(wide_q * wide_q, axis=1), jnp.sum(wide_k * wide_k, axis=1)], axis=1), "tp"
    )
    scales = lax.rsqrt(sums / model_width + EPSILON) * jnp.array([[SCORE_SCALE, 1.0]], jnp.float32)
    halfway = HEAD_DIM // 2
    frequency = 10000.0 ** (-jnp.arange(halfway, dtype=jnp.float32) / halfway)
    angles = positions.astype(jnp.float32)[:, None] * frequency[None, :]
    cosine = jnp.cos(angles)
    sine = jnp.sin(angles)
    cosine = jnp.concatenate([cosine, cosine], axis=1)
    sine = jnp.concatenate([-sine, sine], axis=1)

    physical = device * slot_count + jnp.arange(slot_count, dtype=jnp.int32)
    logical = jnp.sum(
        jnp.where(
            page_table[None, :] == physical[:, None],
            jnp.arange(total_pages, dtype=jnp.int32)[None, :],
            0,
        ),
        axis=1,
    )
    page_ends = jnp.cumsum(cache_pages)
    owners = jnp.sum((page_ends[None, :] <= logical[:, None]).astype(jnp.int32), axis=1)
    owner_pick = owners[:, None] == req_ids[None, :]
    owner_starts = jnp.sum(jnp.where(owner_pick, starts[None, :], 0), axis=1)
    owner_ends = jnp.sum(jnp.where(owner_pick, ends[None, :], 0), axis=1)
    owner_first = owner_starts // tok_dev
    owner_blocks = (owner_ends - 1) // tok_dev - owner_first + 1
    table = jnp.stack([owner_starts, owner_ends, owner_first, owner_blocks], axis=1).reshape(-1)

    near_blocks = device + jnp.arange(4, dtype=jnp.int32)
    near_rows = (near_blocks[:, None] * tok_dev + jnp.arange(tok_dev, dtype=jnp.int32)[None, :]).reshape(-1)
    padded_segs = jnp.concatenate([seg_ids, jnp.full((3 * tok_dev,), -1, jnp.int32)])
    near_segs = lax.dynamic_slice_in_dim(padded_segs, first_row, 4 * tok_dev, 0)
    near_starts = jnp.sum(
        jnp.where(near_segs[:, None] == req_ids[None, :], starts[None, :], 0), axis=1
    )
    near_starts = jnp.where(near_segs < 0, near_rows + size * tok_dev, near_starts)
    near_starts = near_starts.reshape(2, 1, 2 * tok_dev)

    apart = jnp.arange(size, dtype=jnp.int32) ^ device
    beyond = jnp.stack([jnp.int32(size), device])
    natural = jnp.concatenate([jnp.arange(size, dtype=jnp.int32), beyond])
    masks = [1 << i for i in range((size - 1).bit_length())]
    columns = out_weight.shape[1]
    blocks_each = line // tp_size
    tp_device = lax.axis_index("tp")

    groups = group_count(local_width)
    orders = [masks if group in (0, 3) else [2, 1] + masks[2:] for group in range(groups)]
    slots = []
    for order in orders:
        slot = sum(jnp.where((apart & m) > 0, size >> (i + 1), 0) for i, m in enumerate(order))
        slots.append(jnp.concatenate([slot, beyond]))
    gathered, near_keys, parts, stages = [None] * groups, [None] * groups, [None] * groups, []
    after = scales
    for group in [0, 2, 1, 3] if groups > 1 else [0]:
        parts[group], near_keys[group] = turn(
            group, queries, new_keys, scales, query_gain, key_gain, cosine, sine, after
        )
        after = near_keys[group]
        if group % 2 == 0:
            continue
        held = parts[group][None]
        for m in orders[group][:0:-1]:
            held = lax.optimization_barrier(jnp.concatenate([held, send_xor(held, m)], axis=0))
            stages.append(held)
            if held.shape[0] == line:
                after = held
        gathered[group] = held
    whole_blocks = lax.all_gather(
        jnp.concatenate(parts[::2], axis=1)[None], "req", axis=0, tiled=True
    )

    def gather_weights(after):
        weight, _ = lax.optimization_barrier((out_weight.T, after))
        lines = [[z * PLANE + p for z in range(line)] for p in range(PLANE)]
        weight = lax.all_gather(weight, "req", axis=0, tiled=True, axis_index_groups=lines)
        return weight.reshape(tp_size, blocks_each * columns, local_width)

    def swap_weights(weight, after):
        weight, _ = lax.optimization_barrier((weight, after))
        weights = []
        for k in range(tp_size):
            part = lax.dynamic_index_in_dim(weight, (tp_device + k) % tp_size, 0, keepdims=False)
            weights.append(part if k == 0 else send_tp(part, k))
        return weights

    last = len(masks) - 1
    if groups > 1:
        turns = ("a1", "a0", "c1", "a2", "c1", "c0", "a3", "c2", "c1", "c0", "c3", "c2", "l1", "c0", "c3")
        turns += ("c2", "l0", "c3", "l2", "l3")
    else:
        turns = ("a0",) + ("c0",) * last + ("l0",)
    state, stage, attended = {}, {}, []
    before = near_starts
    waits = [near_starts] * 4
    if groups > 1:
        waits[1] = stages[-2]
    weight, weights = None, None
    for turn_name in turns:
        step, names = turn_name[0], turn_name[1:]
        if step == "a":
            group = int(names)
            order = orders[group]
            if group % 2 == 0:
                q_parts = [whole_blocks]
            else:
                q_parts = [gathered[group], send_xor(gathered[group], order[0])]
            state[names] = attend(
                group, table, slots[group], natural if group % 2 == 0 else slots[group], q_parts,
                cache_keys, cache_values, near_keys[group], new_values, near_starts,
                (before, waits[group]),
            )
            stage[names] = 0
            before = state[names][0]
            if weight is None:
                weight = gather_weights(before)
            continue
        if names not in state:
            parts = list(names)
        else:
            parts = [names]
        pairs = []
        for part in parts:
            keep, send = state[part]
            pairs.append((keep, send_xor(send, orders[int(part[0])][stage[part]])))
        stage[names] = stage[parts[0]] + 1
        if step == "c":
            state[names] = combine(pairs, before)
            before = latest = state[names][0]
            if weights is None and names in ("3", str(groups - 1)):
                weights = swap_weights(weight, before)
        else:
            before = combine_last(*pairs[0], before)
            attended.append((names, before))
    if groups > 1:
        attended[:2] = attended[1::-1]
        attended[0] = (attended[0][0], lax.optimization_barrier((attended[0][1], latest))[0])

    projected = 0.0
    share = local_width // groups
    for some in [attended[:-1], attended[-1:]] if groups > 1 else [attended]:
        names = "".join(name for name, _ in some)
        some = joined([part for _, part in some], 0)
        got = [send_xor(some, k) for k in range(1, PLANE)]
        *got, _ = lax.optimization_barrier((*got, attended[-1][1]))
        spread = jnp.concatenate([some] + got, axis=1)
        spans = [(int(names[0]) * share, int(names[-1]) * share + share)]
        for k in range(tp_size):
            part = spread if k == 0 else send_tp(spread, k)
            at = 0
            for low, high in spans:
                projected = projected + jnp.dot(
                    weights[k][:, low:high],
                    part[at : at + high - low],
                    preferred_element_type=jnp.float32,
                )
                at += high - low
    sent = projected.astype(jnp.bfloat16)
    mine = [projected[:, :tok_dev]] + [
        send_xor(sent[:, k * tok_dev : (k + 1) * tok_dev], k).astype(jnp.float32) for k in range(1, PLANE)
    ]
    mine = [part.reshape(blocks_each, columns, tok_dev) for part in mine]
    swapped = [jnp.where((spot & 1) > 0, mine[i ^ 1], mine[i]) for i in range(PLANE)]
    swapped = [jnp.where((spot & 2) > 0, swapped[i ^ 2], swapped[i]) for i in range(PLANE)]
    projected = jnp.stack(swapped, axis=1).reshape(local_width, tok_dev).T

    gate_rows = jnp.dot(own_pick.astype(jnp.float32), gate_mod, precision=lax.Precision.HIGHEST)
    return (hidden_in.astype(jnp.float32) + gate_rows * (projected + out_bias[None, :])).astype(
        jnp.bfloat16
    )


def solution(mesh):
    return jax.shard_map(
        local,
        mesh=mesh,
        in_specs=(
            P("req", "tp"),
            P("req", "tp"),
            P("req", "tp"),
            P("req", "tp"),
            P("tp"),
            P("tp"),
            P("req", None, "tp"),
            P("req", None, "tp"),
            P(),
            P(),
            P(),
            P("tp", "req"),
            P("tp"),
            P(None, "tp"),
        ),
        out_specs=P("req", "tp"),
        check_vma=False,
    )
```

```python
import functools
import math

import jax
import jax.numpy as jnp
from jax import lax
from jax.experimental import pallas as pl
from jax.experimental.pallas import tpu as pltpu
from jax.sharding import PartitionSpec as P

HEAD_DIM = 128
EPSILON = 1e-06
LOW_SCORE = -1e30
PLANE = 4
PIECE = 16
LEVEL_ROWS = 32
SCORE_SCALE = math.log2(math.e) / math.sqrt(HEAD_DIM)


def send_xor(value, by):
    size = lax.axis_size("req")
    return lax.ppermute(value, "req", [(i, i ^ by) for i in range(size)])


def group_count(width):
    return 4 if width // HEAD_DIM % 4 == 0 else 1


def send_tp(value, by):
    size = lax.axis_size("tp")
    return lax.ppermute(value, "tp", [(i, (i + by) % size) for i in range(size)])


def turn_kernel(q_ref, k_ref, scale_ref, gain_q_ref, gain_k_ref, cos_ref, sin_ref, _, q_out, k_out):
    cosine = cos_ref[...]
    sine = sin_ref[...]
    sides = ((q_ref, gain_q_ref, q_out), (k_ref, gain_k_ref, k_out))
    for side, (ref, gain, out) in enumerate(sides):
        scale = scale_ref[:, side : side + 1]
        for col in range(0, ref.shape[1], HEAD_DIM):
            cols = slice(col, col + HEAD_DIM)
            x = ref[:, cols].astype(jnp.float32) * scale * gain[:, cols]
            y = x * cosine + pltpu.roll(x, HEAD_DIM // 2, 1) * sine
            out[:, cols] = y.astype(jnp.bfloat16)


def turn(group, queries, new_keys, scales, gain_q, gain_k, cosine, sine, after):
    rows, width = queries.shape
    width = width // group_count(width)
    part = jax.ShapeDtypeStruct((rows, width), jnp.bfloat16)
    part_spec = pl.BlockSpec((rows, width), lambda i: (0, group))
    gain_spec = pl.BlockSpec((1, width), lambda i: (0, group))
    whole = lambda shape: pl.BlockSpec(shape, lambda i: (0, 0))
    return pl.pallas_call(
        turn_kernel,
        grid=(1,),
        in_specs=[
            part_spec,
            part_spec,
            whole(scales.shape),
            gain_spec,
            gain_spec,
            whole(cosine.shape),
            whole(sine.shape),
            pl.BlockSpec(memory_space=pl.ANY),
        ],
        out_specs=[whole(part.shape), whole(part.shape)],
        out_shape=[part, part],
        compiler_params=pltpu.CompilerParams(vmem_limit_bytes=16 * 2**20),
        name="norm_turn",
    )(queries, new_keys, scales, gain_q[None], gain_k[None], cosine, sine, after)


def joined(parts, axis):
    return parts[0] if len(parts) == 1 else jnp.concatenate(parts, axis=axis)


def attend_kernel(
    q_column,
    table_ref,
    slot_ref,
    q_slot_ref,
    *refs,
):
    *q_refs, keys_ref, values_ref, near_keys_ref, near_values_ref, near_starts_ref, _, _ = refs[:-7]
    keep_ref, send_ref, q_all, acc, peak, total, sems = refs[-7:]
    step = pl.program_id(0)
    half, _, rows = keep_ref.shape
    width = acc.shape[1]
    blocks = 2 * half
    heads = width // HEAD_DIM
    lane = lax.broadcasted_iota(jnp.int32, (1, rows), 1)

    def update(slots, q_slots, keys_ref, values_ref, masks, allowed):
        ones = jnp.ones((PIECE, keys_ref.shape[0]), jnp.bfloat16)
        mask = joined(masks, 1)
        old_peak = joined([peak[s] for s in slots], 1)
        old_total = joined([total[s] for s in slots], 1)
        scores, weights, tops, fades = {}, {}, {}, {}

        def score(h):
            cols = slice(h * HEAD_DIM, (h + 1) * HEAD_DIM)
            q = joined([q_all[s, :, cols] for s in q_slots], 0)
            scores[h] = lax.dot_general(
                keys_ref[:, cols], q, (((1,), (1,)), ((), ())), preferred_element_type=jnp.float32
            )

        def weigh(h):
            found = scores.pop(h)
            if allowed is not None:
                found = jnp.where(allowed, found, LOW_SCORE)
            before = old_peak[h : h + 1]
            top = jnp.maximum(jnp.max(found, axis=0, keepdims=True), before)
            tops[h] = jnp.where(mask, top, before)
            fades[h] = jnp.where(mask, jnp.exp2(before - top), 1.0)
            weights[h] = jnp.exp2(found - jnp.where(mask, top, -LOW_SCORE)).astype(jnp.bfloat16)

        def blend(h):
            cols = slice(h * HEAD_DIM, (h + 1) * HEAD_DIM)
            values = jnp.concatenate([values_ref[:, cols].T, ones], axis=0)
            blended = jnp.dot(values, weights.pop(h), preferred_element_type=jnp.float32)
            fade = fades.pop(h)
            held = [acc[s, cols, :] for s in slots]
            sums = old_total[h : h + 1] * fade + blended[HEAD_DIM : HEAD_DIM + 1]
            for i, s in enumerate(slots):
                span = slice(i * rows, (i + 1) * rows)
                acc[s, cols, :] = held[i] * fade[:, span] + blended[:HEAD_DIM, span]
                peak[s, h : h + 1, :] = tops[h][:, span]
                total[s, h : h + 1, :] = sums[:, span]

        for h in range(heads + 2):
            if h < heads:
                score(h)
            if 1 <= h <= heads:
                weigh(h - 1)
            if h >= 2:
                blend(h - 2)

    @pl.when(step == 0)
    def _():
        share = blocks // len(q_refs)
        copies = [
            pltpu.make_async_copy(
                ref.at[:, :, pl.ds(q_column, width)], q_all.at[pl.ds(i * share, share)], sems.at[i]
            )
            for i, ref in enumerate(q_refs)
        ]
        for copy in copies:
            copy.start()
        q_all[blocks] = jnp.zeros((rows, width), jnp.bfloat16)
        acc[...] = jnp.zeros_like(acc)
        peak[...] = jnp.full(peak.shape, LOW_SCORE, jnp.float32)
        total[...] = jnp.zeros_like(total)
        for copy in copies:
            copy.wait()
        first = slot_ref[blocks + 1]

        def near_pair(j, carry):
            low = first + 2 * j
            row = low * rows + jnp.concatenate([lane, lane + rows], axis=1)
            begin = near_starts_ref[j]
            key = first * rows + lax.broadcasted_iota(jnp.int32, (rows, 2 * rows), 0)
            allowed = (key >= begin) & (key <= row)
            some = begin < (first + 1) * rows
            at = [jnp.minimum(low + i, blocks) for i in range(2)]
            slots, q_slots = [slot_ref[i] for i in at], [q_slot_ref[i] for i in at]
            masks = [some[:, :rows], some[:, rows:]]
            update(slots, q_slots, near_keys_ref, near_values_ref, masks, allowed)
            return carry

        lax.fori_loop(0, 2, near_pair, 0)

    @pl.when(step > 0)
    def _():
        begin = table_ref[4 * step - 4]
        end = table_ref[4 * step - 3]
        first = table_ref[4 * step - 2]
        count = table_ref[4 * step - 1]

        def visit(at):
            masks = [(b * rows + lane >= begin) & (b * rows + lane < end) for b in at]
            slots, q_slots = [slot_ref[b] for b in at], [q_slot_ref[b] for b in at]
            update(slots, q_slots, keys_ref.at[0], values_ref.at[0], masks, None)

        def pair(j, carry):
            visit([first + 2 * j, first + 2 * j + 1])
            return carry

        lax.fori_loop(0, count // 2, pair, 0)

        @pl.when(count % 2 == 1)
        def _():
            visit([first + count - 1])

    @pl.when(step == pl.num_programs(0) - 1)
    def _():
        for at, out in ((0, keep_ref), (half, send_ref)):

            def finish(i, carry, at=at, out=out):
                sums = jnp.maximum(total[at + i], 1.0)
                write_block(
                    out.at[i],
                    lambda h: acc[at + i, h * HEAD_DIM : (h + 1) * HEAD_DIM, :],
                    1.0 / sums,
                    peak[at + i] + jnp.log2(sums),
                    heads,
                )
                return carry

            lax.fori_loop(0, half, finish, 0)


def write_block(out, block, factors, levels, heads):
    for h in range(heads):
        out[h * HEAD_DIM : (h + 1) * HEAD_DIM, :] = (block(h) * factors[h : h + 1]).astype(jnp.bfloat16)
    first = levels.astype(jnp.bfloat16).astype(jnp.float32)
    second = (levels - first).astype(jnp.bfloat16).astype(jnp.float32)
    third = levels - first - second
    stacked = jnp.concatenate([first, second, third, jnp.zeros_like(levels)], axis=0)
    out[heads * HEAD_DIM :, :] = stacked.astype(jnp.bfloat16)


def read_levels(ref, heads):
    stacked = ref[heads * HEAD_DIM :, :].astype(jnp.float32)
    return stacked[:8] + (stacked[8:16] + stacked[16:24])


def attend(
    group, table, slots, q_slots, q_parts, cache_keys, cache_values, near_keys, near_values, near_starts, after
):
    rows, width = near_keys.shape
    half = sum(part.shape[0] for part in q_parts) // 2
    pages, page_len, _ = cache_keys.shape
    heads = width // HEAD_DIM
    blocks = 2 * half
    assert heads <= 8
    out = jax.ShapeDtypeStruct((half, width + LEVEL_ROWS, rows), jnp.bfloat16)
    page_spec = pl.BlockSpec((1, page_len, width), lambda i, *_: (jnp.maximum(i - 1, 0), 0, group))
    near_spec = pl.BlockSpec((rows, width), lambda i, *_: (0, group))
    own_spec = pl.BlockSpec((rows, width), lambda i, *_: (0, 0))
    whole = lambda shape: pl.BlockSpec(shape, lambda i, *_: (0,) * len(shape))
    q_column = group // 2 * width if len(q_parts) == 1 else 0
    return pl.pallas_call(
        functools.partial(attend_kernel, q_column),
        grid_spec=pltpu.PrefetchScalarGridSpec(
            num_scalar_prefetch=3,
            grid=(pages + 1,),
            in_specs=[pl.BlockSpec(memory_space=pl.ANY)] * len(q_parts)
            + [
                page_spec,
                page_spec,
                own_spec,
                near_spec,
                whole((2, 1, 2 * rows)),
                pl.BlockSpec(memory_space=pl.ANY),
                pl.BlockSpec(memory_space=pl.ANY),
            ],
            out_specs=[whole(out.shape), whole(out.shape)],
            scratch_shapes=[
                pltpu.VMEM((blocks + 1, rows, width), jnp.bfloat16),
                pltpu.VMEM((blocks + 1, width, rows), jnp.float32),
                pltpu.VMEM((blocks + 1, 8, rows), jnp.float32),
                pltpu.VMEM((blocks + 1, 8, rows), jnp.float32),
                pltpu.SemaphoreType.DMA((2,)),
            ],
        ),
        out_shape=[out, out],
        compiler_params=pltpu.CompilerParams(
            dimension_semantics=("arbitrary",), vmem_limit_bytes=56 * 2**20
        ),
        cost_estimate=pl.CostEstimate(
            flops=pages * heads * 256 * page_len * HEAD_DIM * 8,
            bytes_accessed=pages * page_len * width * 4,
            transcendentals=pages * heads * 256 * page_len,
        ),
        name="cache_attend",
    )(table, slots, q_slots, *q_parts, cache_keys, cache_values, near_keys, near_values, near_starts, *after)


def merged(refs, heads):
    levels = [read_levels(ref, heads) for ref in refs]
    top = functools.reduce(jnp.maximum, levels)
    weights = [jnp.exp2(level - top) for level in levels]
    total = functools.reduce(jnp.add, weights)
    factors = [w / total for w in weights]

    def block(h):
        cols = slice(h * HEAD_DIM, (h + 1) * HEAD_DIM)
        return functools.reduce(
            jnp.add, [ref[cols, :].astype(jnp.float32) * f[h : h + 1] for ref, f in zip(refs, factors)]
        )

    return block, top + jnp.log2(total)


def combine_kernel(*refs):
    *ins, _, keep_ref, send_ref = refs
    heads = (keep_ref.shape[1] - LEVEL_ROWS) // HEAD_DIM
    for g in range(len(ins) // 4):
        mine_low, mine_high, got_low, got_high = ins[4 * g : 4 * g + 4]
        for mine, got, out in ((mine_low, got_low, keep_ref), (mine_high, got_high, send_ref)):
            block, levels = merged([mine.at[0], got.at[0]], heads)
            write_block(out.at[g], block, jnp.ones_like(levels), levels, heads)


def combine(pairs, after):
    count, depth, rows = pairs[0][0].shape
    groups = len(pairs)
    half = count // 2
    low = pl.BlockSpec((1, depth, rows), lambda i: (i, 0, 0))
    high = pl.BlockSpec((1, depth, rows), lambda i: (i + half, 0, 0))
    into = pl.BlockSpec((groups, depth, rows), lambda i: (i, 0, 0))
    out = jax.ShapeDtypeStruct((half * groups, depth, rows), jnp.bfloat16)
    return pl.pallas_call(
        combine_kernel,
        grid=(half,),
        in_specs=[low, high, low, high] * groups + [pl.BlockSpec(memory_space=pl.ANY)],
        out_specs=[into, into],
        out_shape=[out, out],
        compiler_params=pltpu.CompilerParams(vmem_limit_bytes=24 * 2**20),
        cost_estimate=pl.CostEstimate(
            flops=groups * count * depth * rows * 4,
            bytes_accessed=groups * count * depth * rows * 6,
            transcendentals=0,
        ),
        name="combine_pairs",
    )(*[part for mine, got in pairs for part in (mine, mine, got, got)], after)


def last_kernel(mine_ref, got_ref, _, out_ref):
    groups, depth, _ = mine_ref.shape
    heads = (depth - LEVEL_ROWS) // HEAD_DIM
    for g in range(groups):
        block, _ = merged([mine_ref.at[g], got_ref.at[g]], heads)
        for h in range(heads):
            at = (g * heads + h) * HEAD_DIM
            out_ref[at : at + HEAD_DIM, :] = block(h).astype(jnp.bfloat16)


def combine_last(mine, got, after):
    groups, depth, rows = mine.shape
    whole = pl.BlockSpec(memory_space=pltpu.VMEM)
    return pl.pallas_call(
        last_kernel,
        in_specs=[whole, whole, pl.BlockSpec(memory_space=pl.ANY)],
        out_shape=jax.ShapeDtypeStruct((groups * (depth - LEVEL_ROWS), rows), jnp.bfloat16),
        compiler_params=pltpu.CompilerParams(vmem_limit_bytes=24 * 2**20),
        cost_estimate=pl.CostEstimate(
            flops=groups * depth * rows * 4, bytes_accessed=groups * depth * rows * 6, transcendentals=0
        ),
        name="combine_last",
    )(mine, got, after)


def local(
    hidden_in,
    queries,
    new_keys,
    new_values,
    query_gain,
    key_gain,
    cache_keys,
    cache_values,
    seg_ids,
    cache_pages,
    page_table,
    out_weight,
    out_bias,
    gate_mod,
):
    tok_dev, local_width = queries.shape
    size = lax.axis_size("req")
    tp_size = lax.axis_size("tp")
    model_width = local_width * tp_size
    line = size // PLANE
    device = lax.axis_index("req")
    spot = device % PLANE
    slot_count, page_len, _ = cache_keys.shape
    request_count = cache_pages.shape[0]
    total_pages = page_table.shape[0]
    first_row = device * tok_dev
    own_rows = first_row + jnp.arange(tok_dev, dtype=jnp.int32)
    own_segs = lax.dynamic_slice_in_dim(seg_ids, first_row, tok_dev, 0)
    req_ids = jnp.arange(request_count, dtype=jnp.int32)
    starts = jnp.sum((seg_ids[None, :] < req_ids[:, None]).astype(jnp.int32), axis=1)
    ends = jnp.sum((seg_ids[None, :] <= req_ids[:, None]).astype(jnp.int32), axis=1)
    own_pick = own_segs[:, None] == req_ids[None, :]
    own_start = jnp.sum(jnp.where(own_pick, starts[None, :], 0), axis=1)
    own_cache = jnp.sum(jnp.where(own_pick, cache_pages[None, :], 0), axis=1)
    positions = own_cache * page_len + own_rows - own_start

    wide_q = queries.astype(jnp.float32)
    wide_k = new_keys.astype(jnp.float32)
    sums = lax.psum(
        jnp.stack([jnp.sum(wide_q * wide_q, axis=1), jnp.sum(wide_k * wide_k, axis=1)], axis=1), "tp"
    )
    scales = lax.rsqrt(sums / model_width + EPSILON) * jnp.array([[SCORE_SCALE, 1.0]], jnp.float32)
    halfway = HEAD_DIM // 2
    frequency = 10000.0 ** (-jnp.arange(halfway, dtype=jnp.float32) / halfway)
    angles = positions.astype(jnp.float32)[:, None] * frequency[None, :]
    cosine = jnp.cos(angles)
    sine = jnp.sin(angles)
    cosine = jnp.concatenate([cosine, cosine], axis=1)
    sine = jnp.concatenate([-sine, sine], axis=1)

    physical = device * slot_count + jnp.arange(slot_count, dtype=jnp.int32)
    logical = jnp.sum(
        jnp.where(
            page_table[None, :] == physical[:, None],
            jnp.arange(total_pages, dtype=jnp.int32)[None, :],
            0,
        ),
        axis=1,
    )
    page_ends = jnp.cumsum(cache_pages)
    owners = jnp.sum((page_ends[None, :] <= logical[:, None]).astype(jnp.int32), axis=1)
    owner_pick = owners[:, None] == req_ids[None, :]
    owner_starts = jnp.sum(jnp.where(owner_pick, starts[None, :], 0), axis=1)
    owner_ends = jnp.sum(jnp.where(owner_pick, ends[None, :], 0), axis=1)
    owner_first = owner_starts // tok_dev
    owner_blocks = (owner_ends - 1) // tok_dev - owner_first + 1
    table = jnp.stack([owner_starts, owner_ends, owner_first, owner_blocks], axis=1).reshape(-1)

    near_blocks = device + jnp.arange(4, dtype=jnp.int32)
    near_rows = (near_blocks[:, None] * tok_dev + jnp.arange(tok_dev, dtype=jnp.int32)[None, :]).reshape(-1)
    padded_segs = jnp.concatenate([seg_ids, jnp.full((3 * tok_dev,), -1, jnp.int32)])
    near_segs = lax.dynamic_slice_in_dim(padded_segs, first_row, 4 * tok_dev, 0)
    near_starts = jnp.sum(
        jnp.where(near_segs[:, None] == req_ids[None, :], starts[None, :], 0), axis=1
    )
    near_starts = jnp.where(near_segs < 0, near_rows + size * tok_dev, near_starts)
    near_starts = near_starts.reshape(2, 1, 2 * tok_dev)

    apart = jnp.arange(size, dtype=jnp.int32) ^ device
    beyond = jnp.stack([jnp.int32(size), device])
    natural = jnp.concatenate([jnp.arange(size, dtype=jnp.int32), beyond])
    masks = [1 << i for i in range((size - 1).bit_length())]
    columns = out_weight.shape[1]
    blocks_each = line // tp_size
    tp_device = lax.axis_index("tp")

    groups = group_count(local_width)
    gather_order = [2, 1] + masks[2:]
    slots, gather_slots = [
        jnp.concatenate(
            [sum(jnp.where((apart & m) > 0, size >> (i + 1), 0) for i, m in enumerate(order)), beyond]
        )
        for order in (masks, gather_order)
    ]
    gathered, near_keys, parts, stages = [None] * groups, [None] * groups, [None] * groups, []
    after = scales
    for group in [0, 2, 1, 3] if groups > 1 else [0]:
        parts[group], near_keys[group] = turn(
            group, queries, new_keys, scales, query_gain, key_gain, cosine, sine, after
        )
        after = near_keys[group]
        if group % 2 == 0:
            continue
        held = parts[group][None]
        for m in gather_order[:0:-1]:
            held = lax.optimization_barrier(jnp.concatenate([held, send_xor(held, m)], axis=0))
            stages.append(held)
            if held.shape[0] == line:
                after = held
        gathered[group] = held
    whole_blocks = lax.all_gather(
        jnp.concatenate(parts[::2], axis=1)[None], "req", axis=0, tiled=True
    )

    def gather_weights(after):
        weight, _ = lax.optimization_barrier((out_weight.T, after))
        lines = [[z * PLANE + p for z in range(line)] for p in range(PLANE)]
        weight = lax.all_gather(weight, "req", axis=0, tiled=True, axis_index_groups=lines)
        return weight.reshape(tp_size, blocks_each * columns, local_width)

    def swap_weights(weight, after):
        weight, _ = lax.optimization_barrier((weight, after))
        weights = []
        for k in range(tp_size):
            part = lax.dynamic_index_in_dim(weight, (tp_device + k) % tp_size, 0, keepdims=False)
            weights.append(part if k == 0 else send_tp(part, k))
        return weights

    last = len(masks) - 1
    if groups > 1:
        turns = ("a1", "a0", "c1", "a2", "c0", "c1", "a3", "c2", "c0", "c1", "c0", "c2", "l1", "c3", "l0")
        turns += ("c2", "c3", "l2", "c3", "l3")
    else:
        turns = ("a0",) + ("c0",) * last + ("l0",)
    state, stage, attended = {}, {}, []
    before = near_starts
    waits = [near_starts] * 4
    if groups > 1:
        waits[1] = stages[-2]
    weight, weights = None, None
    for turn_name in turns:
        step, names = turn_name[0], turn_name[1:]
        if step == "a":
            group = int(names)
            if group % 2 == 0:
                q_parts = [whole_blocks]
            else:
                q_parts = [gathered[group], send_xor(gathered[group], gather_order[0])]
            state[names] = attend(
                group, table, slots, natural if group % 2 == 0 else gather_slots, q_parts,
                cache_keys, cache_values, near_keys[group], new_values, near_starts,
                (before, waits[group]),
            )
            stage[names] = 0
            before = state[names][0]
            if weight is None:
                weight = gather_weights(before)
            continue
        if names not in state:
            parts = list(names)
        else:
            parts = [names]
        pairs = []
        for part in parts:
            keep, send = state[part]
            pairs.append((keep, send_xor(send, masks[stage[part]])))
        stage[names] = stage[parts[0]] + 1
        if step == "c":
            state[names] = combine(pairs, before)
            before = state[names][0]
            if stage[names] == last - 1:
                latest = before
            if weights is None and names in ("3", str(groups - 1)):
                weights = swap_weights(weight, before)
        else:
            before = combine_last(*pairs[0], before)
            attended.append((names, before))
    if groups > 1:
        attended[:2] = attended[1::-1]
        attended[0] = (attended[0][0], lax.optimization_barrier((attended[0][1], latest))[0])

    projected = 0.0
    share = local_width // groups
    for some in [attended[:-1], attended[-1:]] if groups > 1 else [attended]:
        names = "".join(name for name, _ in some)
        some = joined([part for _, part in some], 0)
        got = [send_xor(some, k) for k in range(1, PLANE)]
        *got, _ = lax.optimization_barrier((*got, attended[-1][1]))
        spread = jnp.concatenate([some] + got, axis=1)
        spans = [(int(names[0]) * share, int(names[-1]) * share + share)]
        for k in range(tp_size):
            part = spread if k == 0 else send_tp(spread, k)
            at = 0
            for low, high in spans:
                projected = projected + jnp.dot(
                    weights[k][:, low:high],
                    part[at : at + high - low],
                    preferred_element_type=jnp.float32,
                )
                at += high - low
    sent = projected.astype(jnp.bfloat16)
    mine = [projected[:, :tok_dev]] + [
        send_xor(sent[:, k * tok_dev : (k + 1) * tok_dev], k).astype(jnp.float32) for k in range(1, PLANE)
    ]
    mine = [part.reshape(blocks_each, columns, tok_dev) for part in mine]
    swapped = [jnp.where((spot & 1) > 0, mine[i ^ 1], mine[i]) for i in range(PLANE)]
    swapped = [jnp.where((spot & 2) > 0, swapped[i ^ 2], swapped[i]) for i in range(PLANE)]
    projected = jnp.stack(swapped, axis=1).reshape(local_width, tok_dev).T

    gate_rows = jnp.dot(own_pick.astype(jnp.float32), gate_mod, precision=lax.Precision.HIGHEST)
    return (hidden_in.astype(jnp.float32) + gate_rows * (projected + out_bias[None, :])).astype(
        jnp.bfloat16
    )


def solution(mesh):
    return jax.shard_map(
        local,
        mesh=mesh,
        in_specs=(
            P("req", "tp"),
            P("req", "tp"),
            P("req", "tp"),
            P("req", "tp"),
            P("tp"),
            P("tp"),
            P("req", None, "tp"),
            P("req", None, "tp"),
            P(),
            P(),
            P(),
            P("tp", "req"),
            P("tp"),
            P(None, "tp"),
        ),
        out_specs=P("req", "tp"),
        check_vma=False,
    )
```

```python
import functools
import math

import jax
import jax.numpy as jnp
from jax import lax
from jax.experimental import pallas as pl
from jax.experimental.pallas import tpu as pltpu
from jax.sharding import PartitionSpec as P

HEAD_DIM = 128
EPSILON = 1e-06
LOW_SCORE = -1e30
PLANE = 4
PIECE = 16
LEVEL_ROWS = 32
SCORE_SCALE = math.log2(math.e) / math.sqrt(HEAD_DIM)


def send_xor(value, by):
    size = lax.axis_size("req")
    return lax.ppermute(value, "req", [(i, i ^ by) for i in range(size)])


def group_count(width):
    return 4 if width // HEAD_DIM % 4 == 0 else 1


def send_tp(value, by):
    size = lax.axis_size("tp")
    return lax.ppermute(value, "tp", [(i, (i + by) % size) for i in range(size)])


def turn_kernel(q_ref, k_ref, scale_ref, gain_q_ref, gain_k_ref, cos_ref, sin_ref, _, q_out, k_out):
    cosine = cos_ref[...]
    sine = sin_ref[...]
    sides = ((q_ref, gain_q_ref, q_out), (k_ref, gain_k_ref, k_out))
    for side, (ref, gain, out) in enumerate(sides):
        scale = scale_ref[:, side : side + 1]
        for col in range(0, ref.shape[1], HEAD_DIM):
            cols = slice(col, col + HEAD_DIM)
            x = ref[:, cols].astype(jnp.float32) * scale * gain[:, cols]
            y = x * cosine + pltpu.roll(x, HEAD_DIM // 2, 1) * sine
            out[:, cols] = y.astype(jnp.bfloat16)


def turn(group, queries, new_keys, scales, gain_q, gain_k, cosine, sine, after):
    rows, width = queries.shape
    width = width // group_count(width)
    part = jax.ShapeDtypeStruct((rows, width), jnp.bfloat16)
    part_spec = pl.BlockSpec((rows, width), lambda i: (0, group))
    gain_spec = pl.BlockSpec((1, width), lambda i: (0, group))
    whole = lambda shape: pl.BlockSpec(shape, lambda i: (0, 0))
    return pl.pallas_call(
        turn_kernel,
        grid=(1,),
        in_specs=[
            part_spec,
            part_spec,
            whole(scales.shape),
            gain_spec,
            gain_spec,
            whole(cosine.shape),
            whole(sine.shape),
            pl.BlockSpec(memory_space=pl.ANY),
        ],
        out_specs=[whole(part.shape), whole(part.shape)],
        out_shape=[part, part],
        compiler_params=pltpu.CompilerParams(vmem_limit_bytes=16 * 2**20),
        name="norm_turn",
    )(queries, new_keys, scales, gain_q[None], gain_k[None], cosine, sine, after)


def joined(parts, axis):
    return parts[0] if len(parts) == 1 else jnp.concatenate(parts, axis=axis)


def attend_kernel(
    q_column,
    table_ref,
    slot_ref,
    q_slot_ref,
    *refs,
):
    *q_refs, keys_ref, values_ref, near_keys_ref, near_values_ref, near_starts_ref, _, _ = refs[:-7]
    keep_ref, send_ref, q_all, acc, peak, total, sems = refs[-7:]
    step = pl.program_id(0)
    half, _, rows = keep_ref.shape
    width = acc.shape[1]
    blocks = 2 * half
    heads = width // HEAD_DIM
    lane = lax.broadcasted_iota(jnp.int32, (1, rows), 1)

    def update(slots, q_slots, keys_ref, values_ref, masks, allowed):
        ones = jnp.ones((PIECE, keys_ref.shape[0]), jnp.bfloat16)
        mask = joined(masks, 1)
        old_peak = joined([peak[s] for s in slots], 1)
        old_total = joined([total[s] for s in slots], 1)
        scores, weights, tops, fades = {}, {}, {}, {}

        def score(h):
            cols = slice(h * HEAD_DIM, (h + 1) * HEAD_DIM)
            q = joined([q_all[s, :, cols] for s in q_slots], 0)
            scores[h] = lax.dot_general(
                keys_ref[:, cols], q, (((1,), (1,)), ((), ())), preferred_element_type=jnp.float32
            )

        def weigh(h):
            found = scores.pop(h)
            if allowed is not None:
                found = jnp.where(allowed, found, LOW_SCORE)
            before = old_peak[h : h + 1]
            top = jnp.maximum(jnp.max(found, axis=0, keepdims=True), before)
            tops[h] = jnp.where(mask, top, before)
            fades[h] = jnp.where(mask, jnp.exp2(before - top), 1.0)
            weights[h] = jnp.exp2(found - jnp.where(mask, top, -LOW_SCORE)).astype(jnp.bfloat16)

        def blend(h):
            cols = slice(h * HEAD_DIM, (h + 1) * HEAD_DIM)
            values = jnp.concatenate([values_ref[:, cols].T, ones], axis=0)
            blended = jnp.dot(values, weights.pop(h), preferred_element_type=jnp.float32)
            fade = fades.pop(h)
            held = [acc[s, cols, :] for s in slots]
            sums = old_total[h : h + 1] * fade + blended[HEAD_DIM : HEAD_DIM + 1]
            for i, s in enumerate(slots):
                span = slice(i * rows, (i + 1) * rows)
                acc[s, cols, :] = held[i] * fade[:, span] + blended[:HEAD_DIM, span]
                peak[s, h : h + 1, :] = tops[h][:, span]
                total[s, h : h + 1, :] = sums[:, span]

        for h in range(heads + 2):
            if h < heads:
                score(h)
            if 1 <= h <= heads:
                weigh(h - 1)
            if h >= 2:
                blend(h - 2)

    @pl.when(step == 0)
    def _():
        share = blocks // len(q_refs)
        copies = [
            pltpu.make_async_copy(
                ref.at[:, :, pl.ds(q_column, width)], q_all.at[pl.ds(i * share, share)], sems.at[i]
            )
            for i, ref in enumerate(q_refs)
        ]
        for copy in copies:
            copy.start()
        q_all[blocks] = jnp.zeros((rows, width), jnp.bfloat16)
        acc[...] = jnp.zeros_like(acc)
        peak[...] = jnp.full(peak.shape, LOW_SCORE, jnp.float32)
        total[...] = jnp.zeros_like(total)
        for copy in copies:
            copy.wait()
        first = slot_ref[blocks + 1]

        def near_pair(j, carry):
            low = first + 2 * j
            row = low * rows + jnp.concatenate([lane, lane + rows], axis=1)
            begin = near_starts_ref[j]
            key = first * rows + lax.broadcasted_iota(jnp.int32, (rows, 2 * rows), 0)
            allowed = (key >= begin) & (key <= row)
            some = begin < (first + 1) * rows
            at = [jnp.minimum(low + i, blocks) for i in range(2)]
            slots, q_slots = [slot_ref[i] for i in at], [q_slot_ref[i] for i in at]
            masks = [some[:, :rows], some[:, rows:]]
            update(slots, q_slots, near_keys_ref, near_values_ref, masks, allowed)
            return carry

        lax.fori_loop(0, 2, near_pair, 0)

    @pl.when(step > 0)
    def _():
        begin = table_ref[4 * step - 4]
        end = table_ref[4 * step - 3]
        first = table_ref[4 * step - 2]
        count = table_ref[4 * step - 1]

        def visit(at):
            masks = [(b * rows + lane >= begin) & (b * rows + lane < end) for b in at]
            slots, q_slots = [slot_ref[b] for b in at], [q_slot_ref[b] for b in at]
            update(slots, q_slots, keys_ref.at[0], values_ref.at[0], masks, None)

        def pair(j, carry):
            visit([first + 2 * j, first + 2 * j + 1])
            return carry

        lax.fori_loop(0, count // 2, pair, 0)

        @pl.when(count % 2 == 1)
        def _():
            visit([first + count - 1])

    @pl.when(step == pl.num_programs(0) - 1)
    def _():
        for at, out in ((0, keep_ref), (half, send_ref)):

            def finish(i, carry, at=at, out=out):
                sums = jnp.maximum(total[at + i], 1.0)
                write_block(
                    out.at[i],
                    lambda h: acc[at + i, h * HEAD_DIM : (h + 1) * HEAD_DIM, :],
                    1.0 / sums,
                    peak[at + i] + jnp.log2(sums),
                    heads,
                )
                return carry

            lax.fori_loop(0, half, finish, 0)


def write_block(out, block, factors, levels, heads):
    for h in range(heads):
        out[h * HEAD_DIM : (h + 1) * HEAD_DIM, :] = (block(h) * factors[h : h + 1]).astype(jnp.bfloat16)
    first = levels.astype(jnp.bfloat16).astype(jnp.float32)
    second = (levels - first).astype(jnp.bfloat16).astype(jnp.float32)
    third = levels - first - second
    stacked = jnp.concatenate([first, second, third, jnp.zeros_like(levels)], axis=0)
    out[heads * HEAD_DIM :, :] = stacked.astype(jnp.bfloat16)


def read_levels(ref, heads):
    stacked = ref[heads * HEAD_DIM :, :].astype(jnp.float32)
    return stacked[:8] + (stacked[8:16] + stacked[16:24])


def attend(
    group, table, slots, q_slots, q_parts, cache_keys, cache_values, near_keys, near_values, near_starts, after
):
    rows, width = near_keys.shape
    half = sum(part.shape[0] for part in q_parts) // 2
    pages, page_len, _ = cache_keys.shape
    heads = width // HEAD_DIM
    blocks = 2 * half
    assert heads <= 8
    out = jax.ShapeDtypeStruct((half, width + LEVEL_ROWS, rows), jnp.bfloat16)
    page_spec = pl.BlockSpec((1, page_len, width), lambda i, *_: (jnp.maximum(i - 1, 0), 0, group))
    near_spec = pl.BlockSpec((rows, width), lambda i, *_: (0, group))
    own_spec = pl.BlockSpec((rows, width), lambda i, *_: (0, 0))
    whole = lambda shape: pl.BlockSpec(shape, lambda i, *_: (0,) * len(shape))
    q_column = group // 2 * width if len(q_parts) == 1 else 0
    return pl.pallas_call(
        functools.partial(attend_kernel, q_column),
        grid_spec=pltpu.PrefetchScalarGridSpec(
            num_scalar_prefetch=3,
            grid=(pages + 1,),
            in_specs=[pl.BlockSpec(memory_space=pl.ANY)] * len(q_parts)
            + [
                page_spec,
                page_spec,
                own_spec,
                near_spec,
                whole((2, 1, 2 * rows)),
                pl.BlockSpec(memory_space=pl.ANY),
                pl.BlockSpec(memory_space=pl.ANY),
            ],
            out_specs=[whole(out.shape), whole(out.shape)],
            scratch_shapes=[
                pltpu.VMEM((blocks + 1, rows, width), jnp.bfloat16),
                pltpu.VMEM((blocks + 1, width, rows), jnp.float32),
                pltpu.VMEM((blocks + 1, 8, rows), jnp.float32),
                pltpu.VMEM((blocks + 1, 8, rows), jnp.float32),
                pltpu.SemaphoreType.DMA((2,)),
            ],
        ),
        out_shape=[out, out],
        compiler_params=pltpu.CompilerParams(
            dimension_semantics=("arbitrary",), vmem_limit_bytes=56 * 2**20
        ),
        cost_estimate=pl.CostEstimate(
            flops=pages * heads * 256 * page_len * HEAD_DIM * 8,
            bytes_accessed=pages * page_len * width * 4,
            transcendentals=pages * heads * 256 * page_len,
        ),
        name="cache_attend",
    )(table, slots, q_slots, *q_parts, cache_keys, cache_values, near_keys, near_values, near_starts, *after)


def merged(refs, heads):
    levels = [read_levels(ref, heads) for ref in refs]
    top = functools.reduce(jnp.maximum, levels)
    weights = [jnp.exp2(level - top) for level in levels]
    total = functools.reduce(jnp.add, weights)
    factors = [w / total for w in weights]

    def block(h):
        cols = slice(h * HEAD_DIM, (h + 1) * HEAD_DIM)
        return functools.reduce(
            jnp.add, [ref[cols, :].astype(jnp.float32) * f[h : h + 1] for ref, f in zip(refs, factors)]
        )

    return block, top + jnp.log2(total)


def combine_kernel(*refs):
    *ins, _, keep_ref, send_ref = refs
    heads = (keep_ref.shape[1] - LEVEL_ROWS) // HEAD_DIM
    for g in range(len(ins) // 4):
        mine_low, mine_high, got_low, got_high = ins[4 * g : 4 * g + 4]
        for mine, got, out in ((mine_low, got_low, keep_ref), (mine_high, got_high, send_ref)):
            block, levels = merged([mine.at[0], got.at[0]], heads)
            write_block(out.at[g], block, jnp.ones_like(levels), levels, heads)


def combine(pairs, after):
    count, depth, rows = pairs[0][0].shape
    groups = len(pairs)
    half = count // 2
    low = pl.BlockSpec((1, depth, rows), lambda i: (i, 0, 0))
    high = pl.BlockSpec((1, depth, rows), lambda i: (i + half, 0, 0))
    into = pl.BlockSpec((groups, depth, rows), lambda i: (i, 0, 0))
    out = jax.ShapeDtypeStruct((half * groups, depth, rows), jnp.bfloat16)
    return pl.pallas_call(
        combine_kernel,
        grid=(half,),
        in_specs=[low, high, low, high] * groups + [pl.BlockSpec(memory_space=pl.ANY)],
        out_specs=[into, into],
        out_shape=[out, out],
        compiler_params=pltpu.CompilerParams(vmem_limit_bytes=24 * 2**20),
        cost_estimate=pl.CostEstimate(
            flops=groups * count * depth * rows * 4,
            bytes_accessed=groups * count * depth * rows * 6,
            transcendentals=0,
        ),
        name="combine_pairs",
    )(*[part for mine, got in pairs for part in (mine, mine, got, got)], after)


def last_kernel(mine_ref, got_ref, _, out_ref):
    groups, depth, _ = mine_ref.shape
    heads = (depth - LEVEL_ROWS) // HEAD_DIM
    for g in range(groups):
        block, _ = merged([mine_ref.at[g], got_ref.at[g]], heads)
        for h in range(heads):
            at = (g * heads + h) * HEAD_DIM
            out_ref[at : at + HEAD_DIM, :] = block(h).astype(jnp.bfloat16)


def combine_last(mine, got, after):
    groups, depth, rows = mine.shape
    whole = pl.BlockSpec(memory_space=pltpu.VMEM)
    return pl.pallas_call(
        last_kernel,
        in_specs=[whole, whole, pl.BlockSpec(memory_space=pl.ANY)],
        out_shape=jax.ShapeDtypeStruct((groups * (depth - LEVEL_ROWS), rows), jnp.bfloat16),
        compiler_params=pltpu.CompilerParams(vmem_limit_bytes=24 * 2**20),
        cost_estimate=pl.CostEstimate(
            flops=groups * depth * rows * 4, bytes_accessed=groups * depth * rows * 6, transcendentals=0
        ),
        name="combine_last",
    )(mine, got, after)


def local(
    hidden_in,
    queries,
    new_keys,
    new_values,
    query_gain,
    key_gain,
    cache_keys,
    cache_values,
    seg_ids,
    cache_pages,
    page_table,
    out_weight,
    out_bias,
    gate_mod,
):
    tok_dev, local_width = queries.shape
    size = lax.axis_size("req")
    tp_size = lax.axis_size("tp")
    model_width = local_width * tp_size
    line = size // PLANE
    device = lax.axis_index("req")
    spot = device % PLANE
    slot_count, page_len, _ = cache_keys.shape
    request_count = cache_pages.shape[0]
    total_pages = page_table.shape[0]
    first_row = device * tok_dev
    own_rows = first_row + jnp.arange(tok_dev, dtype=jnp.int32)
    own_segs = lax.dynamic_slice_in_dim(seg_ids, first_row, tok_dev, 0)
    req_ids = jnp.arange(request_count, dtype=jnp.int32)
    starts = jnp.sum((seg_ids[None, :] < req_ids[:, None]).astype(jnp.int32), axis=1)
    ends = jnp.sum((seg_ids[None, :] <= req_ids[:, None]).astype(jnp.int32), axis=1)
    own_pick = own_segs[:, None] == req_ids[None, :]
    own_start = jnp.sum(jnp.where(own_pick, starts[None, :], 0), axis=1)
    own_cache = jnp.sum(jnp.where(own_pick, cache_pages[None, :], 0), axis=1)
    positions = own_cache * page_len + own_rows - own_start

    wide_q = queries.astype(jnp.float32)
    wide_k = new_keys.astype(jnp.float32)
    sums = lax.psum(
        jnp.stack([jnp.sum(wide_q * wide_q, axis=1), jnp.sum(wide_k * wide_k, axis=1)], axis=1), "tp"
    )
    scales = lax.rsqrt(sums / model_width + EPSILON) * jnp.array([[SCORE_SCALE, 1.0]], jnp.float32)
    halfway = HEAD_DIM // 2
    frequency = 10000.0 ** (-jnp.arange(halfway, dtype=jnp.float32) / halfway)
    angles = positions.astype(jnp.float32)[:, None] * frequency[None, :]
    cosine = jnp.cos(angles)
    sine = jnp.sin(angles)
    cosine = jnp.concatenate([cosine, cosine], axis=1)
    sine = jnp.concatenate([-sine, sine], axis=1)

    physical = device * slot_count + jnp.arange(slot_count, dtype=jnp.int32)
    logical = jnp.sum(
        jnp.where(
            page_table[None, :] == physical[:, None],
            jnp.arange(total_pages, dtype=jnp.int32)[None, :],
            0,
        ),
        axis=1,
    )
    page_ends = jnp.cumsum(cache_pages)
    owners = jnp.sum((page_ends[None, :] <= logical[:, None]).astype(jnp.int32), axis=1)
    owner_pick = owners[:, None] == req_ids[None, :]
    owner_starts = jnp.sum(jnp.where(owner_pick, starts[None, :], 0), axis=1)
    owner_ends = jnp.sum(jnp.where(owner_pick, ends[None, :], 0), axis=1)
    owner_first = owner_starts // tok_dev
    owner_blocks = (owner_ends - 1) // tok_dev - owner_first + 1
    table = jnp.stack([owner_starts, owner_ends, owner_first, owner_blocks], axis=1).reshape(-1)

    near_blocks = device + jnp.arange(4, dtype=jnp.int32)
    near_rows = (near_blocks[:, None] * tok_dev + jnp.arange(tok_dev, dtype=jnp.int32)[None, :]).reshape(-1)
    padded_segs = jnp.concatenate([seg_ids, jnp.full((3 * tok_dev,), -1, jnp.int32)])
    near_segs = lax.dynamic_slice_in_dim(padded_segs, first_row, 4 * tok_dev, 0)
    near_starts = jnp.sum(
        jnp.where(near_segs[:, None] == req_ids[None, :], starts[None, :], 0), axis=1
    )
    near_starts = jnp.where(near_segs < 0, near_rows + size * tok_dev, near_starts)
    near_starts = near_starts.reshape(2, 1, 2 * tok_dev)

    apart = jnp.arange(size, dtype=jnp.int32) ^ device
    beyond = jnp.stack([jnp.int32(size), device])
    natural = jnp.concatenate([jnp.arange(size, dtype=jnp.int32), beyond])
    masks = [1 << i for i in range((size - 1).bit_length())]
    columns = out_weight.shape[1]
    blocks_each = line // tp_size
    tp_device = lax.axis_index("tp")

    groups = group_count(local_width)
    gather_order = [2, 1] + masks[2:]
    slots, gather_slots = [
        jnp.concatenate(
            [sum(jnp.where((apart & m) > 0, size >> (i + 1), 0) for i, m in enumerate(order)), beyond]
        )
        for order in (masks, gather_order)
    ]
    gathered, near_keys, parts, stages = [None] * groups, [None] * groups, [None] * groups, []
    after = scales
    for group in [0, 2, 1, 3] if groups > 1 else [0]:
        parts[group], near_keys[group] = turn(
            group, queries, new_keys, scales, query_gain, key_gain, cosine, sine, after
        )
        after = near_keys[group]
        if group % 2 == 0:
            continue
        held = parts[group][None]
        for m in gather_order[:0:-1]:
            held = lax.optimization_barrier(jnp.concatenate([held, send_xor(held, m)], axis=0))
            stages.append(held)
            if held.shape[0] == line:
                after = held
        gathered[group] = held
    whole_blocks = lax.all_gather(
        jnp.concatenate(parts[::2], axis=1)[None], "req", axis=0, tiled=True
    )

    def gather_weights(after):
        weight, _ = lax.optimization_barrier((out_weight.T, after))
        lines = [[z * PLANE + p for z in range(line)] for p in range(PLANE)]
        weight = lax.all_gather(weight, "req", axis=0, tiled=True, axis_index_groups=lines)
        return weight.reshape(tp_size, blocks_each * columns, local_width)

    def swap_weights(weight, after):
        weight, _ = lax.optimization_barrier((weight, after))
        weights = []
        for k in range(tp_size):
            part = lax.dynamic_index_in_dim(weight, (tp_device + k) % tp_size, 0, keepdims=False)
            weights.append(part if k == 0 else send_tp(part, k))
        return weights

    last = len(masks) - 1
    if groups > 1:
        turns = ("a1", "a0", "c1", "a2", "c0", "c1", "a3", "c2", "c0", "c1", "c3", "c0", "c2", "l1", "l0")
        turns += ("c2", "c3", "l2", "c3", "l3")
    else:
        turns = ("a0",) + ("c0",) * last + ("l0",)
    state, stage, attended = {}, {}, []
    before = near_starts
    waits = [near_starts] * 4
    if groups > 1:
        waits[1] = stages[-1]
        gathered[1], _ = lax.optimization_barrier((gathered[1], stages[-2]))
    weight, weights = None, None
    for turn_name in turns:
        step, names = turn_name[0], turn_name[1:]
        if step == "a":
            group = int(names)
            if group % 2 == 0:
                q_parts = [whole_blocks]
            else:
                q_parts = [gathered[group], send_xor(gathered[group], gather_order[0])]
            state[names] = attend(
                group, table, slots, natural if group % 2 == 0 else gather_slots, q_parts,
                cache_keys, cache_values, near_keys[group], new_values, near_starts,
                (before, waits[group]),
            )
            stage[names] = 0
            before = state[names][0]
            if weight is None:
                weight = gather_weights(before)
            continue
        if names not in state:
            parts = list(names)
        else:
            parts = [names]
        pairs = []
        for part in parts:
            keep, send = state[part]
            pairs.append((keep, send_xor(send, masks[stage[part]])))
        stage[names] = stage[parts[0]] + 1
        if step == "c":
            state[names] = combine(pairs, before)
            before = state[names][0]
            if stage[names] == last - 1:
                latest = before
            if weights is None and names in ("3", str(groups - 1)):
                weights = swap_weights(weight, before)
        else:
            before = combine_last(*pairs[0], before)
            attended.append((names, before))
    if groups > 1:
        attended[:2] = attended[1::-1]
        attended[0] = (attended[0][0], lax.optimization_barrier((attended[0][1], latest))[0])

    projected = 0.0
    share = local_width // groups
    for some in [attended[:-1], attended[-1:]] if groups > 1 else [attended]:
        names = "".join(name for name, _ in some)
        some = joined([part for _, part in some], 0)
        got = [send_xor(some, k) for k in range(1, PLANE)]
        *got, _ = lax.optimization_barrier((*got, attended[-1][1]))
        spread = jnp.concatenate([some] + got, axis=1)
        spans = [(int(names[0]) * share, int(names[-1]) * share + share)]
        for k in range(tp_size):
            part = spread if k == 0 else send_tp(spread, k)
            at = 0
            for low, high in spans:
                projected = projected + jnp.dot(
                    weights[k][:, low:high],
                    part[at : at + high - low],
                    preferred_element_type=jnp.float32,
                )
                at += high - low
    sent = projected.astype(jnp.bfloat16)
    mine = [projected[:, :tok_dev]] + [
        send_xor(sent[:, k * tok_dev : (k + 1) * tok_dev], k).astype(jnp.float32) for k in range(1, PLANE)
    ]
    mine = [part.reshape(blocks_each, columns, tok_dev) for part in mine]
    swapped = [jnp.where((spot & 1) > 0, mine[i ^ 1], mine[i]) for i in range(PLANE)]
    swapped = [jnp.where((spot & 2) > 0, swapped[i ^ 2], swapped[i]) for i in range(PLANE)]
    projected = jnp.stack(swapped, axis=1).reshape(local_width, tok_dev).T

    gate_rows = jnp.dot(own_pick.astype(jnp.float32), gate_mod, precision=lax.Precision.HIGHEST)
    return (hidden_in.astype(jnp.float32) + gate_rows * (projected + out_bias[None, :])).astype(
        jnp.bfloat16
    )


def solution(mesh):
    return jax.shard_map(
        local,
        mesh=mesh,
        in_specs=(
            P("req", "tp"),
            P("req", "tp"),
            P("req", "tp"),
            P("req", "tp"),
            P("tp"),
            P("tp"),
            P("req", None, "tp"),
            P("req", None, "tp"),
            P(),
            P(),
            P(),
            P("tp", "req"),
            P("tp"),
            P(None, "tp"),
        ),
        out_specs=P("req", "tp"),
        check_vma=False,
    )
```

```python
import functools
import math

import jax
import jax.numpy as jnp
from jax import lax
from jax.experimental import pallas as pl
from jax.experimental.pallas import tpu as pltpu
from jax.sharding import PartitionSpec as P

HEAD_DIM = 128
EPSILON = 1e-06
LOW_SCORE = -1e30
PLANE = 4
PIECE = 16
LEVEL_ROWS = 32
SCORE_SCALE = math.log2(math.e) / math.sqrt(HEAD_DIM)


def send_xor(value, by):
    size = lax.axis_size("req")
    return lax.ppermute(value, "req", [(i, i ^ by) for i in range(size)])


def group_count(width):
    return 4 if width // HEAD_DIM % 4 == 0 else 1


def send_tp(value, by):
    size = lax.axis_size("tp")
    return lax.ppermute(value, "tp", [(i, (i + by) % size) for i in range(size)])


def turn_kernel(q_ref, k_ref, scale_ref, gain_q_ref, gain_k_ref, cos_ref, sin_ref, _, q_out, k_out):
    cosine = cos_ref[...]
    sine = sin_ref[...]
    sides = ((q_ref, gain_q_ref, q_out), (k_ref, gain_k_ref, k_out))
    for side, (ref, gain, out) in enumerate(sides):
        scale = scale_ref[:, side : side + 1]
        for col in range(0, ref.shape[1], HEAD_DIM):
            cols = slice(col, col + HEAD_DIM)
            x = ref[:, cols].astype(jnp.float32) * scale * gain[:, cols]
            y = x * cosine + pltpu.roll(x, HEAD_DIM // 2, 1) * sine
            out[:, cols] = y.astype(jnp.bfloat16)


def turn(group, queries, new_keys, scales, gain_q, gain_k, cosine, sine, after):
    rows, width = queries.shape
    width = width // group_count(width)
    part = jax.ShapeDtypeStruct((rows, width), jnp.bfloat16)
    part_spec = pl.BlockSpec((rows, width), lambda i: (0, group))
    gain_spec = pl.BlockSpec((1, width), lambda i: (0, group))
    whole = lambda shape: pl.BlockSpec(shape, lambda i: (0, 0))
    return pl.pallas_call(
        turn_kernel,
        grid=(1,),
        in_specs=[
            part_spec,
            part_spec,
            whole(scales.shape),
            gain_spec,
            gain_spec,
            whole(cosine.shape),
            whole(sine.shape),
            pl.BlockSpec(memory_space=pl.ANY),
        ],
        out_specs=[whole(part.shape), whole(part.shape)],
        out_shape=[part, part],
        compiler_params=pltpu.CompilerParams(vmem_limit_bytes=16 * 2**20),
        name="norm_turn",
    )(queries, new_keys, scales, gain_q[None], gain_k[None], cosine, sine, after)


def joined(parts, axis):
    return parts[0] if len(parts) == 1 else jnp.concatenate(parts, axis=axis)


def attend_kernel(
    q_column,
    table_ref,
    slot_ref,
    q_slot_ref,
    *refs,
):
    *q_refs, keys_ref, values_ref, near_keys_ref, near_values_ref, near_starts_ref, _, _ = refs[:-7]
    keep_ref, send_ref, q_all, acc, peak, total, sems = refs[-7:]
    step = pl.program_id(0)
    half, _, rows = keep_ref.shape
    width = acc.shape[1]
    blocks = 2 * half
    heads = width // HEAD_DIM
    lane = lax.broadcasted_iota(jnp.int32, (1, rows), 1)

    def update(slots, q_slots, keys_ref, values_ref, masks, allowed):
        ones = jnp.ones((PIECE, keys_ref.shape[0]), jnp.bfloat16)
        mask = joined(masks, 1)
        old_peak = joined([peak[s] for s in slots], 1)
        old_total = joined([total[s] for s in slots], 1)
        scores, weights, tops, fades = {}, {}, {}, {}

        def score(h):
            cols = slice(h * HEAD_DIM, (h + 1) * HEAD_DIM)
            q = joined([q_all[s, :, cols] for s in q_slots], 0)
            scores[h] = lax.dot_general(
                keys_ref[:, cols], q, (((1,), (1,)), ((), ())), preferred_element_type=jnp.float32
            )

        def weigh(h):
            found = scores.pop(h)
            if allowed is not None:
                found = jnp.where(allowed, found, LOW_SCORE)
            before = old_peak[h : h + 1]
            top = jnp.maximum(jnp.max(found, axis=0, keepdims=True), before)
            tops[h] = jnp.where(mask, top, before)
            fades[h] = jnp.where(mask, jnp.exp2(before - top), 1.0)
            weights[h] = jnp.exp2(found - jnp.where(mask, top, -LOW_SCORE)).astype(jnp.bfloat16)

        def blend(h):
            cols = slice(h * HEAD_DIM, (h + 1) * HEAD_DIM)
            values = jnp.concatenate([values_ref[:, cols].T, ones], axis=0)
            blended = jnp.dot(values, weights.pop(h), preferred_element_type=jnp.float32)
            fade = fades.pop(h)
            held = [acc[s, cols, :] for s in slots]
            sums = old_total[h : h + 1] * fade + blended[HEAD_DIM : HEAD_DIM + 1]
            for i, s in enumerate(slots):
                span = slice(i * rows, (i + 1) * rows)
                acc[s, cols, :] = held[i] * fade[:, span] + blended[:HEAD_DIM, span]
                peak[s, h : h + 1, :] = tops[h][:, span]
                total[s, h : h + 1, :] = sums[:, span]

        for h in range(heads + 2):
            if h < heads:
                score(h)
            if 1 <= h <= heads:
                weigh(h - 1)
            if h >= 2:
                blend(h - 2)

    @pl.when(step == 0)
    def _():
        share = blocks // len(q_refs)
        copies = [
            pltpu.make_async_copy(
                ref.at[:, :, pl.ds(q_column, width)], q_all.at[pl.ds(i * share, share)], sems.at[i]
            )
            for i, ref in enumerate(q_refs)
        ]
        for copy in copies:
            copy.start()
        q_all[blocks] = jnp.zeros((rows, width), jnp.bfloat16)
        acc[...] = jnp.zeros_like(acc)
        peak[...] = jnp.full(peak.shape, LOW_SCORE, jnp.float32)
        total[...] = jnp.zeros_like(total)
        for copy in copies:
            copy.wait()
        first = slot_ref[blocks + 1]

        def near_pair(j, carry):
            low = first + 2 * j
            row = low * rows + jnp.concatenate([lane, lane + rows], axis=1)
            begin = near_starts_ref[j]
            key = first * rows + lax.broadcasted_iota(jnp.int32, (rows, 2 * rows), 0)
            allowed = (key >= begin) & (key <= row)
            some = begin < (first + 1) * rows
            at = [jnp.minimum(low + i, blocks) for i in range(2)]
            slots, q_slots = [slot_ref[i] for i in at], [q_slot_ref[i] for i in at]
            masks = [some[:, :rows], some[:, rows:]]
            update(slots, q_slots, near_keys_ref, near_values_ref, masks, allowed)
            return carry

        lax.fori_loop(0, 2, near_pair, 0)

    @pl.when(step > 0)
    def _():
        begin = table_ref[4 * step - 4]
        end = table_ref[4 * step - 3]
        first = table_ref[4 * step - 2]
        count = table_ref[4 * step - 1]

        def visit(at):
            masks = [(b * rows + lane >= begin) & (b * rows + lane < end) for b in at]
            slots, q_slots = [slot_ref[b] for b in at], [q_slot_ref[b] for b in at]
            update(slots, q_slots, keys_ref.at[0], values_ref.at[0], masks, None)

        def pair(j, carry):
            visit([first + 2 * j, first + 2 * j + 1])
            return carry

        lax.fori_loop(0, count // 2, pair, 0)

        @pl.when(count % 2 == 1)
        def _():
            visit([first + count - 1])

    @pl.when(step == pl.num_programs(0) - 1)
    def _():
        for at, out in ((0, keep_ref), (half, send_ref)):

            def finish(i, carry, at=at, out=out):
                sums = jnp.maximum(total[at + i], 1.0)
                write_block(
                    out.at[i],
                    lambda h: acc[at + i, h * HEAD_DIM : (h + 1) * HEAD_DIM, :],
                    1.0 / sums,
                    peak[at + i] + jnp.log2(sums),
                    heads,
                )
                return carry

            lax.fori_loop(0, half, finish, 0)


def write_block(out, block, factors, levels, heads):
    for h in range(heads):
        out[h * HEAD_DIM : (h + 1) * HEAD_DIM, :] = (block(h) * factors[h : h + 1]).astype(jnp.bfloat16)
    first = levels.astype(jnp.bfloat16).astype(jnp.float32)
    second = (levels - first).astype(jnp.bfloat16).astype(jnp.float32)
    third = levels - first - second
    stacked = jnp.concatenate([first, second, third, jnp.zeros_like(levels)], axis=0)
    out[heads * HEAD_DIM :, :] = stacked.astype(jnp.bfloat16)


def read_levels(ref, heads):
    stacked = ref[heads * HEAD_DIM :, :].astype(jnp.float32)
    return stacked[:8] + (stacked[8:16] + stacked[16:24])


def attend(
    group, table, slots, q_slots, q_parts, cache_keys, cache_values, near_keys, near_values, near_starts, after
):
    rows, width = near_keys.shape
    half = sum(part.shape[0] for part in q_parts) // 2
    pages, page_len, _ = cache_keys.shape
    heads = width // HEAD_DIM
    blocks = 2 * half
    assert heads <= 8
    out = jax.ShapeDtypeStruct((half, width + LEVEL_ROWS, rows), jnp.bfloat16)
    page_spec = pl.BlockSpec((1, page_len, width), lambda i, *_: (jnp.maximum(i - 1, 0), 0, group))
    near_spec = pl.BlockSpec((rows, width), lambda i, *_: (0, group))
    own_spec = pl.BlockSpec((rows, width), lambda i, *_: (0, 0))
    whole = lambda shape: pl.BlockSpec(shape, lambda i, *_: (0,) * len(shape))
    q_column = group // 2 * width if len(q_parts) == 1 else 0
    return pl.pallas_call(
        functools.partial(attend_kernel, q_column),
        grid_spec=pltpu.PrefetchScalarGridSpec(
            num_scalar_prefetch=3,
            grid=(pages + 1,),
            in_specs=[pl.BlockSpec(memory_space=pl.ANY)] * len(q_parts)
            + [
                page_spec,
                page_spec,
                own_spec,
                near_spec,
                whole((2, 1, 2 * rows)),
                pl.BlockSpec(memory_space=pl.ANY),
                pl.BlockSpec(memory_space=pl.ANY),
            ],
            out_specs=[whole(out.shape), whole(out.shape)],
            scratch_shapes=[
                pltpu.VMEM((blocks + 1, rows, width), jnp.bfloat16),
                pltpu.VMEM((blocks + 1, width, rows), jnp.float32),
                pltpu.VMEM((blocks + 1, 8, rows), jnp.float32),
                pltpu.VMEM((blocks + 1, 8, rows), jnp.float32),
                pltpu.SemaphoreType.DMA((2,)),
            ],
        ),
        out_shape=[out, out],
        compiler_params=pltpu.CompilerParams(
            dimension_semantics=("arbitrary",), vmem_limit_bytes=56 * 2**20
        ),
        cost_estimate=pl.CostEstimate(
            flops=pages * heads * 256 * page_len * HEAD_DIM * 8,
            bytes_accessed=pages * page_len * width * 4,
            transcendentals=pages * heads * 256 * page_len,
        ),
        name="cache_attend",
    )(table, slots, q_slots, *q_parts, cache_keys, cache_values, near_keys, near_values, near_starts, *after)


def merged(refs, heads):
    levels = [read_levels(ref, heads) for ref in refs]
    top = functools.reduce(jnp.maximum, levels)
    weights = [jnp.exp2(level - top) for level in levels]
    total = functools.reduce(jnp.add, weights)
    factors = [w / total for w in weights]

    def block(h):
        cols = slice(h * HEAD_DIM, (h + 1) * HEAD_DIM)
        return functools.reduce(
            jnp.add, [ref[cols, :].astype(jnp.float32) * f[h : h + 1] for ref, f in zip(refs, factors)]
        )

    return block, top + jnp.log2(total)


def combine_kernel(*refs):
    *ins, _, keep_ref, send_ref = refs
    heads = (keep_ref.shape[1] - LEVEL_ROWS) // HEAD_DIM
    for g in range(len(ins) // 4):
        mine_low, mine_high, got_low, got_high = ins[4 * g : 4 * g + 4]
        for mine, got, out in ((mine_low, got_low, keep_ref), (mine_high, got_high, send_ref)):
            block, levels = merged([mine.at[0], got.at[0]], heads)
            write_block(out.at[g], block, jnp.ones_like(levels), levels, heads)


def combine(pairs, after):
    count, depth, rows = pairs[0][0].shape
    groups = len(pairs)
    half = count // 2
    low = pl.BlockSpec((1, depth, rows), lambda i: (i, 0, 0))
    high = pl.BlockSpec((1, depth, rows), lambda i: (i + half, 0, 0))
    into = pl.BlockSpec((groups, depth, rows), lambda i: (i, 0, 0))
    out = jax.ShapeDtypeStruct((half * groups, depth, rows), jnp.bfloat16)
    return pl.pallas_call(
        combine_kernel,
        grid=(half,),
        in_specs=[low, high, low, high] * groups + [pl.BlockSpec(memory_space=pl.ANY)],
        out_specs=[into, into],
        out_shape=[out, out],
        compiler_params=pltpu.CompilerParams(vmem_limit_bytes=24 * 2**20),
        cost_estimate=pl.CostEstimate(
            flops=groups * count * depth * rows * 4,
            bytes_accessed=groups * count * depth * rows * 6,
            transcendentals=0,
        ),
        name="combine_pairs",
    )(*[part for mine, got in pairs for part in (mine, mine, got, got)], after)


def last_kernel(mine_ref, got_ref, _, out_ref):
    groups, depth, _ = mine_ref.shape
    heads = (depth - LEVEL_ROWS) // HEAD_DIM
    for g in range(groups):
        block, _ = merged([mine_ref.at[g], got_ref.at[g]], heads)
        for h in range(heads):
            at = (g * heads + h) * HEAD_DIM
            out_ref[at : at + HEAD_DIM, :] = block(h).astype(jnp.bfloat16)


def combine_last(mine, got, after):
    groups, depth, rows = mine.shape
    whole = pl.BlockSpec(memory_space=pltpu.VMEM)
    return pl.pallas_call(
        last_kernel,
        in_specs=[whole, whole, pl.BlockSpec(memory_space=pl.ANY)],
        out_shape=jax.ShapeDtypeStruct((groups * (depth - LEVEL_ROWS), rows), jnp.bfloat16),
        compiler_params=pltpu.CompilerParams(vmem_limit_bytes=24 * 2**20),
        cost_estimate=pl.CostEstimate(
            flops=groups * depth * rows * 4, bytes_accessed=groups * depth * rows * 6, transcendentals=0
        ),
        name="combine_last",
    )(mine, got, after)


def local(
    hidden_in,
    queries,
    new_keys,
    new_values,
    query_gain,
    key_gain,
    cache_keys,
    cache_values,
    seg_ids,
    cache_pages,
    page_table,
    out_weight,
    out_bias,
    gate_mod,
):
    tok_dev, local_width = queries.shape
    size = lax.axis_size("req")
    tp_size = lax.axis_size("tp")
    model_width = local_width * tp_size
    line = size // PLANE
    device = lax.axis_index("req")
    spot = device % PLANE
    slot_count, page_len, _ = cache_keys.shape
    request_count = cache_pages.shape[0]
    total_pages = page_table.shape[0]
    first_row = device * tok_dev
    own_rows = first_row + jnp.arange(tok_dev, dtype=jnp.int32)
    own_segs = lax.dynamic_slice_in_dim(seg_ids, first_row, tok_dev, 0)
    req_ids = jnp.arange(request_count, dtype=jnp.int32)
    starts = jnp.sum((seg_ids[None, :] < req_ids[:, None]).astype(jnp.int32), axis=1)
    ends = jnp.sum((seg_ids[None, :] <= req_ids[:, None]).astype(jnp.int32), axis=1)
    own_pick = own_segs[:, None] == req_ids[None, :]
    own_start = jnp.sum(jnp.where(own_pick, starts[None, :], 0), axis=1)
    own_cache = jnp.sum(jnp.where(own_pick, cache_pages[None, :], 0), axis=1)
    positions = own_cache * page_len + own_rows - own_start

    wide_q = queries.astype(jnp.float32)
    wide_k = new_keys.astype(jnp.float32)
    sums = lax.psum(
        jnp.stack([jnp.sum(wide_q * wide_q, axis=1), jnp.sum(wide_k * wide_k, axis=1)], axis=1), "tp"
    )
    scales = lax.rsqrt(sums / model_width + EPSILON) * jnp.array([[SCORE_SCALE, 1.0]], jnp.float32)
    halfway = HEAD_DIM // 2
    frequency = 10000.0 ** (-jnp.arange(halfway, dtype=jnp.float32) / halfway)
    angles = positions.astype(jnp.float32)[:, None] * frequency[None, :]
    cosine = jnp.cos(angles)
    sine = jnp.sin(angles)
    cosine = jnp.concatenate([cosine, cosine], axis=1)
    sine = jnp.concatenate([-sine, sine], axis=1)

    physical = device * slot_count + jnp.arange(slot_count, dtype=jnp.int32)
    logical = jnp.sum(
        jnp.where(
            page_table[None, :] == physical[:, None],
            jnp.arange(total_pages, dtype=jnp.int32)[None, :],
            0,
        ),
        axis=1,
    )
    page_ends = jnp.cumsum(cache_pages)
    owners = jnp.sum((page_ends[None, :] <= logical[:, None]).astype(jnp.int32), axis=1)
    owner_pick = owners[:, None] == req_ids[None, :]
    owner_starts = jnp.sum(jnp.where(owner_pick, starts[None, :], 0), axis=1)
    owner_ends = jnp.sum(jnp.where(owner_pick, ends[None, :], 0), axis=1)
    owner_first = owner_starts // tok_dev
    owner_blocks = (owner_ends - 1) // tok_dev - owner_first + 1
    table = jnp.stack([owner_starts, owner_ends, owner_first, owner_blocks], axis=1).reshape(-1)

    near_blocks = device + jnp.arange(4, dtype=jnp.int32)
    near_rows = (near_blocks[:, None] * tok_dev + jnp.arange(tok_dev, dtype=jnp.int32)[None, :]).reshape(-1)
    padded_segs = jnp.concatenate([seg_ids, jnp.full((3 * tok_dev,), -1, jnp.int32)])
    near_segs = lax.dynamic_slice_in_dim(padded_segs, first_row, 4 * tok_dev, 0)
    near_starts = jnp.sum(
        jnp.where(near_segs[:, None] == req_ids[None, :], starts[None, :], 0), axis=1
    )
    near_starts = jnp.where(near_segs < 0, near_rows + size * tok_dev, near_starts)
    near_starts = near_starts.reshape(2, 1, 2 * tok_dev)

    apart = jnp.arange(size, dtype=jnp.int32) ^ device
    beyond = jnp.stack([jnp.int32(size), device])
    natural = jnp.concatenate([jnp.arange(size, dtype=jnp.int32), beyond])
    masks = [1 << i for i in range((size - 1).bit_length())]
    columns = out_weight.shape[1]
    blocks_each = line // tp_size
    tp_device = lax.axis_index("tp")

    groups = group_count(local_width)
    gather_order = [2, 1] + masks[2:]
    slots, gather_slots = [
        jnp.concatenate(
            [sum(jnp.where((apart & m) > 0, size >> (i + 1), 0) for i, m in enumerate(order)), beyond]
        )
        for order in (masks, gather_order)
    ]
    gathered, near_keys, parts, stages = [None] * groups, [None] * groups, [None] * groups, []
    after = scales
    for group in [0, 2, 1, 3] if groups > 1 else [0]:
        parts[group], near_keys[group] = turn(
            group, queries, new_keys, scales, query_gain, key_gain, cosine, sine, after
        )
        after = near_keys[group]
        if group % 2 == 0:
            continue
        held = parts[group][None]
        for m in gather_order[:0:-1]:
            held = lax.optimization_barrier(jnp.concatenate([held, send_xor(held, m)], axis=0))
            stages.append(held)
            if held.shape[0] == line:
                after = held
        gathered[group] = held
    whole_blocks = lax.all_gather(
        jnp.concatenate(parts[::2], axis=1)[None], "req", axis=0, tiled=True
    )

    def gather_weights(after):
        weight, _ = lax.optimization_barrier((out_weight.T, after))
        lines = [[z * PLANE + p for z in range(line)] for p in range(PLANE)]
        weight = lax.all_gather(weight, "req", axis=0, tiled=True, axis_index_groups=lines)
        return weight.reshape(tp_size, blocks_each * columns, local_width)

    def swap_weights(weight, after):
        weight, _ = lax.optimization_barrier((weight, after))
        weights = []
        for k in range(tp_size):
            part = lax.dynamic_index_in_dim(weight, (tp_device + k) % tp_size, 0, keepdims=False)
            weights.append(part if k == 0 else send_tp(part, k))
        return weights

    last = len(masks) - 1
    if groups > 1:
        turns = ("a1", "a0", "c1", "a2", "c0", "c1", "a3", "c2", "c0", "c1", "c3", "c0", "c2", "l1", "l0")
        turns += ("c3", "c2", "c3", "l2", "l3")
    else:
        turns = ("a0",) + ("c0",) * last + ("l0",)
    state, stage, attended = {}, {}, []
    before = near_starts
    waits = [near_starts] * 4
    if groups > 1:
        waits[1] = stages[-1]
        gathered[1], _ = lax.optimization_barrier((gathered[1], stages[-2]))
    weight, weights = None, None
    for turn_name in turns:
        step, names = turn_name[0], turn_name[1:]
        if step == "a":
            group = int(names)
            if group % 2 == 0:
                q_parts = [whole_blocks]
            else:
                q_parts = [gathered[group], send_xor(gathered[group], gather_order[0])]
            state[names] = attend(
                group, table, slots, natural if group % 2 == 0 else gather_slots, q_parts,
                cache_keys, cache_values, near_keys[group], new_values, near_starts,
                (before, waits[group]),
            )
            stage[names] = 0
            before = state[names][0]
            if weight is None:
                weight = gather_weights(stages[2] if groups > 1 else before)
            continue
        if names not in state:
            parts = list(names)
        else:
            parts = [names]
        pairs = []
        for part in parts:
            keep, send = state[part]
            pairs.append((keep, send_xor(send, masks[stage[part]])))
        stage[names] = stage[parts[0]] + 1
        if step == "c":
            state[names] = combine(pairs, before)
            before = state[names][0]
            if stage[names] == last - 1:
                latest = before
            if weights is None and names in ("3", str(groups - 1)):
                weights = swap_weights(weight, before)
        else:
            before = combine_last(*pairs[0], before)
            attended.append((names, before))
    if groups > 1:
        attended[:2] = attended[1::-1]
        attended[0] = (attended[0][0], lax.optimization_barrier((attended[0][1], latest))[0])

    projected = 0.0
    share = local_width // groups
    for some in [attended[:-1], attended[-1:]] if groups > 1 else [attended]:
        names = "".join(name for name, _ in some)
        some = joined([part for _, part in some], 0)
        got = [send_xor(some, k) for k in range(1, PLANE)]
        *got, _ = lax.optimization_barrier((*got, attended[-1][1]))
        spread = jnp.concatenate([some] + got, axis=1)
        spans = [(int(names[0]) * share, int(names[-1]) * share + share)]
        for k in range(tp_size):
            part = spread if k == 0 else send_tp(spread, k)
            at = 0
            for low, high in spans:
                projected = projected + jnp.dot(
                    weights[k][:, low:high],
                    part[at : at + high - low],
                    preferred_element_type=jnp.float32,
                )
                at += high - low
    sent = projected.astype(jnp.bfloat16)
    mine = [projected[:, :tok_dev]] + [
        send_xor(sent[:, k * tok_dev : (k + 1) * tok_dev], k).astype(jnp.float32) for k in range(1, PLANE)
    ]
    mine = [part.reshape(blocks_each, columns, tok_dev) for part in mine]
    swapped = [jnp.where((spot & 1) > 0, mine[i ^ 1], mine[i]) for i in range(PLANE)]
    swapped = [jnp.where((spot & 2) > 0, swapped[i ^ 2], swapped[i]) for i in range(PLANE)]
    projected = jnp.stack(swapped, axis=1).reshape(local_width, tok_dev).T

    gate_rows = jnp.dot(own_pick.astype(jnp.float32), gate_mod, precision=lax.Precision.HIGHEST)
    return (hidden_in.astype(jnp.float32) + gate_rows * (projected + out_bias[None, :])).astype(
        jnp.bfloat16
    )


def solution(mesh):
    return jax.shard_map(
        local,
        mesh=mesh,
        in_specs=(
            P("req", "tp"),
            P("req", "tp"),
            P("req", "tp"),
            P("req", "tp"),
            P("tp"),
            P("tp"),
            P("req", None, "tp"),
            P("req", None, "tp"),
            P(),
            P(),
            P(),
            P("tp", "req"),
            P("tp"),
            P(None, "tp"),
        ),
        out_specs=P("req", "tp"),
        check_vma=False,
    )
```
